128 devices in a mesh: mem: 4 (over y), lat: 4 (over z_lo, core), lon: 8 (over x, z_hi).
Axes of the slice: x: 4, y: 4, z: 4 (z_hi: 2, z_lo: 2; z = z_hi * 2 + z_lo), core: 2. Of those that a mesh axis runs over, the one named last changes fastest.
Arguments:
- control: bfloat16 [4, 64, 768, 1536], P('mem', None, 'lon', 'lat'), may hold values from -6 to 6
- perturbation: bfloat16 [4, 64, 768, 1536], P('mem', None, 'lon', 'lat'), may hold values from -6 to 6
- slab_levels: int32 [32], replicated, may hold values from 1 to 3, 64 in all
- member_group: int32 [4], P('mem'), may hold values from 0 to 3
- band_width: int32 [4], replicated, may hold values from 1 to 8
- zonal_rate: float32 [32, 768], replicated, may hold values from 0.0003 to 0.4
- meridional_rate: float32 [32, 768], replicated, may hold values from 0.0003 to 0.03
Outputs:
- increment: float32 [64, 768, 1536], P('mem', 'lon', 'lat')
The draws below stay inside these ranges and needn't reach their ends.
Inputs may be any that keep to these rules, and one draw needn't show every extreme that they name: `slab_levels`: the counts sum to 64 and the largest is exactly 3.
All inputs are finite; a program needn't handle non-finite values.
Results may differ from the reference program's by a relative error of at most 0.0046.
Values may be sent and summed in bfloat16 or wider, within the bound.
No kernel may reach another device: no remote copies, remote signals or barrier semaphores. Data moves between devices by JAX's collectives and lax.ppermute only.
A program may use at most 192 MiB of HBM per device.

```python
import math
import jax
import jax.numpy as jnp
import numpy as np
from jax import lax

NX = 1536
NY = 768
SLAB_MOST = 3
NGROUP = 4
BAND_MOST = 8
MEMBERS = 4
NSLAB = 32
LEVELS = 64


def log_spread(key, lowest, highest):
    unit = jax.random.uniform(key, (NSLAB, NY), jnp.float32)
    return lowest * (highest / lowest) ** unit


def mixed_rates(key, fast_share, slow_lo, slow_hi, fast_lo, fast_hi):
    pick_key, slow_key, fast_key = jax.random.split(key, 3)
    picked = jax.random.uniform(pick_key, (NSLAB, NY), jnp.float32)
    slow_part = log_spread(slow_key, slow_lo, slow_hi)
    fast_part = log_spread(fast_key, fast_lo, fast_hi)
    return jnp.where(picked < fast_share, fast_part, slow_part)


def draw_zonal_rate(key, part):
    key = jax.random.fold_in(key, 5)
    return mixed_rates(key, 0.4, 0.001, 0.03, 0.15, 0.4)


def draw_meridional_rate(key, part):
    key = jax.random.fold_in(key, 7)
    return log_spread(key, 0.001, 0.03)


def touch_ends(values, key, low, largest):
    extent = values.shape
    index_at = [jax.random.randint(jax.random.fold_in(key, axis), (), 0, extent[axis]) for axis in range(len(extent))]
    values = values.at[tuple(index_at)].set(low)
    longest = extent.index(max(extent))
    index_at[longest] = (index_at[longest] + 1) % extent[longest]
    return values.at[tuple(index_at)].set(largest)


def level_of(key, extent, cuts, least, top_value):
    def one(axis_at, shards_of):
        steps = jax.random.uniform(jax.random.fold_in(jax.random.fold_in(key, 6), axis_at), (shards_of,), jnp.float32, least / len(cuts), top_value / len(cuts))
        return jnp.repeat(jnp.exp(steps), extent[axis_at] // shards_of).reshape((-1,) + (1,) * (len(extent) - axis_at - 1))

    level = one(*cuts[0])
    for cut in cuts[1:]:
        level = level * one(*cut)
    return level


def profile(count, total, limit, skew):
    loads = [(1 << 20) // math.isqrt(standing ** skew) + 1 for standing in range(2, count + 1)]
    spare, given = total - limit - (count - 1), [1] * (count - 1)
    while spare > 0:
        candidates = [i for i in range(count - 1) if given[i] < limit]
        mass, left = sum([loads[i] for i in candidates]), spare
        for i in candidates:
            extra = min(limit - given[i], max(1, left * loads[i] // mass), spare)
            given[i] = given[i] + extra
            spare = spare - extra
    return np.array([limit] + given)


def uneven_parts(own_key, number_of, total, bound, lean):
    if number_of == 2:
        one = jax.random.randint(own_key, (), max(1, total - bound), min(bound, total - 1) + 1)
        return jnp.stack([one, total - one])
    lengths = jnp.asarray(profile(number_of, total, bound, lean), jnp.int32)
    pairs = (number_of - 1) // 2
    donor, receiver = lengths[1:1 + 2 * pairs:2], lengths[2:2 + 2 * pairs:2]
    slack = jnp.minimum(donor - 1, bound - receiver)
    moved = jax.random.randint(jax.random.fold_in(own_key, 1), (pairs,), 0, 1 << 20) % (slack + 1)
    lengths = lengths.at[1:1 + 2 * pairs:2].set(donor - moved).at[2:2 + 2 * pairs:2].set(receiver + moved)
    return lengths[jax.random.permutation(jax.random.fold_in(own_key, 2), number_of)]


def noise(rng, shape, width, most, cuts=(), held_as=jnp.bfloat16):
    factor_of = level_of(rng, shape, cuts, -0.22, 0.18) if cuts else 1.0
    drawn = jax.random.normal(rng, shape, jnp.float32) * width * factor_of
    return jnp.minimum(jnp.maximum(drawn, -most), most).astype(held_as)


def setup_inputs(seed: int = 0) -> dict:
    key_of = jax.random.split(jax.random.key(seed), 8)
    return {
        "control": noise(key_of[0], (MEMBERS, LEVELS, NY, NX), 1.0, 6.0, ((0, 4), (2, 8), (3, 4))),
        "perturbation": noise(key_of[1], (MEMBERS, LEVELS, NY, NX), 1.0, 6.0, ((0, 4), (2, 8), (3, 4))),
        "slab_levels": uneven_parts(key_of[2], NSLAB, LEVELS, SLAB_MOST, 2).astype(jnp.int32),
        "member_group": touch_ends(jax.random.randint(key_of[3], (MEMBERS,), 0, NGROUP), jax.random.fold_in(key_of[3], 1), 0, NGROUP - 1).astype(jnp.int32),
        "band_width": touch_ends(jax.random.randint(key_of[4], (NGROUP,), 1, BAND_MOST + 1), jax.random.fold_in(key_of[4], 1), 1, BAND_MOST).astype(jnp.int32),
        "zonal_rate": draw_zonal_rate(jax.random.fold_in(key_of[7], 71), 0),
        "meridional_rate": draw_meridional_rate(jax.random.fold_in(key_of[7], 71), 0),
    }


def gains_of(rate):
    remain = 1.0 - rate
    return (remain, (rate * (2.0 - rate)) ** 0.75 * (1.0 + remain * remain) ** (-0.25))

def zonal_sweep(field, decay, gain, backward):

    def advance(carry, column_cells):
        value = gain * column_cells + decay * carry
        return (value, value)
    return lax.scan(advance, jnp.zeros_like(field[0]), field, reverse=backward)[1]

def meridional_sweep(field, decay, gain, backward):

    def advance(carry, element):
        value = element[2] * element[0] + element[1] * carry
        return (value, value)
    return lax.scan(advance, jnp.zeros_like(field[0]), (field, decay, gain), reverse=backward)[1]

def reference(control, perturbation, slab_levels, member_group, band_width, zonal_rate, meridional_rate):
    level_index = jnp.arange(LEVELS, dtype=jnp.int32)
    slab_ends = jnp.cumsum(slab_levels).astype(jnp.int32)
    level_slab = lax.optimization_barrier(jnp.sum((level_index[:, None] >= slab_ends[None, :]).astype(jnp.int32), axis=1))
    zonal_decay, zonal_gain = gains_of(zonal_rate[level_slab])
    meridional_decay, meridional_gain = gains_of(meridional_rate[level_slab])
    row_decay = jnp.transpose(meridional_decay)[:, :, None]
    row_gain = jnp.transpose(meridional_gain)[:, :, None]
    spacing = (level_index[:, None] - level_index[None, :]).astype(jnp.float32)
    member_band = band_width[member_group].astype(jnp.float32)
    weight = 1.0 / math.sqrt(MEMBERS - 1)

    def add_member(running_sum, item):
        field_in, spread_field, band_reach = item
        kernel = jnp.where(jnp.abs(spacing) <= band_reach, jnp.exp(-2.0 * (spacing / band_reach) ** 2), 0.0).astype(jnp.bfloat16)
        column = jnp.dot(kernel, field_in.reshape(LEVELS, NY * NX), preferred_element_type=jnp.float32)
        column = column.astype(jnp.bfloat16).reshape(LEVELS, NY, NX)
        field = jnp.moveaxis(column.astype(jnp.float32), 2, 0)
        field = zonal_sweep(field, zonal_decay, zonal_gain, False)
        field = zonal_sweep(field, zonal_decay, zonal_gain, True)
        field = jnp.moveaxis(jnp.moveaxis(field, 0, 2), 1, 0)
        field = meridional_sweep(field, row_decay, row_gain, False)
        field = meridional_sweep(field, row_decay, row_gain, True)
        filtered = jnp.moveaxis(field, 0, 1).astype(jnp.bfloat16)
        return (running_sum + spread_field.astype(jnp.float32) * filtered.astype(jnp.float32), None)
    running_sum = lax.scan(add_member, jnp.zeros((LEVELS, NY, NX), jnp.float32), (control, perturbation, member_band))[0]
    return running_sum * weight
```

```python
import functools
import math

import jax
import jax.numpy as jnp
import numpy as np
from jax import lax
from jax.experimental import pallas as pl
from jax.experimental.pallas import tpu as pltpu
from jax.sharding import PartitionSpec as P

CHUNKS = 4
LANES = 128
ROW_GROUP = 16
VMEM_LIMIT = 48 * 1024 * 1024

F32 = jnp.float32
BF16 = jnp.bfloat16


def iota(shape, axis):
    return lax.broadcasted_iota(jnp.int32, shape, axis)


def log_decay(rate):
    t = rate / (2.0 - rate)
    s = t * t
    series = 1.0 + s * (1 / 3 + s * (1 / 5 + s * (1 / 7 + s * (1 / 9 + s * (1 / 11 + s / 13)))))
    return -2.0 * t * series


def split3(x):
    hi = x.astype(BF16)
    rest = x - hi.astype(F32)
    mid = rest.astype(BF16)
    return hi, mid, (rest - mid.astype(F32)).astype(BF16)


def split2(x):
    hi = x.astype(BF16)
    return hi, (x - hi.astype(F32)).astype(BF16)


def dot_nn(a, b):
    return lax.dot_general(a, b, (((1,), (0,)), ((), ())), preferred_element_type=F32)


def dot_nt(a, b):
    return lax.dot_general(a, b, (((1,), (1,)), ((), ())), preferred_element_type=F32)


def times_exact(x, zero_one):
    rows = x.shape[0]
    product = dot_nn(jnp.concatenate(split3(x), axis=0), zero_one)
    return product[:rows] + product[rows : 2 * rows] + product[2 * rows :]


def exact_times_t(zero_one, x):
    return sum(dot_nt(zero_one, part) for part in split3(x))


def level_of_place(place, levels, chunks, quarters):
    steps = levels // (chunks * quarters)
    in_chunk = steps * quarters
    chunk, rest = place // in_chunk, place % in_chunk
    return (rest // steps) * (levels // quarters) + chunk * steps + rest % steps


def traced_level(place, levels, chunks, quarters):
    steps = levels // (chunks * quarters)
    in_chunk = steps * quarters
    log_steps, log_chunk = int(math.log2(steps)), int(math.log2(in_chunk))
    chunk = jnp.right_shift(place, log_chunk)
    rest = jnp.bitwise_and(place, in_chunk - 1)
    return (
        jnp.right_shift(rest, log_steps) * (levels // quarters)
        + chunk * steps
        + jnp.bitwise_and(rest, steps - 1)
    )


def rates_by_place(slab_levels, rates, levels, quarters):
    slabs = rates.shape[0]
    level = traced_level(iota((levels, slabs), 0), levels, CHUNKS, quarters)
    index = jnp.zeros((levels, slabs), jnp.int32)
    end = jnp.int32(0)
    for s in range(slabs):
        end = end + slab_levels[s]
        index = index + (level >= end).astype(jnp.int32)
    chosen = (index == iota((levels, slabs), 1)).astype(F32).astype(BF16)
    return sum(dot_nn(chosen, part) for part in split3(rates))


def lane_of(table, lane):
    return jnp.take_along_axis(table, jnp.full(table.shape, lane, jnp.int32), axis=1)


def column_kernel(
    sizes, where_ref, slab_ref, group_ref, band_ref, control_ref, rate_ref,
    column_ref, decay_ref, gain_ref, end_ref, send1_ref, send2_ref, send3_ref,
    kron, decay_all,
):
    levels, rows, cols, quarters, lat_count = sizes
    step = pl.program_id(0)
    lat, lon = where_ref[1], where_ref[2]
    full = levels * 8

    @pl.when(step == 0)
    def _():
        band = band_ref[group_ref[0]].astype(F32)
        out_level = traced_level(jnp.right_shift(iota((full, full), 0), 3), levels, CHUNKS, quarters)
        spacing = out_level - jnp.right_shift(iota((full, full), 1), 3)
        same = jnp.bitwise_and(iota((full, full), 0), 7) == jnp.bitwise_and(iota((full, full), 1), 7)
        ratio = spacing.astype(F32) / band
        weight = jnp.exp(-2.0 * (ratio * ratio))
        keep = jnp.logical_and(same, jnp.abs(spacing).astype(F32) <= band)
        kron[...] = jnp.where(keep, weight, 0.0).astype(BF16)
        level_rates = rates_by_place(slab_ref, rate_ref[...], levels, quarters)
        own = iota((rows, rate_ref.shape[1]), 1) == lon * rows + iota((rows, rate_ref.shape[1]), 0)
        rate = exact_times_t(own.astype(F32).astype(BF16), level_rates)
        remain = 1.0 - rate
        decay_all[...] = log_decay(rate)
        decay_ref[...] = decay_all[...]
        gain_ref[...] = jnp.sqrt(rate * (2.0 - rate) / (1.0 + remain * remain))

    block = control_ref[0].astype(F32)
    halves = []
    for half in range(2):
        part = block[:, 8 * half : 8 * half + 8, :].reshape(full, cols).astype(BF16)
        halves.append(dot_nn(kron[...], part).reshape(levels, 8, cols))
    column = jnp.concatenate(halves, axis=1).astype(BF16)
    column_ref[...] = column

    log_a = decay_all[pl.ds(step * ROW_GROUP, ROW_GROUP), :]
    lane = iota((ROW_GROUP, LANES), 1).astype(F32)
    place_lane = iota((ROW_GROUP, levels), 1)
    forward = jnp.zeros((ROW_GROUP, levels), F32)
    backward = jnp.zeros((ROW_GROUP, levels), F32)
    blocks = cols // LANES
    for place in range(levels):
        log_b = jnp.broadcast_to(log_a[:, place : place + 1], (ROW_GROUP, LANES))
        over = jnp.exp(log_b * float(LANES))
        x = column_ref[place].astype(F32)
        parts = [x[:, LANES * b : LANES * (b + 1)] for b in range(blocks)]
        along, against = parts[0], parts[-1]
        for b in range(1, blocks):
            along = parts[b] + over * along
            against = parts[-1 - b] + over * against
        along = jnp.sum(along * jnp.exp(log_b * (LANES - 1.0 - lane)), axis=1, keepdims=True)
        against = jnp.sum(against * jnp.exp(log_b * lane), axis=1, keepdims=True)
        forward = jnp.where(place_lane == place, along, forward)
        backward = jnp.where(place_lane == place, against, backward)
    power = (1 + cols * (2 * (lat_count - 1 - lat) + 1)).astype(F32)
    returning = backward - jnp.exp(log_a * power) * forward
    end_ref[...] = forward
    for shift, ref in ((1, send1_ref), (2, send2_ref), (3, send3_ref)):
        ref[...] = jnp.where(lat + shift < lat_count, forward, returning)


def row_kernel(
    sizes, where_ref, slab_ref, rate_ref,
    left_ref, left_sum_ref, right_ref, right_sum_ref, chain_ref,
):
    levels, rows, quarters, lon_count = sizes
    lon = where_ref[2]
    total = rate_ref.shape[1]
    rate = rates_by_place(slab_ref, rate_ref[...], levels, quarters)
    remain = 1.0 - rate
    root = jnp.sqrt(rate * (2.0 - rate))
    gain = root * jnp.sqrt(root) / jnp.sqrt(jnp.sqrt(1.0 + remain * remain))
    log_c = log_decay(rate)
    owner = lambda at: jnp.right_shift(at * ((1 << 16) // rows + 1), 16)
    first, second = iota((total, total), 0), iota((total, total), 1)
    same = owner(first) == owner(second)
    upper = jnp.logical_and(same, first <= second).astype(F32).astype(BF16)
    lower = jnp.logical_and(same, first >= second).astype(F32).astype(BF16)
    running = times_exact(log_c, upper)
    before = running - log_c
    weight = gain * jnp.exp(running + before)
    sums = times_exact(weight, lower)
    left = jnp.exp(-before)
    right = gain * jnp.exp(-running)
    own = (iota((rows, total), 1) == lon * rows + iota((rows, total), 0)).astype(F32).astype(BF16)
    own_t = (iota((total, rows), 0) == lon * rows + iota((total, rows), 1)).astype(F32).astype(BF16)
    left_ref[...] = exact_times_t(own, left)
    left_sum_ref[...] = exact_times_t(own, left * sums)
    right_ref[...] = times_exact(right, own_t)
    right_sum_ref[...] = times_exact(right * sums, own_t)

    inside = (owner(iota((total, LANES), 0)) == iota((total, LANES), 1)).astype(F32).astype(BF16)
    log_over = times_exact(log_c, inside)
    bounce = times_exact(weight, inside)
    source, target = iota((LANES, LANES), 0), iota((LANES, LANES), 1)
    between = jnp.logical_and(source > lon, source < target).astype(F32).astype(BF16)
    device = iota((levels, LANES), 1)
    beyond = jnp.logical_and(device > lon, device < lon_count)
    echo = jnp.sum(
        jnp.where(beyond, bounce * jnp.exp(2.0 * times_exact(log_over, between)), 0.0),
        axis=1,
        keepdims=True,
    )
    over = jnp.sum(jnp.where(device == lon, jnp.exp(log_over), 0.0), axis=1, keepdims=True)
    origin = jnp.where(lon >= target, lon - target, lon - target + lon_count)
    low, high = jnp.minimum(origin, lon), jnp.maximum(origin, lon)
    path = jnp.logical_and(source > low, source < high).astype(F32).astype(BF16)
    reach = jnp.exp(times_exact(log_over, path))
    shift = device
    along = jnp.where(jnp.logical_and(shift >= 1, shift <= lon), reach, 0.0)
    against = jnp.where(jnp.logical_and(shift > lon, shift < lon_count), reach, 0.0)
    lane = device
    chain = jnp.where(lane < lon_count, along, 0.0)
    chain = chain + jnp.concatenate(
        [jnp.zeros((levels, 64), F32), against[:, :64]], axis=1
    )
    chain = jnp.where(lane == 32, over, chain)
    chain_ref[...] = jnp.where(lane == 33, echo, chain)


def field_kernel(
    sizes, where_ref, column_ref, decay_ref, gain_ref, end_ref, got1_ref, got2_ref, got3_ref,
    left_ref, left_sum_ref, right_ref, right_sum_ref, chain_ref, triangle_ref,
    field_ref, out_end_ref, *rest,
):
    rows, cols, chunk, in_chunk, per_step, lat_count, lon_count = sizes
    send_refs = rest[: lon_count - 1]
    tables, rights, edges = rest[lon_count - 1 :]
    step = pl.program_id(0)
    lat, lon = where_ref[1], where_ref[2]
    blocks = cols // LANES

    @pl.when(step == 0)
    def _():
        log_a, gain = decay_ref[...], gain_ref[...]
        enter_left = jnp.zeros(log_a.shape, F32)
        enter_right = jnp.zeros(log_a.shape, F32)
        for shift, ref in ((1, got1_ref), (2, got2_ref), (3, got3_ref)):
            got = ref[...]
            is_left = lat >= shift
            power = jnp.where(is_left, shift - 1, lat_count - 1 - shift) * cols
            scaled = jnp.exp(log_a * power.astype(F32)) * got
            enter_left = enter_left + jnp.where(is_left, scaled, 0.0)
            enter_right = enter_right + jnp.where(is_left, 0.0, scaled)
        leaving = end_ref[...] + jnp.exp(log_a * float(cols)) * enter_left
        power = (1 + 2 * cols * (lat_count - 1 - lat)).astype(F32)
        enter_right = enter_right - jnp.exp(log_a * power) * leaving
        enter_left = gain * jnp.exp(log_a) * enter_left
        enter_right = gain * jnp.exp(log_a * float(LANES)) * enter_right
        tables[0] = jnp.concatenate([log_a, gain], axis=1)
        tables[1] = jnp.concatenate([enter_left, enter_right], axis=1)
        tables[2] = jnp.concatenate([left_ref[...], left_sum_ref[...]], axis=1)

    half = tables.shape[2] // 2
    lane = iota((rows, LANES), 1).astype(F32)
    triangle = triangle_ref[...]
    below = iota((rows, rows), 0) >= iota((rows, rows), 1)
    row_number = iota((8, rows), 0)
    for u in range(per_step):
        row = step * per_step + u
        place = chunk * in_chunk + row
        log_a = lane_of(tables[0], place)
        gain = lane_of(tables[0], place + half)
        from_left = lane_of(tables[1], place)
        from_right = lane_of(tables[1], place + half)
        left = lane_of(tables[2], place)[:, :rows]
        left_sum = lane_of(tables[2], place + half)[:, :rows]
        grow = jnp.exp(log_a * lane)
        shrink = jnp.exp(log_a * (-lane))
        over = jnp.exp(log_a * float(LANES))
        decay = jnp.exp(log_a)
        gain_grow, gain_shrink = gain * grow, gain * shrink
        x = column_ref[u].astype(F32)
        parts = [x[:, LANES * b : LANES * (b + 1)] for b in range(blocks)]
        scaled = jnp.concatenate(
            [jnp.concatenate([p * gain_shrink, p * gain_grow], axis=1) for p in parts], axis=0
        )
        high, low = split2(scaled)
        sums = dot_nn(high, triangle) + dot_nn(low, triangle)
        ahead = [grow * sums[rows * b : rows * (b + 1), :LANES] for b in range(blocks)]
        behind = [sums[rows * b : rows * (b + 1), LANES:] for b in range(blocks)]
        lefts, rights_in = [from_left], [from_right]
        for b in range(blocks - 1):
            end = jnp.broadcast_to(ahead[b][:, LANES - 1 :], (rows, LANES))
            lefts.append(over * lefts[-1] + decay * end)
        for b in range(blocks - 1, 0, -1):
            whole = behind[b] + scaled[rows * b : rows * (b + 1), LANES:]
            end = jnp.broadcast_to(whole[:, :1], (rows, LANES))
            rights_in.append(over * (rights_in[-1] + end))
        rights_in = rights_in[::-1]
        field = jnp.concatenate(
            [
                ahead[b] + grow * lefts[b] + shrink * (behind[b] + rights_in[b])
                for b in range(blocks)
            ],
            axis=1,
        )
        right = right_ref[pl.ds(row, 1), :]
        right_sum = right_sum_ref[pl.ds(row, 1), :]
        matrix = jnp.where(below, left_sum * right, left * right_sum)
        extra = jnp.where(row_number == 0, right, jnp.where(row_number == 1, right_sum, 0.0))
        matrix_high, matrix_low = split2(jnp.concatenate([matrix, extra], axis=0))
        field_high, field_low = split2(field)
        result = (
            dot_nn(matrix_high, field_high)
            + dot_nn(matrix_high, field_low)
            + dot_nn(matrix_low, field_high)
        )
        field_ref[u] = result[:rows]
        chain = chain_ref[pl.ds(row, 1), :]
        over_rows, echo = chain[:, 32:33], chain[:, 33:34]
        end = over_rows * result[rows : rows + 1]
        edges[0, pl.ds(row, 1), :] = end
        edges[1, pl.ds(row, 1), :] = result[rows + 1 : rows + 2] + over_rows * echo * end

    @pl.when(step == pl.num_programs(0) - 1)
    def _():
        end, returning = edges[0], edges[1]
        out_end_ref[...] = end
        for shift, ref in enumerate(send_refs, 1):
            ref[...] = jnp.where(lon + shift < lon_count, end, returning)


def product(field, left, left_sum, enter, leave, spread):
    filtered = field + left_sum * enter + left * leave
    return spread.astype(F32) * filtered.astype(BF16).astype(F32)


def wide_lane(table_ref, lane, cols):
    one = lane_of(table_ref[...], lane)
    return jnp.concatenate([one] * (cols // LANES), axis=1)


def one_product(field_ref, spread_ref, table_ref, enter_ref, leave_ref, chunk, in_chunk, row, u):
    cols = field_ref.shape[-1]
    place = chunk * in_chunk + row
    half = table_ref.shape[1] // 2
    left = wide_lane(table_ref, place, cols)
    left_sum = wide_lane(table_ref, place + half, cols)
    enter, leave = enter_ref[pl.ds(row, 1), :], leave_ref[pl.ds(row, 1), :]
    return product(field_ref[u], left, left_sum, enter, leave, spread_ref[0, u])


def first_kernel(sizes, where_ref, *refs):
    chunk, in_chunk, steps, quarters, lon_count = sizes
    got_refs = refs[: lon_count - 1]
    end_ref, chain_ref, left_ref, left_sum_ref, field_ref, spread_ref = refs[lon_count - 1 : lon_count + 5]
    enter_ref, leave_ref, table_ref, up_ref, down_ref = refs[lon_count + 5 :]
    chain = chain_ref[...]
    enter = jnp.zeros(end_ref.shape, F32)
    leave = jnp.zeros(end_ref.shape, F32)
    for shift, ref in enumerate(got_refs, 1):
        got = ref[...]
        enter = enter + chain[:, shift : shift + 1] * got
        leave = leave + chain[:, 64 + shift : 65 + shift] * got
    over, echo = chain[:, 32:33], chain[:, 33:34]
    enter_ref[...] = enter
    leave_ref[...] = over * (leave + echo * (end_ref[...] + over * enter))
    table_ref[...] = jnp.concatenate([left_ref[...], left_sum_ref[...]], axis=1)
    quarter = lax.rem(where_ref[0] + 2, quarters)
    for u in range(steps):
        value = one_product(
            field_ref, spread_ref, table_ref, enter_ref, leave_ref, chunk, in_chunk, quarter * steps + u, u
        ).astype(BF16)
        if u < steps // 2:
            up_ref[u] = value
        else:
            down_ref[u - steps // 2] = value


def second_kernel(
    sizes, where_ref, field1_ref, spread1_ref, field3_ref, spread3_ref, enter_ref, leave_ref, table_ref,
    up_ref, down_ref, out1_ref, out3_ref,
):
    chunk, in_chunk, steps, quarters = sizes
    for u in range(steps):
        for turn, field_ref, spread_ref, out_ref in (
            (1, field1_ref, spread1_ref, out1_ref),
            (3, field3_ref, spread3_ref, out3_ref),
        ):
            quarter = lax.rem(where_ref[0] + turn, quarters)
            value = one_product(
                field_ref, spread_ref, table_ref, enter_ref, leave_ref, chunk, in_chunk, quarter * steps + u, u
            )
            if turn == 1 and u < steps // 2:
                value = value + up_ref[u].astype(F32)
            if turn == 3 and u >= steps // 2:
                value = value + down_ref[u - steps // 2].astype(F32)
            out_ref[u] = value.astype(BF16)


def third_kernel(
    sizes, where_ref, field_ref, spread_ref, enter_ref, leave_ref, table_ref, got1_ref, got3_ref, *rest
):
    chunk, in_chunk, steps, scale = sizes
    out_ref = rest[-1]
    for u in range(steps):
        value = one_product(
            field_ref, spread_ref, table_ref, enter_ref, leave_ref, chunk, in_chunk, where_ref[0] * steps + u, u
        )
        out_ref[u] = (value + got1_ref[u].astype(F32) + got3_ref[u].astype(F32)) * scale


def whole(shape):
    return pl.BlockSpec(shape, lambda *_: (0,) * len(shape))


def smem():
    return pl.BlockSpec(memory_space=pltpu.SMEM)


def call(kernel, name, inputs, in_specs, outputs, out_specs, scratch=(), grid=(1,), aliases=None, cost=None):
    return pl.pallas_call(
        kernel,
        out_shape=outputs,
        grid_spec=pltpu.PrefetchScalarGridSpec(
            num_scalar_prefetch=1,
            grid=grid,
            in_specs=in_specs,
            out_specs=out_specs,
            scratch_shapes=list(scratch),
        ),
        input_output_aliases=aliases or {},
        compiler_params=pltpu.CompilerParams(vmem_limit_bytes=VMEM_LIMIT),
        cost_estimate=cost,
        name=name,
    )(*inputs)


def cost(flops, data):
    return pl.CostEstimate(flops=flops, bytes_accessed=data, transcendentals=0)


def triangle_table():
    at = np.arange(LANES)
    table = np.zeros((2 * LANES, 2 * LANES), np.float32)
    table[:LANES, :LANES] = at[:, None] <= at[None, :]
    table[LANES:, LANES:] = at[:, None] > at[None, :]
    return jnp.asarray(table, BF16)


def ring(axis, shift):
    count = lax.axis_size(axis)
    return [(i, (i + shift) % count) for i in range(count)]


def per_device(control, perturbation, slab_levels, member_group, band_width, zonal_rate, meridional_rate):
    _, levels, rows, cols = control.shape
    quarters, lat_count, lon_count = (lax.axis_size(a) for a in ("mem", "lat", "lon"))
    steps = levels // (CHUNKS * quarters)
    in_chunk = steps * quarters
    total_rows = zonal_rate.shape[1]
    where = jnp.stack([lax.axis_index(a) for a in ("mem", "lat", "lon")]).astype(jnp.int32)
    sds = jax.ShapeDtypeStruct
    table = sds((rows, levels), F32)
    table_spec = pl.BlockSpec((ROW_GROUP, levels), lambda g, _: (g, 0))

    column, decay, gain, end, *sends = call(
        functools.partial(column_kernel, (levels, rows, cols, quarters, lat_count)),
        "vertical_columns",
        (where, slab_levels, member_group, band_width, control, zonal_rate),
        [
            smem(), smem(), smem(),
            pl.BlockSpec((1, levels, ROW_GROUP, cols), lambda g, _: (0, 0, g, 0)),
            whole(zonal_rate.shape),
        ],
        (sds((levels, rows, cols), BF16), table, table, table, table, table, table),
        (
            pl.BlockSpec((levels, ROW_GROUP, cols), lambda g, _: (0, g, 0)),
            whole((rows, levels)), whole((rows, levels)),
            table_spec, table_spec, table_spec, table_spec,
        ),
        scratch=[pltpu.VMEM((levels * 8, levels * 8), BF16), pltpu.VMEM((rows, levels), F32)],
        grid=(rows // ROW_GROUP,),
        cost=cost(2 * 512 * 512 * 384 * 12, 2 * levels * rows * cols * 2),
    )
    got = [lax.ppermute(s, "lat", ring("lat", i + 1)) for i, s in enumerate(sends)]
    left, left_sum, right, right_sum, chain = call(
        functools.partial(row_kernel, (levels, rows, quarters, lon_count)),
        "row_terms",
        (where, slab_levels, meridional_rate),
        [smem(), whole(meridional_rate.shape)],
        (table, table, sds((levels, rows), F32), sds((levels, rows), F32), sds((levels, LANES), F32)),
        (
            whole((rows, levels)), whole((rows, levels)),
            whole((levels, rows)), whole((levels, rows)), whole((levels, LANES)),
        ),
        cost=cost(2 * 3 * 64 * 768 * 768 * 2, 1 << 20),
    )

    triangle = triangle_table()
    scale = 1.0 / math.sqrt(control.shape[0] * quarters - 1)
    plane = rows * cols
    row_spec = pl.BlockSpec((in_chunk, cols), lambda *_: (0, 0))
    fields, ends, far = [], [], []
    for c in range(CHUNKS):
        by_place = lambda width: pl.BlockSpec((in_chunk, width), lambda g, _, c=c: (c, 0))
        field, out_end, *out_sends = call(
            functools.partial(field_kernel, (rows, cols, c, in_chunk, steps, lat_count, lon_count)),
            "zonal_rows",
            (where, column, decay, gain, end, *got, left, left_sum, right, right_sum, chain, triangle),
            [pl.BlockSpec((steps, rows, cols), lambda g, _, c=c: (c * quarters + g, 0, 0))]
            + [whole((rows, levels))] * 8
            + [by_place(rows), by_place(rows), by_place(LANES), whole(triangle.shape)],
            (sds((in_chunk, rows, cols), F32),) + (sds((in_chunk, cols), F32),) * lon_count,
            (pl.BlockSpec((steps, rows, cols), lambda g, _: (g, 0, 0)),) + (row_spec,) * lon_count,
            scratch=[
                pltpu.VMEM((3, rows, 2 * levels), F32),
                pltpu.VMEM((8, LANES), F32),
                pltpu.VMEM((2, in_chunk, cols), F32),
            ],
            grid=(quarters,),
            cost=cost(in_chunk * plane * 2 * 1024, in_chunk * plane * 6),
        )
        fields.append(field)
        ends.append(out_end)
        far.append([lax.ppermute(s, "lon", ring("lon", i + 1)) for i, s in enumerate(out_sends)])

    quarter_field = lambda turn: pl.BlockSpec(
        (steps, rows, cols), lambda g, w: (lax.rem(w[0] + turn, quarters), 0, 0)
    )
    quarter_spread = lambda turn, c: pl.BlockSpec(
        (1, steps, rows, cols), lambda g, w: (0, lax.rem(w[0] + turn, quarters) * CHUNKS + c, 0, 0)
    )
    piece = sds((steps, rows, cols), BF16)
    half_piece = sds((steps // 2, rows, cols), BF16)
    table_wide = sds((rows, 2 * levels), F32)
    row_pair = (row_spec, row_spec, whole((rows, 2 * levels)))
    arrived = []
    for c in range(CHUNKS):
        enter, leave, lanes, up, down = call(
            functools.partial(first_kernel, (c, in_chunk, steps, quarters, lon_count)),
            "first_products",
            (where, *far[c], ends[c], chain, left, left_sum, fields[c], perturbation),
            [row_spec] * lon_count
            + [
                pl.BlockSpec((in_chunk, LANES), lambda g, _, c=c: (c, 0)),
                whole((rows, levels)), whole((rows, levels)),
                quarter_field(2), quarter_spread(2, c),
            ],
            (sds((in_chunk, cols), F32), sds((in_chunk, cols), F32), table_wide, half_piece, half_piece),
            row_pair + (whole(half_piece.shape), whole(half_piece.shape)),
            cost=cost(steps * plane * 8, steps * plane * 8),
        )
        up = lax.ppermute(up, "mem", ring("mem", 1))
        down = lax.ppermute(down, "mem", ring("mem", -1))
        arrived.append((enter, leave, lanes, up, down))
    result = None
    gathered = []
    for c in range(CHUNKS):
        enter, leave, lanes, up, down = arrived[c]
        out1, out3 = call(
            functools.partial(second_kernel, (c, in_chunk, steps, quarters)),
            "second_products",
            (where, fields[c], perturbation, fields[c], perturbation, enter, leave, lanes, up, down),
            [quarter_field(1), quarter_spread(1, c), quarter_field(3), quarter_spread(3, c)]
            + list(row_pair)
            + [whole(half_piece.shape), whole(half_piece.shape)],
            (piece, piece),
            (whole(piece.shape), whole(piece.shape)),
            cost=cost(2 * steps * plane * 8, 2 * steps * plane * 8),
        )
        gathered.append(
            (lax.ppermute(out1, "mem", ring("mem", 1)), lax.ppermute(out3, "mem", ring("mem", -1)))
        )
    for c in range(CHUNKS):
        enter, leave, lanes, _, _ = arrived[c]
        extra = () if result is None else (result,)
        result = call(
            functools.partial(third_kernel, (c, in_chunk, steps, scale)),
            "third_products",
            (where, fields[c], perturbation, enter, leave, lanes, *gathered[c], *extra),
            [quarter_field(0), quarter_spread(0, c), *row_pair, whole(piece.shape), whole(piece.shape)]
            + [pl.BlockSpec(memory_space=pl.ANY)] * len(extra),
            sds((levels // quarters, rows, cols), F32),
            pl.BlockSpec((steps, rows, cols), lambda g, _, c=c: (c, 0, 0)),
            aliases={8: 0} if extra else None,
            cost=cost(steps * plane * 8, steps * plane * 14),
        )
    return result


def solution(mesh):
    return jax.shard_map(
        per_device,
        mesh=mesh,
        in_specs=(
            P("mem", None, "lon", "lat"),
            P("mem", None, "lon", "lat"),
            P(),
            P("mem"),
            P(),
            P(),
            P(),
        ),
        out_specs=P("mem", "lon", "lat"),
        check_vma=False,
    )
```

```python
import functools
import math

import jax
import jax.numpy as jnp
import numpy as np
from jax import lax
from jax.experimental import pallas as pl
from jax.experimental.pallas import tpu as pltpu
from jax.sharding import PartitionSpec as P

CHUNKS = 2
LANES = 128
GROUP_AT = 3
BAND_AT = 4
SLAB_AT = 8
ROW_GROUP = 16
FIELD_STEP = 4
PRODUCT_STEP = 2
VMEM_LIMIT = 48 * 1024 * 1024

F32 = jnp.float32
BF16 = jnp.bfloat16


def iota(shape, axis):
    return lax.broadcasted_iota(jnp.int32, shape, axis)


def log_decay(rate):
    t = rate / (2.0 - rate)
    s = t * t
    series = 1.0 + s * (1 / 3 + s * (1 / 5 + s * (1 / 7 + s * (1 / 9 + s * (1 / 11 + s / 13)))))
    return -2.0 * t * series


def split3(x):
    hi = x.astype(BF16)
    rest = x - hi.astype(F32)
    mid = rest.astype(BF16)
    return hi, mid, (rest - mid.astype(F32)).astype(BF16)


def split2(x):
    hi = x.astype(BF16)
    return hi, (x - hi.astype(F32)).astype(BF16)


def dot_nn(a, b):
    return lax.dot_general(a, b, (((1,), (0,)), ((), ())), preferred_element_type=F32)


def dot_nt(a, b):
    return lax.dot_general(a, b, (((1,), (1,)), ((), ())), preferred_element_type=F32)


def times_exact(x, zero_one):
    rows = x.shape[0]
    product = dot_nn(jnp.concatenate(split3(x), axis=0), zero_one)
    return product[:rows] + product[rows : 2 * rows] + product[2 * rows :]


def exact_times_t(zero_one, x):
    return sum(dot_nt(zero_one, part) for part in split3(x))


def level_of_place(place, levels, chunks, quarters):
    steps = levels // (chunks * quarters)
    in_chunk = steps * quarters
    chunk, rest = place // in_chunk, place % in_chunk
    return (rest // steps) * (levels // quarters) + chunk * steps + rest % steps


def traced_level(place, levels, chunks, quarters):
    steps = levels // (chunks * quarters)
    in_chunk = steps * quarters
    log_steps, log_chunk = int(math.log2(steps)), int(math.log2(in_chunk))
    chunk = jnp.right_shift(place, log_chunk)
    rest = jnp.bitwise_and(place, in_chunk - 1)
    return (
        jnp.right_shift(rest, log_steps) * (levels // quarters)
        + chunk * steps
        + jnp.bitwise_and(rest, steps - 1)
    )


def rates_by_place(slab_levels, rates, levels, quarters):
    slabs = rates.shape[0]
    level = traced_level(iota((levels, slabs), 0), levels, CHUNKS, quarters)
    index = jnp.zeros((levels, slabs), jnp.int32)
    end = jnp.int32(0)
    for s in range(slabs):
        end = end + slab_levels[SLAB_AT + s]
        index = index + (level >= end).astype(jnp.int32)
    chosen = (index == iota((levels, slabs), 1)).astype(F32).astype(BF16)
    return sum(dot_nn(chosen, part) for part in split3(rates))


def lane_of(table, lane):
    return jnp.take_along_axis(table, jnp.full(table.shape, lane, jnp.int32), axis=1)


def column_kernel(
    sizes, where_ref, control_ref, rate_ref,
    column_ref, decay_ref, gain_ref, end_ref, send1_ref, send2_ref, send3_ref,
    kron, decay_all, weighted,
):
    levels, rows, cols, quarters, lat_count = sizes
    step = pl.program_id(0)
    lat, lon = where_ref[1], where_ref[2]
    full = levels * 8

    @pl.when(step == 0)
    def _():
        band = where_ref[BAND_AT + where_ref[GROUP_AT]].astype(F32)
        out_level = traced_level(jnp.right_shift(iota((full, full), 0), 3), levels, CHUNKS, quarters)
        spacing = out_level - jnp.right_shift(iota((full, full), 1), 3)
        same = jnp.bitwise_and(iota((full, full), 0), 7) == jnp.bitwise_and(iota((full, full), 1), 7)
        ratio = spacing.astype(F32) / band
        weight = jnp.exp(-2.0 * (ratio * ratio))
        keep = jnp.logical_and(same, jnp.abs(spacing).astype(F32) <= band)
        kron[...] = jnp.where(keep, weight, 0.0).astype(BF16)
        level_rates = rates_by_place(where_ref, rate_ref[...], levels, quarters)
        own = iota((rows, rate_ref.shape[1]), 1) == lon * rows + iota((rows, rate_ref.shape[1]), 0)
        rate = exact_times_t(own.astype(F32).astype(BF16), level_rates)
        remain = 1.0 - rate
        decay_all[...] = log_decay(rate)
        decay_ref[...] = decay_all[...]
        gain_ref[...] = jnp.sqrt(rate * (2.0 - rate) / (1.0 + remain * remain))

    block = control_ref[0].astype(F32)
    halves = []
    for half in range(2):
        part = block[:, 8 * half : 8 * half + 8, :].reshape(full, cols).astype(BF16)
        halves.append(dot_nn(kron[...], part).reshape(levels, 8, cols))
    column = jnp.concatenate(halves, axis=1).astype(BF16)
    column_ref[...] = column

    log_a = decay_all[pl.ds(step * ROW_GROUP, ROW_GROUP), :]
    lane = iota((ROW_GROUP, LANES), 1).astype(F32)
    blocks = cols // LANES
    for place in range(levels):
        log_b = jnp.broadcast_to(log_a[:, place : place + 1], (ROW_GROUP, LANES))
        over = jnp.exp(log_b * float(LANES))
        x = column_ref[place].astype(F32)
        parts = [x[:, LANES * b : LANES * (b + 1)] for b in range(blocks)]
        along, against = parts[0], parts[-1]
        for b in range(1, blocks):
            along = parts[b] + over * along
            against = parts[-1 - b] + over * against
        weighted[0, place] = along * jnp.exp(log_b * (LANES - 1.0 - lane))
        weighted[1, place] = against * jnp.exp(log_b * lane)
    place_lane = iota((ROW_GROUP, levels), 1)
    forward = jnp.zeros((ROW_GROUP, levels), F32)
    backward = jnp.zeros((ROW_GROUP, levels), F32)
    for place in range(levels):
        along = jnp.sum(weighted[0, place], axis=1, keepdims=True)
        against = jnp.sum(weighted[1, place], axis=1, keepdims=True)
        forward = jnp.where(place_lane == place, along, forward)
        backward = jnp.where(place_lane == place, against, backward)
    power = (1 + cols * (2 * (lat_count - 1 - lat) + 1)).astype(F32)
    returning = backward - jnp.exp(log_a * power) * forward
    end_ref[...] = forward
    for shift, ref in ((1, send1_ref), (2, send2_ref), (3, send3_ref)):
        ref[...] = jnp.where(lat + shift < lat_count, forward, returning)


def row_kernel(
    sizes, where_ref, rate_ref,
    left_ref, left_sum_ref, right_ref, right_sum_ref, chain_ref,
):
    levels, rows, quarters, lon_count = sizes
    lon = where_ref[2]
    total = rate_ref.shape[1]
    rate = rates_by_place(where_ref, rate_ref[...], levels, quarters)
    remain = 1.0 - rate
    root = jnp.sqrt(rate * (2.0 - rate))
    gain = root * jnp.sqrt(root) / jnp.sqrt(jnp.sqrt(1.0 + remain * remain))
    log_c = log_decay(rate)
    owner = lambda at: jnp.right_shift(at * ((1 << 16) // rows + 1), 16)
    first, second = iota((total, total), 0), iota((total, total), 1)
    same = owner(first) == owner(second)
    upper = jnp.logical_and(same, first <= second).astype(F32).astype(BF16)
    lower = jnp.logical_and(same, first >= second).astype(F32).astype(BF16)
    running = times_exact(log_c, upper)
    before = running - log_c
    weight = gain * jnp.exp(running + before)
    sums = times_exact(weight, lower)
    left = jnp.exp(-before)
    right = gain * jnp.exp(-running)
    own = (iota((rows, total), 1) == lon * rows + iota((rows, total), 0)).astype(F32).astype(BF16)
    own_t = (iota((total, rows), 0) == lon * rows + iota((total, rows), 1)).astype(F32).astype(BF16)
    left_ref[...] = exact_times_t(own, left)
    left_sum_ref[...] = exact_times_t(own, left * sums)
    right_ref[...] = times_exact(right, own_t)
    right_sum_ref[...] = times_exact(right * sums, own_t)

    inside = (owner(iota((total, LANES), 0)) == iota((total, LANES), 1)).astype(F32).astype(BF16)
    log_over = times_exact(log_c, inside)
    bounce = times_exact(weight, inside)
    source, target = iota((LANES, LANES), 0), iota((LANES, LANES), 1)
    between = jnp.logical_and(source > lon, source < target).astype(F32).astype(BF16)
    device = iota((levels, LANES), 1)
    beyond = jnp.logical_and(device > lon, device < lon_count)
    echo = jnp.sum(
        jnp.where(beyond, bounce * jnp.exp(2.0 * times_exact(log_over, between)), 0.0),
        axis=1,
        keepdims=True,
    )
    every = jnp.exp(log_over)
    over = jnp.sum(jnp.where(device == lon, every, 0.0), axis=1, keepdims=True)
    partner = jnp.bitwise_xor(lon, 1)
    partner_over = jnp.sum(jnp.where(device == partner, every, 0.0), axis=1, keepdims=True)
    pair, pairs = jnp.right_shift(lon, 1), lon_count // 2
    shift = jnp.bitwise_and(target, 63)
    is_before = pair >= shift
    low = jnp.where(is_before, 2 * (pair - shift) + 1, lon)
    high = jnp.where(is_before, lon, 2 * (pair - shift + pairs))
    path = jnp.logical_and(source > low, source < high).astype(F32).astype(BF16)
    reach = jnp.exp(times_exact(log_over, path))
    shift = jnp.bitwise_and(device, 63)
    counted = jnp.logical_and(shift >= 1, shift < pairs)
    counted = jnp.logical_and(counted, (pair >= shift) == (device < 64))
    chain = jnp.where(counted, reach, 0.0)
    for at, value in ((32, over), (33, echo), (34, partner_over)):
        chain = jnp.where(device == at, value, chain)
    chain_ref[...] = chain


def field_kernel(
    sizes, where_ref, column_ref, decay_ref, gain_ref, end_ref, got1_ref, got2_ref, got3_ref,
    left_ref, left_sum_ref, right_ref, right_sum_ref, chain_ref, triangle_ref,
    field_ref, edge_ref, tables,
):
    rows, cols, chunk, in_chunk, per_step, lat_count = sizes
    step = pl.program_id(0)
    lat = where_ref[1]
    blocks = cols // LANES

    @pl.when(step == 0)
    def _():
        log_a, gain = decay_ref[...], gain_ref[...]
        enter_left = jnp.zeros(log_a.shape, F32)
        enter_right = jnp.zeros(log_a.shape, F32)
        for shift, ref in ((1, got1_ref), (2, got2_ref), (3, got3_ref)):
            got = ref[...]
            is_left = lat >= shift
            power = jnp.where(is_left, shift - 1, lat_count - 1 - shift) * cols
            scaled = jnp.exp(log_a * power.astype(F32)) * got
            enter_left = enter_left + jnp.where(is_left, scaled, 0.0)
            enter_right = enter_right + jnp.where(is_left, 0.0, scaled)
        leaving = end_ref[...] + jnp.exp(log_a * float(cols)) * enter_left
        power = (1 + 2 * cols * (lat_count - 1 - lat)).astype(F32)
        enter_right = enter_right - jnp.exp(log_a * power) * leaving
        enter_left = gain * jnp.exp(log_a) * enter_left
        enter_right = gain * jnp.exp(log_a * float(LANES)) * enter_right
        tables[0] = jnp.concatenate([log_a, gain], axis=1)
        tables[1] = jnp.concatenate([enter_left, enter_right], axis=1)
        tables[2] = jnp.concatenate([left_ref[...], left_sum_ref[...]], axis=1)

    half = tables.shape[2] // 2
    lane = iota((rows, LANES), 1).astype(F32)
    triangle = triangle_ref[...]
    below = iota((rows, rows), 0) >= iota((rows, rows), 1)
    row_number = iota((8, rows), 0)
    for u in range(per_step):
        row = step * per_step + u
        place = chunk * in_chunk + row
        log_a = lane_of(tables[0], place)
        gain = lane_of(tables[0], place + half)
        from_left = lane_of(tables[1], place)
        from_right = lane_of(tables[1], place + half)
        left = lane_of(tables[2], place)[:, :rows]
        left_sum = lane_of(tables[2], place + half)[:, :rows]
        grow = jnp.exp(log_a * lane)
        shrink = jnp.exp(log_a * (-lane))
        over = jnp.exp(log_a * float(LANES))
        decay = jnp.exp(log_a)
        gain_grow, gain_shrink = gain * grow, gain * shrink
        x = column_ref[u].astype(F32)
        parts = [x[:, LANES * b : LANES * (b + 1)] for b in range(blocks)]
        scaled = jnp.concatenate(
            [jnp.concatenate([p * gain_shrink, p * gain_grow], axis=1) for p in parts], axis=0
        )
        high, low = split2(scaled)
        sums = dot_nn(high, triangle) + dot_nn(low, triangle)
        ahead = [grow * sums[rows * b : rows * (b + 1), :LANES] for b in range(blocks)]
        behind = [sums[rows * b : rows * (b + 1), LANES:] for b in range(blocks)]
        lefts, rights_in = [from_left], [from_right]
        for b in range(blocks - 1):
            end = jnp.broadcast_to(ahead[b][:, LANES - 1 :], (rows, LANES))
            lefts.append(over * lefts[-1] + decay * end)
        for b in range(blocks - 1, 0, -1):
            whole = behind[b] + scaled[rows * b : rows * (b + 1), LANES:]
            end = jnp.broadcast_to(whole[:, :1], (rows, LANES))
            rights_in.append(over * (rights_in[-1] + end))
        rights_in = rights_in[::-1]
        field = jnp.concatenate(
            [
                ahead[b] + grow * lefts[b] + shrink * (behind[b] + rights_in[b])
                for b in range(blocks)
            ],
            axis=1,
        )
        right = right_ref[pl.ds(row, 1), :]
        right_sum = right_sum_ref[pl.ds(row, 1), :]
        matrix = jnp.where(below, left_sum * right, left * right_sum)
        extra = jnp.where(row_number == 0, right, jnp.where(row_number == 1, right_sum, 0.0))
        matrix_high, matrix_low = split2(jnp.concatenate([matrix, extra], axis=0))
        field_high, field_low = split2(field)
        result = (
            dot_nn(matrix_high, field_high)
            + dot_nn(matrix_high, field_low)
            + dot_nn(matrix_low, field_high)
        )
        field_ref[u] = result[:rows]
        chain = chain_ref[pl.ds(row, 1), :]
        over_rows, echo = chain[:, 32:33], chain[:, 33:34]
        end = over_rows * result[rows : rows + 1]
        edge_ref[0, pl.ds(row, 1), :] = end
        edge_ref[1, pl.ds(row, 1), :] = result[rows + 1 : rows + 2] + over_rows * echo * end


def pair_kernel(where_ref, own_ref, got_ref, chain_ref, send1_ref, send2_ref, send3_ref, *, pairs):
    lon = where_ref[2]
    second = jnp.bitwise_and(lon, 1) == 1
    pair = jnp.right_shift(lon, 1)
    chain = chain_ref[...]
    over, partner_over = chain[:, 32:33], chain[:, 34:35]
    end, returning = own_ref[0], own_ref[1]
    got_end, got_returning = got_ref[0], got_ref[1]
    pair_end = jnp.where(second, end + over * got_end, got_end + partner_over * end)
    pair_returning = jnp.where(
        second, got_returning + partner_over * returning, returning + over * got_returning
    )
    for shift, ref in ((1, send1_ref), (2, send2_ref), (3, send3_ref)):
        ref[...] = jnp.where(pair + shift < pairs, pair_end, pair_returning)


def enter_kernel(where_ref, own_ref, got_ref, got1_ref, got2_ref, got3_ref, chain_ref, left_ref, left_sum_ref,
                 enter_ref, leave_ref, table_ref):
    second = jnp.bitwise_and(where_ref[2], 1) == 1
    chain = chain_ref[...]
    over, echo = chain[:, 32:33], chain[:, 33:34]
    enter = jnp.where(second, got_ref[0], 0.0)
    leave = jnp.where(second, 0.0, got_ref[1])
    for shift, ref in ((1, got1_ref), (2, got2_ref), (3, got3_ref)):
        enter = enter + chain[:, shift : shift + 1] * ref[...]
        leave = leave + chain[:, 64 + shift : 65 + shift] * ref[...]
    enter_ref[...] = enter
    leave_ref[...] = over * (leave + echo * (own_ref[0] + over * enter))
    table_ref[...] = jnp.concatenate([left_ref[...], left_sum_ref[...]], axis=1)


def one_product(where_ref, refs, sizes, turn, step, u):
    field_ref, spread_ref, enter_ref, leave_ref, table_ref = refs
    chunk, in_chunk, steps, quarters = sizes
    cols = field_ref.shape[-1]
    row = lax.rem(where_ref[0] + turn, quarters) * steps + step
    place = chunk * in_chunk + row
    half = table_ref.shape[1] // 2
    wide = lambda lane: jnp.concatenate([lane_of(table_ref[...], lane)] * (cols // LANES), axis=1)
    enter, leave = enter_ref[pl.ds(row, 1), :], leave_ref[pl.ds(row, 1), :]
    filtered = field_ref[u] + wide(place + half) * enter + wide(place) * leave
    return spread_ref[0, u].astype(F32) * filtered.astype(BF16).astype(F32)


def send_kernel(sizes, items, added, where_ref, enter_ref, leave_ref, table_ref, *refs):
    steps = sizes[2]
    count = len(items)
    ins, adds, outs = refs[: 2 * count], refs[2 * count : -count], refs[-count:]
    for at, (turn, half) in enumerate(items):
        for u in range(PRODUCT_STEP):
            step = half * (steps // 2) + pl.program_id(0) * PRODUCT_STEP + u
            row_refs = (ins[2 * at], ins[2 * at + 1], enter_ref, leave_ref, table_ref)
            value = one_product(where_ref, row_refs, sizes, turn, step, u)
            if added:
                value = value + adds[at][u].astype(F32)
            outs[at][u] = value.astype(BF16)


def last_kernel(
    sizes, scale, where_ref, enter_ref, leave_ref, table_ref, field_ref, spread_ref,
    a0_ref, a1_ref, b0_ref, b1_ref, *rest
):
    steps = sizes[2]
    out_ref = rest[-1]
    in_first = pl.program_id(0) * PRODUCT_STEP < steps // 2
    for u in range(PRODUCT_STEP):
        step = pl.program_id(0) * PRODUCT_STEP + u
        row_refs = (field_ref, spread_ref, enter_ref, leave_ref, table_ref)
        value = one_product(where_ref, row_refs, sizes, 0, step, u)
        got_a = jnp.where(in_first, a0_ref[u].astype(F32), a1_ref[u].astype(F32))
        got_b = jnp.where(in_first, b0_ref[u].astype(F32), b1_ref[u].astype(F32))
        out_ref[u] = (value + got_a + got_b) * scale


def whole(shape):
    return pl.BlockSpec(shape, lambda *_: (0,) * len(shape))


def call(kernel, name, inputs, in_specs, outputs, out_specs, scratch=(), grid=(1,), aliases=None, cost=None):
    return pl.pallas_call(
        kernel,
        out_shape=outputs,
        grid_spec=pltpu.PrefetchScalarGridSpec(
            num_scalar_prefetch=1,
            grid=grid,
            in_specs=in_specs,
            out_specs=out_specs,
            scratch_shapes=list(scratch),
        ),
        input_output_aliases=aliases or {},
        compiler_params=pltpu.CompilerParams(vmem_limit_bytes=VMEM_LIMIT),
        cost_estimate=cost,
        name=name,
    )(*inputs)


def cost(flops, data):
    return pl.CostEstimate(flops=flops, bytes_accessed=data, transcendentals=0)


def triangle_table():
    at = np.arange(LANES)
    table = np.zeros((2 * LANES, 2 * LANES), np.float32)
    table[:LANES, :LANES] = at[:, None] <= at[None, :]
    table[LANES:, LANES:] = at[:, None] > at[None, :]
    return jnp.asarray(table, BF16)


def ring(axis, shift):
    count = lax.axis_size(axis)
    return [(i, (i + shift) % count) for i in range(count)]


def per_device(control, perturbation, slab_levels, member_group, band_width, zonal_rate, meridional_rate):
    _, levels, rows, cols = control.shape
    quarters, lat_count, lon_count = (lax.axis_size(a) for a in ("mem", "lat", "lon"))
    steps = levels // (CHUNKS * quarters)
    in_chunk = steps * quarters
    total_rows = zonal_rate.shape[1]
    here = jnp.stack([lax.axis_index(a) for a in ("mem", "lat", "lon")]).astype(jnp.int32)
    where = jnp.concatenate([here, member_group, band_width, slab_levels])
    sds = jax.ShapeDtypeStruct
    table = sds((rows, levels), F32)
    table_spec = pl.BlockSpec((ROW_GROUP, levels), lambda g, _: (g, 0))

    column, decay, gain, end, *sends = call(
        functools.partial(column_kernel, (levels, rows, cols, quarters, lat_count)),
        "vertical_columns",
        (where, control, zonal_rate),
        [
            pl.BlockSpec((1, levels, ROW_GROUP, cols), lambda g, _: (0, 0, g, 0)),
            whole(zonal_rate.shape),
        ],
        (sds((levels, rows, cols), BF16), table, table, table, table, table, table),
        (
            pl.BlockSpec((levels, ROW_GROUP, cols), lambda g, _: (0, g, 0)),
            whole((rows, levels)), whole((rows, levels)),
            table_spec, table_spec, table_spec, table_spec,
        ),
        scratch=[
            pltpu.VMEM((levels * 8, levels * 8), BF16),
            pltpu.VMEM((rows, levels), F32),
            pltpu.VMEM((2, levels, ROW_GROUP, LANES), F32),
        ],
        grid=(rows // ROW_GROUP,),
        cost=cost(2 * 512 * 512 * 384 * 12, 2 * levels * rows * cols * 2),
    )
    got = [lax.ppermute(s, "lat", ring("lat", i + 1)) for i, s in enumerate(sends)]
    left, left_sum, right, right_sum, chain = call(
        functools.partial(row_kernel, (levels, rows, quarters, lon_count)),
        "row_terms",
        (where, meridional_rate),
        [whole(meridional_rate.shape)],
        (table, table, sds((levels, rows), F32), sds((levels, rows), F32), sds((levels, LANES), F32)),
        (
            whole((rows, levels)), whole((rows, levels)),
            whole((levels, rows)), whole((levels, rows)), whole((levels, LANES)),
        ),
        cost=cost(2 * 3 * 64 * 768 * 768 * 2, 1 << 20),
    )

    triangle = triangle_table()
    scale = 1.0 / math.sqrt(control.shape[0] * quarters - 1)
    plane = rows * cols
    row_spec = pl.BlockSpec((in_chunk, cols), lambda *_: (0, 0))
    row_spec = whole((in_chunk, cols))
    edge_spec = whole((2, in_chunk, cols))
    table_wide = sds((rows, 2 * levels), F32)
    edge_row = sds((in_chunk, cols), F32)
    sizes_of = lambda c: (c, in_chunk, steps, quarters)
    half_steps = steps // 2
    half_piece = sds((half_steps, rows, cols), BF16)
    half_spec = pl.BlockSpec((PRODUCT_STEP, rows, cols), lambda g, _: (g, 0, 0))
    to_partner = [(i, i ^ 1) for i in range(lon_count)]
    to_pair = lambda s: [(i, (i + 2 * s) % lon_count) for i in range(lon_count)]
    per_half = half_steps // PRODUCT_STEP
    first_half = pl.BlockSpec((PRODUCT_STEP, rows, cols), lambda g, _: (jnp.minimum(g, per_half - 1), 0, 0))
    last_half = pl.BlockSpec((PRODUCT_STEP, rows, cols), lambda g, _: (jnp.maximum(g - per_half, 0), 0, 0))

    def quarter_specs(c, turn, half):
        at = lambda g, w, wide: (lax.rem(w[0] + turn, quarters) * wide + half) * per_half + g
        return [
            pl.BlockSpec((PRODUCT_STEP, rows, cols), lambda g, w: (at(g, w, 2), 0, 0)),
            pl.BlockSpec(
                (1, PRODUCT_STEP, rows, cols),
                lambda g, w: (0, at(g, w, 2 * CHUNKS) + c * 2 * per_half, 0, 0),
            ),
        ]

    def send(c, name, state, items, adds=()):
        field, enter, leave, lanes = state
        return call(
            functools.partial(send_kernel, sizes_of(c), items, bool(adds)),
            name,
            (where, enter, leave, lanes, *([field, perturbation] * len(items)), *adds),
            [row_spec, row_spec, whole(table_wide.shape)]
            + [spec for item in items for spec in quarter_specs(c, *item)]
            + [half_spec] * len(adds),
            (half_piece,) * len(items),
            (half_spec,) * len(items),
            grid=(per_half,),
            cost=cost(steps * plane * 8, steps * plane * 8),
        )

    up, down = ring("mem", 1), ring("mem", -1)
    states, fields = [], []
    for c in range(CHUNKS):
        by_place = lambda width: pl.BlockSpec((in_chunk, width), lambda g, _, c=c: (c, 0))
        field_steps = in_chunk // FIELD_STEP
        field, edge = call(
            functools.partial(field_kernel, (rows, cols, c, in_chunk, FIELD_STEP, lat_count)),
            "zonal_rows",
            (where, column, decay, gain, end, *got, left, left_sum, right, right_sum, chain, triangle),
            [pl.BlockSpec((FIELD_STEP, rows, cols), lambda g, _, c=c: (c * field_steps + g, 0, 0))]
            + [whole((rows, levels))] * 8
            + [by_place(rows), by_place(rows), by_place(LANES), whole(triangle.shape)],
            (sds((in_chunk, rows, cols), F32), sds((2, in_chunk, cols), F32)),
            (pl.BlockSpec((FIELD_STEP, rows, cols), lambda g, _: (g, 0, 0)), edge_spec),
            scratch=[pltpu.VMEM((3, rows, 2 * levels), F32)],
            grid=(field_steps,),
            cost=cost(in_chunk * plane * 2 * 1024, in_chunk * plane * 6),
        )
        fields.append(field)
        partner = lax.ppermute(edge, "lon", to_partner)
        pair_sends = call(
            functools.partial(pair_kernel, pairs=lon_count // 2),
            "pair_ends",
            (where, edge, partner, chain),
            [edge_spec, edge_spec, by_place(LANES)],
            (edge_row,) * 3,
            (row_spec,) * 3,
        )
        pair_got = [lax.ppermute(s, "lon", to_pair(i + 1)) for i, s in enumerate(pair_sends)]
        enter, leave, lanes = call(
            enter_kernel,
            "entering",
            (where, edge, partner, *pair_got, chain, left, left_sum),
            [edge_spec, edge_spec, row_spec, row_spec, row_spec, by_place(LANES)]
            + [whole((rows, levels))] * 2,
            (edge_row, edge_row, table_wide),
            (row_spec, row_spec, whole(table_wide.shape)),
        )
        states.append((field, enter, leave, lanes))
    result = None
    moved = []
    for c in range(CHUNKS):
        two_up, two_down = send(c, "products_two_away", states[c], ((2, 0), (2, 1)))
        two_up, two_down = lax.ppermute(two_up, "mem", up), lax.ppermute(two_down, "mem", down)
        one_up, one_down = send(c, "products_one_away", states[c], ((1, 1), (3, 0)))
        one_up, one_down = lax.ppermute(one_up, "mem", up), lax.ppermute(one_down, "mem", down)
        sum_up, sum_down = send(c, "products_added", states[c], ((1, 0), (3, 1)), (two_up, two_down))
        sum_up, sum_down = lax.ppermute(sum_up, "mem", up), lax.ppermute(sum_down, "mem", down)
        moved.append((sum_up, one_up, one_down, sum_down))
    for c in range(CHUNKS):
        field, enter, leave, lanes = states[c]
        extra = () if result is None else (result,)
        full_specs = quarter_specs(c, 0, 0)
        result = call(
            functools.partial(last_kernel, sizes_of(c), scale),
            "products_here",
            (where, enter, leave, lanes, field, perturbation, *moved[c], *extra),
            [row_spec, row_spec, whole(table_wide.shape), *full_specs]
            + [first_half, last_half, first_half, last_half]
            + [pl.BlockSpec(memory_space=pl.ANY)] * len(extra),
            sds((levels // quarters, rows, cols), F32),
            pl.BlockSpec((PRODUCT_STEP, rows, cols), lambda g, _, c=c: (c * 2 * per_half + g, 0, 0)),
            grid=(2 * per_half,),
            aliases={10: 0} if extra else None,
            cost=cost(steps * plane * 8, steps * plane * 14),
        )
    return result


def solution(mesh):
    return jax.shard_map(
        per_device,
        mesh=mesh,
        in_specs=(
            P("mem", None, "lon", "lat"),
            P("mem", None, "lon", "lat"),
            P(),
            P("mem"),
            P(),
            P(),
            P(),
        ),
        out_specs=P("mem", "lon", "lat"),
        check_vma=False,
    )
```

```python
import functools
import math

import jax
import jax.numpy as jnp
import numpy as np
from jax import lax
from jax.experimental import pallas as pl
from jax.experimental.pallas import tpu as pltpu
from jax.sharding import PartitionSpec as P

CHUNKS = ((8, 8),)
LANES = 128
GROUP_AT = 3
BAND_AT = 4
SLAB_AT = 8
ROW_GROUP = 16
FIELD_STEP = 8
PRODUCT_STEP = 4
VMEM_LIMIT = 8 * 1024 * 1024
COLUMN_VMEM_LIMIT = 14 * 1024 * 1024
FIELD_VMEM_LIMIT = 16 * 1024 * 1024

F32 = jnp.float32
BF16 = jnp.bfloat16


def iota(shape, axis):
    return lax.broadcasted_iota(jnp.int32, shape, axis)


def log_decay(rate):
    t = rate / (2.0 - rate)
    s = t * t
    series = 1.0 + s * (1 / 3 + s * (1 / 5 + s * (1 / 7 + s * (1 / 9 + s * (1 / 11 + s / 13)))))
    return -2.0 * t * series


def split3(x):
    hi = x.astype(BF16)
    rest = x - hi.astype(F32)
    mid = rest.astype(BF16)
    return hi, mid, (rest - mid.astype(F32)).astype(BF16)


def split2(x):
    hi = x.astype(BF16)
    return hi, (x - hi.astype(F32)).astype(BF16)


def dot_nn(a, b):
    return lax.dot_general(a, b, (((1,), (0,)), ((), ())), preferred_element_type=F32)


def dot_nt(a, b):
    return lax.dot_general(a, b, (((1,), (1,)), ((), ())), preferred_element_type=F32)


def times_exact(x, zero_one):
    rows = x.shape[0]
    product = dot_nn(jnp.concatenate(split3(x), axis=0), zero_one)
    return product[:rows] + product[rows : 2 * rows] + product[2 * rows :]


def exact_times_t(zero_one, x):
    return sum(dot_nt(zero_one, part) for part in split3(x))


def traced_level(place, levels, quarters):
    level = jnp.zeros_like(place)
    first, begin = 0, 0
    for parts in CHUNKS:
        steps = sum(parts)
        rest = place - first
        quarter = sum((rest >= k * steps).astype(jnp.int32) for k in range(1, quarters))
        here = quarter * (levels // quarters - steps) + rest + begin
        level = jnp.where(rest >= 0, here, level)
        first, begin = first + steps * quarters, begin + steps
    return level


def rates_by_place(slab_levels, rates, levels, quarters):
    slabs = rates.shape[0]
    level = traced_level(iota((levels, slabs), 0), levels, quarters)
    index = jnp.zeros((levels, slabs), jnp.int32)
    end = jnp.int32(0)
    for s in range(slabs):
        end = end + slab_levels[SLAB_AT + s]
        index = index + (level >= end).astype(jnp.int32)
    chosen = (index == iota((levels, slabs), 1)).astype(F32).astype(BF16)
    return sum(dot_nn(chosen, part) for part in split3(rates))


def lane_of(table, lane):
    return jnp.take_along_axis(table, jnp.full(table.shape, lane, jnp.int32), axis=1)


def column_kernel(
    sizes, where_ref, control_ref, rate_ref,
    column_ref, decay_ref, gain_ref, end_ref, send1_ref, send2_ref, send3_ref,
    kron, decay_all, weighted,
):
    levels, rows, cols, quarters, lat_count = sizes
    step = pl.program_id(0)
    lat, lon = where_ref[1], where_ref[2]
    full = levels * 8

    @pl.when(step == 0)
    def _():
        band = where_ref[BAND_AT + where_ref[GROUP_AT]].astype(F32)
        out_level = traced_level(jnp.right_shift(iota((full, full), 0), 3), levels, quarters)
        spacing = out_level - jnp.right_shift(iota((full, full), 1), 3)
        same = jnp.bitwise_and(iota((full, full), 0), 7) == jnp.bitwise_and(iota((full, full), 1), 7)
        ratio = spacing.astype(F32) / band
        weight = jnp.exp(-2.0 * (ratio * ratio))
        keep = jnp.logical_and(same, jnp.abs(spacing).astype(F32) <= band)
        kron[...] = jnp.where(keep, weight, 0.0).astype(BF16)
        level_rates = rates_by_place(where_ref, rate_ref[...], levels, quarters)
        own = iota((rows, rate_ref.shape[1]), 1) == lon * rows + iota((rows, rate_ref.shape[1]), 0)
        rate = exact_times_t(own.astype(F32).astype(BF16), level_rates)
        remain = 1.0 - rate
        decay_all[...] = log_decay(rate)
        decay_ref[...] = decay_all[...]
        gain_ref[...] = jnp.sqrt(rate * (2.0 - rate) / (1.0 + remain * remain))

    block = control_ref[0].astype(F32)
    halves = []
    for half in range(2):
        part = block[:, 8 * half : 8 * half + 8, :].reshape(full, cols).astype(BF16)
        halves.append(dot_nn(kron[...], part).reshape(levels, 8, cols))
    column = jnp.concatenate(halves, axis=1).astype(BF16)
    column_ref[...] = column

    log_a = decay_all[pl.ds(step * ROW_GROUP, ROW_GROUP), :]
    lane = iota((ROW_GROUP, LANES), 1).astype(F32)
    blocks = cols // LANES
    for place in range(levels):
        log_b = jnp.broadcast_to(log_a[:, place : place + 1], (ROW_GROUP, LANES))
        over = jnp.exp(log_b * float(LANES))
        x = column_ref[place].astype(F32)
        parts = [x[:, LANES * b : LANES * (b + 1)] for b in range(blocks)]
        along, against = parts[0], parts[-1]
        for b in range(1, blocks):
            along = parts[b] + over * along
            against = parts[-1 - b] + over * against
        weighted[0, place] = along * jnp.exp(log_b * (LANES - 1.0 - lane))
        weighted[1, place] = against * jnp.exp(log_b * lane)
    place_lane = iota((ROW_GROUP, levels), 1)
    forward = jnp.zeros((ROW_GROUP, levels), F32)
    backward = jnp.zeros((ROW_GROUP, levels), F32)
    for place in range(levels):
        along = jnp.sum(weighted[0, place], axis=1, keepdims=True)
        against = jnp.sum(weighted[1, place], axis=1, keepdims=True)
        forward = jnp.where(place_lane == place, along, forward)
        backward = jnp.where(place_lane == place, against, backward)
    power = (1 + cols * (2 * (lat_count - 1 - lat) + 1)).astype(F32)
    returning = backward - jnp.exp(log_a * power) * forward
    end_ref[...] = forward
    for shift, ref in ((1, send1_ref), (2, send2_ref), (3, send3_ref)):
        ref[...] = jnp.where(lat + shift < lat_count, forward, returning)


def row_kernel(
    sizes, where_ref, rate_ref,
    left_ref, left_sum_ref, right_ref, right_sum_ref, chain_ref,
):
    levels, rows, quarters, lon_count = sizes
    lon = where_ref[2]
    total = rate_ref.shape[1]
    rate = rates_by_place(where_ref, rate_ref[...], levels, quarters)
    remain = 1.0 - rate
    root = jnp.sqrt(rate * (2.0 - rate))
    gain = root * jnp.sqrt(root) / jnp.sqrt(jnp.sqrt(1.0 + remain * remain))
    log_c = log_decay(rate)
    owner = lambda at: jnp.right_shift(at * ((1 << 16) // rows + 1), 16)
    first, second = iota((total, total), 0), iota((total, total), 1)
    same = owner(first) == owner(second)
    upper = jnp.logical_and(same, first <= second).astype(F32).astype(BF16)
    lower = jnp.logical_and(same, first >= second).astype(F32).astype(BF16)
    running = times_exact(log_c, upper)
    before = running - log_c
    weight = gain * jnp.exp(running + before)
    sums = times_exact(weight, lower)
    left = jnp.exp(-before)
    right = gain * jnp.exp(-running)
    own = (iota((rows, total), 1) == lon * rows + iota((rows, total), 0)).astype(F32).astype(BF16)
    own_t = iota((total, LANES), 0) == lon * rows + iota((total, LANES), 1)
    own_t = jnp.logical_and(own_t, iota((total, LANES), 1) < rows).astype(F32).astype(BF16)
    left_ref[...] = exact_times_t(own, left)
    left_sum_ref[...] = exact_times_t(own, left * sums)
    right_ref[...] = times_exact(right, own_t)
    right_sum_ref[...] = times_exact(right * sums, own_t)

    inside = (owner(iota((total, LANES), 0)) == iota((total, LANES), 1)).astype(F32).astype(BF16)
    log_over = times_exact(log_c, inside)
    bounce = times_exact(weight, inside)
    source, target = iota((LANES, LANES), 0), iota((LANES, LANES), 1)
    between = jnp.logical_and(source > lon, source < target).astype(F32).astype(BF16)
    device = iota((levels, LANES), 1)
    beyond = jnp.logical_and(device > lon, device < lon_count)
    echo = jnp.sum(
        jnp.where(beyond, bounce * jnp.exp(2.0 * times_exact(log_over, between)), 0.0),
        axis=1,
        keepdims=True,
    )
    every = jnp.exp(log_over)
    over = jnp.sum(jnp.where(device == lon, every, 0.0), axis=1, keepdims=True)
    partner = jnp.bitwise_xor(lon, 1)
    partner_over = jnp.sum(jnp.where(device == partner, every, 0.0), axis=1, keepdims=True)
    pair, pairs = jnp.right_shift(lon, 1), lon_count // 2
    shift = jnp.bitwise_and(target, 63)
    is_before = pair >= shift
    low = jnp.where(is_before, 2 * (pair - shift) + 1, lon)
    high = jnp.where(is_before, lon, 2 * (pair - shift + pairs))
    path = jnp.logical_and(source > low, source < high).astype(F32).astype(BF16)
    reach = jnp.exp(times_exact(log_over, path))
    shift = jnp.bitwise_and(device, 63)
    counted = jnp.logical_and(shift >= 1, shift < pairs)
    counted = jnp.logical_and(counted, (pair >= shift) == (device < 64))
    chain = jnp.where(counted, reach, 0.0)
    for at, value in ((32, over), (33, echo), (34, partner_over)):
        chain = jnp.where(device == at, value, chain)
    chain_ref[...] = chain


def field_kernel(
    sizes, where_ref, column_ref, decay_ref, gain_ref, end_ref, got1_ref, got2_ref, got3_ref,
    right_ref, right_sum_ref, chain_ref, triangle_ref,
    fields, edge_ref, tables, powers, enters, scaled, sums,
):
    rows, cols, first_place, per_step, lat_count = sizes
    step = pl.program_id(0)
    lat = where_ref[1]
    blocks = cols // LANES

    @pl.when(step == 0)
    def _():
        log_a, gain = decay_ref[...], gain_ref[...]
        enter_left = jnp.zeros(log_a.shape, F32)
        enter_right = jnp.zeros(log_a.shape, F32)
        for shift, ref in ((1, got1_ref), (2, got2_ref), (3, got3_ref)):
            got = ref[...]
            is_left = lat >= shift
            power = jnp.where(is_left, shift - 1, lat_count - 1 - shift) * cols
            scaled = jnp.exp(log_a * power.astype(F32)) * got
            enter_left = enter_left + jnp.where(is_left, scaled, 0.0)
            enter_right = enter_right + jnp.where(is_left, 0.0, scaled)
        leaving = end_ref[...] + jnp.exp(log_a * float(cols)) * enter_left
        power = (1 + 2 * cols * (lat_count - 1 - lat)).astype(F32)
        enter_right = enter_right - jnp.exp(log_a * power) * leaving
        enter_left = gain * jnp.exp(log_a) * enter_left
        enter_right = gain * jnp.exp(log_a * float(LANES)) * enter_right
        tables[0] = jnp.concatenate([log_a, gain], axis=1)
        tables[1] = jnp.concatenate([enter_left, enter_right], axis=1)

    half = tables.shape[2] // 2
    lane = iota((rows, LANES), 1).astype(F32)
    row_number = iota((16, LANES), 0)
    tall = blocks * rows
    place_of = lambda u: first_place + step * per_step + u
    for u in range(per_step):
        log_a = lane_of(tables[0], place_of(u))
        gain = lane_of(tables[0], place_of(u) + half)
        enters[u, 0] = lane_of(tables[1], place_of(u))
        enters[u, 1] = lane_of(tables[1], place_of(u) + half)
        grow = jnp.exp(log_a * lane)
        shrink = jnp.exp(log_a * (-lane))
        powers[u, 0] = grow
        powers[u, 1] = shrink
        powers[u, 2] = jnp.exp(log_a * float(LANES))
        powers[u, 3] = jnp.exp(log_a)
        gain_grow, gain_shrink = gain * grow, gain * shrink
        x = column_ref[u].astype(F32)
        for b in range(blocks):
            part = x[:, LANES * b : LANES * (b + 1)]
            rows_at = slice(u * tall + b * rows, u * tall + (b + 1) * rows)
            for side, factor in enumerate((gain_shrink, gain_grow)):
                high, low = split2(part * factor)
                at = LANES * side
                scaled[rows_at, at : at + LANES] = high
                scaled[rows_at, 2 * LANES + at : 3 * LANES + at] = low
    for u in range(per_step):
        at = slice(u * tall, (u + 1) * tall)
        sums[at, :] = dot_nn(scaled[at, :], triangle_ref[...])
    for u in range(per_step):
        grow, shrink, over, decay = (powers[u, k] for k in range(4))
        at = lambda b: slice(u * tall + b * rows, u * tall + (b + 1) * rows)
        ahead = [grow * sums[at(b), :LANES] for b in range(blocks)]
        behind = [sums[at(b), LANES:] for b in range(blocks)]
        lefts, rights_in = [enters[u, 0]], [enters[u, 1]]
        for b in range(blocks - 1):
            end = jnp.broadcast_to(ahead[b][:, LANES - 1 :], (rows, LANES))
            lefts.append(over * lefts[-1] + decay * end)
        for b in range(blocks - 1, 0, -1):
            first = (
                scaled[at(b), LANES : 2 * LANES].astype(F32)
                + scaled[at(b), 3 * LANES :].astype(F32)
                + behind[b]
            )
            end = jnp.broadcast_to(first[:, :1], (rows, LANES))
            rights_in.append(over * (rights_in[-1] + end))
        rights_in = rights_in[::-1]
        for b in range(blocks):
            field = ahead[b] + grow * lefts[b] + shrink * (behind[b] + rights_in[b])
            high, low = split2(field)
            fields[u, :rows, LANES * b : LANES * (b + 1)] = high
            fields[u, LANES : LANES + rows, LANES * b : LANES * (b + 1)] = low
        nothing = jnp.zeros((LANES - rows, cols), BF16)
        fields[u, rows:LANES, :] = nothing
        fields[u, LANES + rows :, :] = nothing
    for u in range(per_step):
        ends = [split2(ref[u : u + 1, :]) for ref in (right_ref, right_sum_ref)]
        first = jnp.zeros((16, LANES), F32)
        for at, part in enumerate((ends[0][0], ends[1][0], ends[0][1], ends[1][1])):
            first = jnp.where(row_number == at, part.astype(F32), first)
        second = jnp.where(row_number < 2, first, 0.0)
        result = dot_nn(jnp.concatenate([first, second], axis=1).astype(BF16), fields[u])
        row = step * per_step + u
        chain_row = chain_ref[u : u + 1, :]
        over_rows, echo = chain_row[:, 32:33], chain_row[:, 33:34]
        end = over_rows * (result[0:1] + result[2:3])
        edge_ref[0, pl.ds(row, 1), :] = end
        edge_ref[1, pl.ds(row, 1), :] = result[1:2] + result[3:4] + over_rows * echo * end


def row_kernel_of(rows, first_place):
    def kernel(where_ref, fields_ref, left_ref, left_sum_ref, right_ref, right_sum_ref, *rest):
        field_ref, table, matrices = rest[-3:]
        step, per_step = pl.program_id(0), fields_ref.shape[0]
        half = table.shape[1] // 2
        below = iota((rows, LANES), 0) >= iota((rows, LANES), 1)

        @pl.when(step == 0)
        def _():
            table[...] = jnp.concatenate([left_ref[...], left_sum_ref[...]], axis=1)
            matrices[...] = jnp.zeros_like(matrices)

        for u in range(per_step):
            place = first_place + step * per_step + u
            left, left_sum = lane_of(table[...], place), lane_of(table[...], place + half)
            right, right_sum = right_ref[u : u + 1, :], right_sum_ref[u : u + 1, :]
            high, low = split2(jnp.where(below, left_sum * right, left * right_sum))
            matrices[u, :rows, :LANES] = high
            matrices[u, :rows, LANES:] = high
            matrices[u, rows:, :LANES] = low
        for u in range(per_step):
            result = dot_nn(matrices[u], fields_ref[u])
            field_ref[u] = result[:rows] + result[rows:]

    return kernel


def pair_kernel(where_ref, own_ref, got_ref, chain_ref, send1_ref, send2_ref, send3_ref, *, pairs, places):
    lon = where_ref[2]
    second = jnp.bitwise_and(lon, 1) == 1
    pair = jnp.right_shift(lon, 1)
    chain = chain_ref[places, :]
    over, partner_over = chain[:, 32:33], chain[:, 34:35]
    end, returning = own_ref[0], own_ref[1]
    got_end, got_returning = got_ref[0], got_ref[1]
    pair_end = jnp.where(second, end + over * got_end, got_end + partner_over * end)
    pair_returning = jnp.where(
        second, got_returning + partner_over * returning, returning + over * got_returning
    )
    for shift, ref in ((1, send1_ref), (2, send2_ref), (3, send3_ref)):
        ref[...] = jnp.where(pair + shift < pairs, pair_end, pair_returning)


def enter_kernel(where_ref, own_ref, got_ref, got1_ref, got2_ref, got3_ref, chain_ref, left_ref, left_sum_ref,
                 enter_ref, leave_ref, table_ref, *, places):
    second = jnp.bitwise_and(where_ref[2], 1) == 1
    chain = chain_ref[places, :]
    over, echo = chain[:, 32:33], chain[:, 33:34]
    enter = jnp.where(second, got_ref[0], 0.0)
    leave = jnp.where(second, 0.0, got_ref[1])
    for shift, ref in ((1, got1_ref), (2, got2_ref), (3, got3_ref)):
        enter = enter + chain[:, shift : shift + 1] * ref[...]
        leave = leave + chain[:, 64 + shift : 65 + shift] * ref[...]
    enter_ref[...] = enter
    leave_ref[...] = over * (leave + echo * (own_ref[0] + over * enter))
    table_ref[...] = jnp.concatenate([left_ref[...], left_sum_ref[...]], axis=1)


def one_product(where_ref, refs, sizes, turn, step, u):
    field_ref, spread_ref, enter_ref, leave_ref, table_ref = refs
    first_place, steps, quarters = sizes
    cols = field_ref.shape[-1]
    row = lax.rem(where_ref[0] + turn, quarters) * steps + step
    place = first_place + row
    half = table_ref.shape[1] // 2
    wide = lambda lane: jnp.concatenate([lane_of(table_ref[...], lane)] * (cols // LANES), axis=1)
    enter, leave = enter_ref[pl.ds(row, 1), :], leave_ref[pl.ds(row, 1), :]
    filtered = field_ref[u] + wide(place + half) * enter + wide(place) * leave
    return spread_ref[0, u].astype(F32) * filtered.astype(BF16).astype(F32)


def send_kernel(sizes, turn, start, where_ref, enter_ref, leave_ref, table_ref, field_ref, spread_ref, *refs):
    *adds, out_ref = refs
    row_refs = (field_ref, spread_ref, enter_ref, leave_ref, table_ref)
    for u in range(PRODUCT_STEP):
        step = start + pl.program_id(0) * PRODUCT_STEP + u
        value = one_product(where_ref, row_refs, sizes, turn, step, u)
        for ref in adds:
            value = value + ref[u].astype(F32)
        out_ref[u] = value.astype(BF16)


def here_kernel(sizes, first_part, where_ref, enter_ref, leave_ref, table_ref, field_ref, spread_ref, got0_ref, got1_ref, out_ref):
    in_first = pl.program_id(0) * PRODUCT_STEP < first_part
    row_refs = (field_ref, spread_ref, enter_ref, leave_ref, table_ref)
    for u in range(PRODUCT_STEP):
        step = pl.program_id(0) * PRODUCT_STEP + u
        value = one_product(where_ref, row_refs, sizes, 0, step, u)
        out_ref[u] = value + jnp.where(in_first, got0_ref[u], got1_ref[u]).astype(F32)


def last_kernel(scale, first_part, where_ref, sum_ref, got0_ref, got1_ref, out_ref):
    in_first = pl.program_id(0) * PRODUCT_STEP < first_part
    out_ref[...] = (sum_ref[...] + jnp.where(in_first, got0_ref[...], got1_ref[...]).astype(F32)) * scale


def whole(shape):
    return pl.BlockSpec(shape, lambda *_: (0,) * len(shape))


def call(
    kernel, name, inputs, in_specs, outputs, out_specs, scratch=(), grid=(1,), cost=None, after=(), vmem=VMEM_LIMIT, aliases=None
):
    count = len(inputs)

    def ordered(*refs):
        return kernel(*refs[:count], *refs[count + len(after) :])

    inputs = (*inputs, *after)
    in_specs = [*in_specs, *([pl.BlockSpec(memory_space=pl.ANY)] * len(after))]
    return pl.pallas_call(
        ordered,
        out_shape=outputs,
        grid_spec=pltpu.PrefetchScalarGridSpec(
            num_scalar_prefetch=1,
            grid=grid,
            in_specs=in_specs,
            out_specs=out_specs,
            scratch_shapes=list(scratch),
        ),
        input_output_aliases=aliases or {},
        compiler_params=pltpu.CompilerParams(vmem_limit_bytes=vmem),
        cost_estimate=cost,
        name=name,
    )(*inputs)


def cost(flops, data):
    return pl.CostEstimate(flops=flops, bytes_accessed=data, transcendentals=0)


def triangle_table():
    at = np.arange(LANES)
    table = np.zeros((2 * LANES, 2 * LANES), np.float32)
    table[:LANES, :LANES] = at[:, None] <= at[None, :]
    table[LANES:, LANES:] = at[:, None] > at[None, :]
    return jnp.asarray(np.concatenate([table, table]), BF16)


def ring(axis, shift):
    count = lax.axis_size(axis)
    return [(i, (i + shift) % count) for i in range(count)]


def per_device(control, perturbation, slab_levels, member_group, band_width, zonal_rate, meridional_rate):
    _, levels, rows, cols = control.shape
    quarters, lat_count, lon_count = (lax.axis_size(a) for a in ("mem", "lat", "lon"))
    per_quarter = levels // quarters
    here = jnp.stack([lax.axis_index(a) for a in ("mem", "lat", "lon")]).astype(jnp.int32)
    where = jnp.concatenate([here, member_group, band_width, slab_levels])
    sds = jax.ShapeDtypeStruct
    table = sds((rows, levels), F32)
    table_spec = pl.BlockSpec((ROW_GROUP, levels), lambda g, _: (g, 0))

    column, decay, gain, end, *sends = call(
        functools.partial(column_kernel, (levels, rows, cols, quarters, lat_count)),
        "vertical_columns",
        (where, control, zonal_rate),
        [
            pl.BlockSpec((1, levels, ROW_GROUP, cols), lambda g, _: (0, 0, g, 0)),
            whole(zonal_rate.shape),
        ],
        (sds((levels, rows, cols), BF16), table, table, table, table, table, table),
        (
            pl.BlockSpec((levels, ROW_GROUP, cols), lambda g, _: (0, g, 0)),
            whole((rows, levels)), whole((rows, levels)),
            table_spec, table_spec, table_spec, table_spec,
        ),
        scratch=[
            pltpu.VMEM((levels * 8, levels * 8), BF16),
            pltpu.VMEM((rows, levels), F32),
            pltpu.VMEM((2, levels, ROW_GROUP, LANES), F32),
        ],
        grid=(rows // ROW_GROUP,),
        cost=cost(2 * 512 * 512 * 384 * 12, 2 * levels * rows * cols * 2),
        vmem=COLUMN_VMEM_LIMIT,
    )
    got = [lax.ppermute(s, "lat", ring("lat", i + 1)) for i, s in enumerate(sends)]
    left, left_sum, right, right_sum, chain = call(
        functools.partial(row_kernel, (levels, rows, quarters, lon_count)),
        "row_terms",
        (where, meridional_rate),
        [whole(meridional_rate.shape)],
        (table, table, sds((levels, LANES), F32), sds((levels, LANES), F32), sds((levels, LANES), F32)),
        (
            whole((rows, levels)), whole((rows, levels)),
            whole((levels, LANES)), whole((levels, LANES)), whole((levels, LANES)),
        ),
        cost=cost(2 * 3 * 64 * 768 * 768 * 2, 1 << 20),
    )

    triangle = triangle_table()
    scale = 1.0 / math.sqrt(control.shape[0] * quarters - 1)
    plane = rows * cols
    table_wide = sds((rows, 2 * levels), F32)
    table_specs = [whole((rows, levels))] * 2
    to_partner = [(i, i ^ 1) for i in range(lon_count)]
    to_pair = lambda k: [(i, (i + 2 * k) % lon_count) for i in range(lon_count)]
    up, down = ring("mem", 1), ring("mem", -1)
    by_step = lambda offset, low=0, high=levels: pl.BlockSpec(
        (PRODUCT_STEP, rows, cols), lambda g, _: (jnp.clip(g - offset, low, high), 0, 0)
    )
    ends = np.cumsum([sum(parts) for parts in CHUNKS])

    def quarter_specs(c, turn, start):
        steps, begin = sum(CHUNKS[c]), int(ends[c]) - sum(CHUNKS[c])
        at = lambda g, w, wide, off: (
            lax.rem(w[0] + turn, quarters) * (wide // PRODUCT_STEP) + (off + start) // PRODUCT_STEP + g
        )
        return [
            pl.BlockSpec((PRODUCT_STEP, rows, cols), lambda g, w: (at(g, w, steps, 0), 0, 0)),
            pl.BlockSpec(
                (1, PRODUCT_STEP, rows, cols), lambda g, w: (0, at(g, w, per_quarter, begin), 0, 0)
            ),
        ]

    def edge_specs(steps):
        row = whole((steps * quarters, cols))
        return [row, row, whole(table_wide.shape)]

    def product_sizes(c):
        steps = sum(CHUNKS[c])
        return (int(ends[c]) - steps) * quarters, steps, quarters

    def send(c, turn, part, adds=(), after=()):
        field, enter, leave, lanes = states[c]
        start, count = part * CHUNKS[c][0], CHUNKS[c][part]
        (piece,) = call(
            functools.partial(send_kernel, product_sizes(c), turn, start),
            f"products_{turn}",
            (where, enter, leave, lanes, field, perturbation, *adds),
            edge_specs(sum(CHUNKS[c])) + quarter_specs(c, turn, start) + [by_step(0)] * len(adds),
            (sds((count, rows, cols), BF16),),
            (by_step(0),),
            grid=(count // PRODUCT_STEP,),
            cost=cost(count * plane * 8, count * plane * 8),
            after=after,
        )
        return piece

    def finish(c, two, one, after=()):
        sum_up = send(c, 1, 0, (two[0],), after)
        moved_up = lax.ppermute(sum_up, "mem", up)
        sum_down = send(c, 3, 1, (two[1],), (sum_up, *after))
        moved_down = lax.ppermute(sum_down, "mem", down)
        steps, first = sum(CHUNKS[c]), CHUNKS[c][0] // PRODUCT_STEP
        halves = [by_step(0, 0, first - 1), by_step(first, 0)]
        field, enter, leave, lanes = states[c]
        own = sds((steps, rows, cols), F32)
        here = call(
            functools.partial(here_kernel, product_sizes(c), CHUNKS[c][0]),
            "products_here",
            (where, enter, leave, lanes, field, perturbation, one[1], one[0]),
            edge_specs(steps) + quarter_specs(c, 0, 0) + halves,
            own,
            by_step(0),
            grid=(steps // PRODUCT_STEP,),
            cost=cost(steps * plane * 8, steps * plane * 14),
            after=(sum_down,),
        )
        return call(
            functools.partial(last_kernel, scale, CHUNKS[c][0]),
            "increment",
            (where, here, moved_up, moved_down),
            [by_step(0), *halves],
            own,
            by_step(0),
            grid=(steps // PRODUCT_STEP,),
            cost=cost(steps * plane * 2, steps * plane * 10),
        )

    states, increments = [], []
    for c, parts in enumerate(CHUNKS):
        steps = sum(parts)
        in_chunk, first_place = steps * quarters, (int(ends[c]) - steps) * quarters
        places = slice(first_place, first_place + in_chunk)
        edge_spec, row_spec = whole((2, in_chunk, cols)), whole((in_chunk, cols))
        edge_row = sds((in_chunk, cols), F32)
        block = first_place // FIELD_STEP
        by_place = pl.BlockSpec((FIELD_STEP, LANES), lambda g, _, block=block: (block + g, 0))
        fields, edge = call(
            functools.partial(field_kernel, (rows, cols, first_place, FIELD_STEP, lat_count)),
            "zonal_rows",
            (where, column, decay, gain, end, *got, right, right_sum, chain, triangle),
            [pl.BlockSpec((FIELD_STEP, rows, cols), lambda g, _, block=block: (block + g, 0, 0))]
            + [whole((rows, levels))] * 6
            + [by_place, by_place, by_place, whole(triangle.shape)],
            (sds((in_chunk, 2 * LANES, cols), BF16), sds((2, in_chunk, cols), F32)),
            (pl.BlockSpec((FIELD_STEP, 2 * LANES, cols), lambda g, _: (g, 0, 0)), edge_spec),
            scratch=[
                pltpu.VMEM((2, rows, 2 * levels), F32),
                pltpu.VMEM((FIELD_STEP, 4, rows, LANES), F32),
                pltpu.VMEM((FIELD_STEP, 2, rows, LANES), F32),
                pltpu.VMEM((FIELD_STEP * rows * cols // LANES, 4 * LANES), BF16),
                pltpu.VMEM((FIELD_STEP * rows * cols // LANES, 2 * LANES), F32),
            ],
            grid=(in_chunk // FIELD_STEP,),
            cost=cost(in_chunk * plane * 2 * 1024 * 3, in_chunk * plane * 6),
            vmem=FIELD_VMEM_LIMIT,
        )
        def filter_rows(part, before, after=()):
            half_steps = in_chunk // FIELD_STEP // 2
            here = block + part * half_steps
            level_rows = pl.BlockSpec((FIELD_STEP, LANES), lambda g, _: (here + g, 0))
            step_of = lambda height: pl.BlockSpec(
                (FIELD_STEP, height, cols), lambda g, _: (part * half_steps + g, 0, 0)
            )
            extra = () if before is None else (before,)
            return call(
                row_kernel_of(rows, first_place + part * half_steps * FIELD_STEP),
                "row_filter",
                (where, fields, left, left_sum, right, right_sum, *extra),
                [step_of(2 * LANES), *table_specs, level_rows, level_rows]
                + [pl.BlockSpec(memory_space=pl.ANY)] * len(extra),
                sds((in_chunk, rows, cols), F32),
                step_of(rows),
                scratch=[
                    pltpu.VMEM((rows, 2 * levels), F32),
                    pltpu.VMEM((FIELD_STEP, 2 * rows, 2 * LANES), BF16),
                ],
                grid=(half_steps,),
                cost=cost(in_chunk * plane * 512, in_chunk * plane * 4),
                after=after,
                aliases={6: 0} if extra else None,
            )

        partner = lax.ppermute(edge, "lon", to_partner)
        field = filter_rows(0, None)
        pair_sends = call(
            functools.partial(pair_kernel, pairs=lon_count // 2, places=places),
            "pair_ends",
            (where, edge, partner, chain),
            [edge_spec, edge_spec, whole((levels, LANES))],
            (edge_row,) * 3,
            (row_spec,) * 3,
            after=(field,),
        )
        field = filter_rows(1, field, after=(pair_sends[0],))
        pair_got = [lax.ppermute(p, "lon", to_pair(k + 1)) for k, p in enumerate(pair_sends)]
        enter, leave, lanes = call(
            functools.partial(enter_kernel, places=places),
            "entering",
            (where, edge, partner, *pair_got, chain, left, left_sum),
            [edge_spec, edge_spec, row_spec, row_spec, row_spec, whole((levels, LANES)), *table_specs],
            (edge_row, edge_row, table_wide),
            (row_spec, row_spec, whole(table_wide.shape)),
        )
        states.append((field, enter, leave, lanes))
        two_up = send(c, 2, 0)
        two_up_moved = lax.ppermute(two_up, "mem", up)
        two_down = send(c, 2, 1, after=(two_up,))
        two = two_up_moved, lax.ppermute(two_down, "mem", down)
        one_up = send(c, 1, 1, after=(two_down,))
        one_up_moved = lax.ppermute(one_up, "mem", up)
        one_down = send(c, 3, 0, after=(one_up,))
        one = one_up_moved, lax.ppermute(one_down, "mem", down)
        increments.append(finish(c, two, one))
    return increments[0] if len(increments) == 1 else jnp.concatenate(increments)


def solution(mesh):
    return jax.shard_map(
        per_device,
        mesh=mesh,
        in_specs=(
            P("mem", None, "lon", "lat"),
            P("mem", None, "lon", "lat"),
            P(),
            P("mem"),
            P(),
            P(),
            P(),
        ),
        out_specs=P("mem", "lon", "lat"),
        check_vma=False,
    )
```

```python
import functools
import math

import jax
import jax.numpy as jnp
import numpy as np
from jax import lax
from jax.experimental import pallas as pl
from jax.experimental.pallas import tpu as pltpu
from jax.sharding import PartitionSpec as P

CHUNKS = ((8, 8),)
LANES = 128
GROUP_AT = 3
BAND_AT = 4
SLAB_AT = 8
ROW_GROUP = 32
FIELD_STEP = 8
PRODUCT_STEP = 4
VMEM_LIMIT = 8 * 1024 * 1024
COLUMN_VMEM_LIMIT = 48 * 1024 * 1024
FIELD_VMEM_LIMIT = 16 * 1024 * 1024

F32 = jnp.float32
BF16 = jnp.bfloat16


def iota(shape, axis):
    return lax.broadcasted_iota(jnp.int32, shape, axis)


def log_decay(rate):
    t = rate / (2.0 - rate)
    s = t * t
    series = 1.0 + s * (1 / 3 + s * (1 / 5 + s * (1 / 7 + s * (1 / 9 + s * (1 / 11 + s / 13)))))
    return -2.0 * t * series


def split3(x):
    hi = x.astype(BF16)
    rest = x - hi.astype(F32)
    mid = rest.astype(BF16)
    return hi, mid, (rest - mid.astype(F32)).astype(BF16)


def split2(x):
    hi = x.astype(BF16)
    return hi, (x - hi.astype(F32)).astype(BF16)


def dot_nn(a, b):
    return lax.dot_general(a, b, (((1,), (0,)), ((), ())), preferred_element_type=F32)


def dot_nt(a, b):
    return lax.dot_general(a, b, (((1,), (1,)), ((), ())), preferred_element_type=F32)


def times_exact(x, zero_one):
    rows = x.shape[0]
    product = dot_nn(jnp.concatenate(split3(x), axis=0), zero_one)
    return product[:rows] + product[rows : 2 * rows] + product[2 * rows :]


def exact_times_t(zero_one, x):
    return sum(dot_nt(zero_one, part) for part in split3(x))


def traced_level(place, levels, quarters):
    level = jnp.zeros_like(place)
    first, begin = 0, 0
    for parts in CHUNKS:
        steps = sum(parts)
        rest = place - first
        quarter = sum((rest >= k * steps).astype(jnp.int32) for k in range(1, quarters))
        here = quarter * (levels // quarters - steps) + rest + begin
        level = jnp.where(rest >= 0, here, level)
        first, begin = first + steps * quarters, begin + steps
    return level


def rates_by_place(slab_levels, rates, levels, quarters):
    slabs = rates.shape[0]
    level = traced_level(iota((levels, slabs), 0), levels, quarters)
    index = jnp.zeros((levels, slabs), jnp.int32)
    end = jnp.int32(0)
    for s in range(slabs):
        end = end + slab_levels[SLAB_AT + s]
        index = index + (level >= end).astype(jnp.int32)
    chosen = (index == iota((levels, slabs), 1)).astype(F32).astype(BF16)
    return sum(dot_nn(chosen, part) for part in split3(rates))


def lane_of(table, lane):
    return jnp.take_along_axis(table, jnp.full(table.shape, lane, jnp.int32), axis=1)


def column_kernel(
    sizes, where_ref, control_ref, rate_hbm,
    column_ref, decay_ref, gain_ref, end_ref, send1_ref, send2_ref, send3_ref,
    kron, decay_all, weighted, rate_ref, arrived,
):
    levels, rows, cols, quarters, lat_count = sizes
    step = pl.program_id(0)
    lat, lon = where_ref[1], where_ref[2]
    full = levels * 8

    @pl.when(step == 0)
    def _():
        fetch = pltpu.make_async_copy(rate_hbm, rate_ref, arrived)
        fetch.start()
        band = where_ref[BAND_AT + where_ref[GROUP_AT]].astype(F32)
        out_level = traced_level(jnp.right_shift(iota((full, full), 0), 3), levels, quarters)
        spacing = out_level - jnp.right_shift(iota((full, full), 1), 3)
        same = jnp.bitwise_and(iota((full, full), 0), 7) == jnp.bitwise_and(iota((full, full), 1), 7)
        ratio = spacing.astype(F32) / band
        weight = jnp.exp(-2.0 * (ratio * ratio))
        keep = jnp.logical_and(same, jnp.abs(spacing).astype(F32) <= band)
        kron[...] = jnp.where(keep, weight, 0.0).astype(BF16)
        fetch.wait()
        level_rates = rates_by_place(where_ref, rate_ref[...], levels, quarters)
        own = iota((rows, rate_ref.shape[1]), 1) == lon * rows + iota((rows, rate_ref.shape[1]), 0)
        rate = exact_times_t(own.astype(F32).astype(BF16), level_rates)
        remain = 1.0 - rate
        decay_all[...] = log_decay(rate)
        decay_ref[...] = decay_all[...]
        gain_ref[...] = jnp.sqrt(rate * (2.0 - rate) / (1.0 + remain * remain))

    block = control_ref[0].astype(F32)
    halves = []
    for half in range(ROW_GROUP // 8):
        part = block[:, 8 * half : 8 * half + 8, :].reshape(full, cols).astype(BF16)
        halves.append(dot_nn(kron[...], part).reshape(levels, 8, cols))
    column = jnp.concatenate(halves, axis=1).astype(BF16)
    column_ref[...] = column

    log_a = decay_all[pl.ds(step * ROW_GROUP, ROW_GROUP), :]
    lane = iota((ROW_GROUP, LANES), 1).astype(F32)
    blocks = cols // LANES
    for place in range(levels):
        log_b = jnp.broadcast_to(log_a[:, place : place + 1], (ROW_GROUP, LANES))
        over = jnp.exp(log_b * float(LANES))
        x = column_ref[place].astype(F32)
        parts = [x[:, LANES * b : LANES * (b + 1)] for b in range(blocks)]
        along, against = parts[0], parts[-1]
        for b in range(1, blocks):
            along = parts[b] + over * along
            against = parts[-1 - b] + over * against
        weighted[0, place] = along * jnp.exp(log_b * (LANES - 1.0 - lane))
        weighted[1, place] = against * jnp.exp(log_b * lane)
    place_lane = iota((ROW_GROUP, levels), 1)
    forward = jnp.zeros((ROW_GROUP, levels), F32)
    backward = jnp.zeros((ROW_GROUP, levels), F32)
    for place in range(levels):
        along = jnp.sum(weighted[0, place], axis=1, keepdims=True)
        against = jnp.sum(weighted[1, place], axis=1, keepdims=True)
        forward = jnp.where(place_lane == place, along, forward)
        backward = jnp.where(place_lane == place, against, backward)
    power = (1 + cols * (2 * (lat_count - 1 - lat) + 1)).astype(F32)
    returning = backward - jnp.exp(log_a * power) * forward
    end_ref[...] = forward
    for shift, ref in ((1, send1_ref), (2, send2_ref), (3, send3_ref)):
        ref[...] = jnp.where(lat + shift < lat_count, forward, returning)


def row_kernel(
    sizes, where_ref, rate_ref,
    left_ref, left_sum_ref, right_ref, right_sum_ref, chain_ref,
):
    levels, rows, quarters, lon_count = sizes
    lon = where_ref[2]
    total = rate_ref.shape[1]
    rate = rates_by_place(where_ref, rate_ref[...], levels, quarters)
    remain = 1.0 - rate
    root = jnp.sqrt(rate * (2.0 - rate))
    gain = root * jnp.sqrt(root) / jnp.sqrt(jnp.sqrt(1.0 + remain * remain))
    log_c = log_decay(rate)
    owner = lambda at: jnp.right_shift(at * ((1 << 16) // rows + 1), 16)
    first, second = iota((total, total), 0), iota((total, total), 1)
    same = owner(first) == owner(second)
    upper = jnp.logical_and(same, first <= second).astype(F32).astype(BF16)
    lower = jnp.logical_and(same, first >= second).astype(F32).astype(BF16)
    running = times_exact(log_c, upper)
    before = running - log_c
    weight = gain * jnp.exp(running + before)
    sums = times_exact(weight, lower)
    left = jnp.exp(-before)
    right = gain * jnp.exp(-running)
    own = (iota((rows, total), 1) == lon * rows + iota((rows, total), 0)).astype(F32).astype(BF16)
    own_t = iota((total, LANES), 0) == lon * rows + iota((total, LANES), 1)
    own_t = jnp.logical_and(own_t, iota((total, LANES), 1) < rows).astype(F32).astype(BF16)
    left_ref[...] = exact_times_t(own, left)
    left_sum_ref[...] = exact_times_t(own, left * sums)
    right_ref[...] = times_exact(right, own_t)
    right_sum_ref[...] = times_exact(right * sums, own_t)

    inside = (owner(iota((total, LANES), 0)) == iota((total, LANES), 1)).astype(F32).astype(BF16)
    log_over = times_exact(log_c, inside)
    bounce = times_exact(weight, inside)
    source, target = iota((LANES, LANES), 0), iota((LANES, LANES), 1)
    between = jnp.logical_and(source > lon, source < target).astype(F32).astype(BF16)
    device = iota((levels, LANES), 1)
    beyond = jnp.logical_and(device > lon, device < lon_count)
    echo = jnp.sum(
        jnp.where(beyond, bounce * jnp.exp(2.0 * times_exact(log_over, between)), 0.0),
        axis=1,
        keepdims=True,
    )
    every = jnp.exp(log_over)
    over = jnp.sum(jnp.where(device == lon, every, 0.0), axis=1, keepdims=True)
    partner = jnp.bitwise_xor(lon, 1)
    partner_over = jnp.sum(jnp.where(device == partner, every, 0.0), axis=1, keepdims=True)
    pair, pairs = jnp.right_shift(lon, 1), lon_count // 2
    shift = jnp.bitwise_and(target, 63)
    is_before = pair >= shift
    low = jnp.where(is_before, 2 * (pair - shift) + 1, lon)
    high = jnp.where(is_before, lon, 2 * (pair - shift + pairs))
    path = jnp.logical_and(source > low, source < high).astype(F32).astype(BF16)
    reach = jnp.exp(times_exact(log_over, path))
    shift = jnp.bitwise_and(device, 63)
    counted = jnp.logical_and(shift >= 1, shift < pairs)
    counted = jnp.logical_and(counted, (pair >= shift) == (device < 64))
    chain = jnp.where(counted, reach, 0.0)
    for at, value in ((32, over), (33, echo), (34, partner_over)):
        chain = jnp.where(device == at, value, chain)
    chain_ref[...] = chain


def field_kernel(
    sizes, where_ref, column_ref, decay_ref, gain_ref, end_ref, got1_ref, got2_ref, got3_ref,
    right_ref, right_sum_ref, chain_ref, triangle_ref,
    fields, edge_ref, tables, powers, enters, scaled, sums,
):
    rows, cols, first_place, per_step, lat_count = sizes
    step = pl.program_id(0)
    lat = where_ref[1]
    blocks = cols // LANES

    @pl.when(step == 0)
    def _():
        log_a, gain = decay_ref[...], gain_ref[...]
        enter_left = jnp.zeros(log_a.shape, F32)
        enter_right = jnp.zeros(log_a.shape, F32)
        for shift, ref in ((1, got1_ref), (2, got2_ref), (3, got3_ref)):
            got = ref[...]
            is_left = lat >= shift
            power = jnp.where(is_left, shift - 1, lat_count - 1 - shift) * cols
            scaled = jnp.exp(log_a * power.astype(F32)) * got
            enter_left = enter_left + jnp.where(is_left, scaled, 0.0)
            enter_right = enter_right + jnp.where(is_left, 0.0, scaled)
        leaving = end_ref[...] + jnp.exp(log_a * float(cols)) * enter_left
        power = (1 + 2 * cols * (lat_count - 1 - lat)).astype(F32)
        enter_right = enter_right - jnp.exp(log_a * power) * leaving
        enter_left = gain * jnp.exp(log_a) * enter_left
        enter_right = gain * jnp.exp(log_a * float(LANES)) * enter_right
        tables[0] = jnp.concatenate([log_a, gain], axis=1)
        tables[1] = jnp.concatenate([enter_left, enter_right], axis=1)

    half = tables.shape[2] // 2
    lane = iota((rows, LANES), 1).astype(F32)
    row_number = iota((16, LANES), 0)
    tall = blocks * rows
    place_of = lambda u: first_place + step * per_step + u
    for u in range(per_step):
        log_a = lane_of(tables[0], place_of(u))
        gain = lane_of(tables[0], place_of(u) + half)
        enters[u, 0] = lane_of(tables[1], place_of(u))
        enters[u, 1] = lane_of(tables[1], place_of(u) + half)
        grow = jnp.exp(log_a * lane)
        shrink = jnp.exp(log_a * (-lane))
        powers[u, 0] = grow
        powers[u, 1] = shrink
        powers[u, 2] = jnp.exp(log_a * float(LANES))
        gain_grow, gain_shrink = gain * grow, gain * shrink
        x = column_ref[u].astype(F32)
        for b in range(blocks):
            part = x[:, LANES * b : LANES * (b + 1)]
            rows_at = slice(u * tall + b * rows, u * tall + (b + 1) * rows)
            for side, factor in enumerate((gain_shrink, gain_grow)):
                scaled[rows_at, LANES * side : LANES * (side + 1)] = (part * factor).astype(BF16)
    for u in range(per_step):
        at = slice(u * tall, (u + 1) * tall)
        sums[at, :] = dot_nn(scaled[at, :], triangle_ref[...])
    for u in range(per_step):
        grow, shrink, over = (powers[u, k] for k in range(3))
        at = lambda b: slice(u * tall + b * rows, u * tall + (b + 1) * rows)
        ahead = [sums[at(b), :LANES] for b in range(blocks)]
        behind = [sums[at(b), LANES:] for b in range(blocks)]
        lefts, rights_in = [enters[u, 0]], [enters[u, 1]]
        for b in range(blocks - 1):
            end = jnp.broadcast_to(ahead[b][:, LANES - 1 :], (rows, LANES))
            lefts.append(over * (lefts[-1] + end))
        for b in range(blocks - 1, 0, -1):
            first = scaled[at(b), LANES:].astype(F32) + behind[b]
            end = jnp.broadcast_to(first[:, :1], (rows, LANES))
            rights_in.append(over * (rights_in[-1] + end))
        rights_in = rights_in[::-1]
        for b in range(blocks):
            field = grow * (ahead[b] + lefts[b]) + shrink * (behind[b] + rights_in[b])
            high, low = split2(field)
            fields[u, :rows, LANES * b : LANES * (b + 1)] = high
            fields[u, LANES : LANES + rows, LANES * b : LANES * (b + 1)] = low
        nothing = jnp.zeros((LANES - rows, cols), BF16)
        fields[u, rows:LANES, :] = nothing
        fields[u, LANES + rows :, :] = nothing
    for u in range(per_step):
        ends = [split2(ref[u : u + 1, :]) for ref in (right_ref, right_sum_ref)]
        first = jnp.zeros((16, LANES), F32)
        for at, part in enumerate((ends[0][0], ends[1][0], ends[0][1], ends[1][1])):
            first = jnp.where(row_number == at, part.astype(F32), first)
        second = jnp.where(row_number < 2, first, 0.0)
        result = dot_nn(jnp.concatenate([first, second], axis=1).astype(BF16), fields[u])
        row = step * per_step + u
        chain_row = chain_ref[u : u + 1, :]
        over_rows, echo = chain_row[:, 32:33], chain_row[:, 33:34]
        end = over_rows * (result[0:1] + result[2:3])
        edge_ref[0, pl.ds(row, 1), :] = end
        edge_ref[1, pl.ds(row, 1), :] = result[1:2] + result[3:4] + over_rows * echo * end


def turn_block(scalars, number, quarters, blocks):
    turn = number // blocks
    turn = jnp.where(turn == 0, 2, jnp.where(turn == 1, 1, jnp.where(turn == 2, 3, 0)))
    return lax.rem(scalars[0] + turn, quarters) * blocks + lax.rem(number, blocks)


def row_kernel_of(rows, first, quarters, blocks):
    def kernel(where_ref, fields_ref, left_ref, left_sum_ref, right_ref, right_sum_ref, *rest):
        field_ref, table, matrices = rest[-3:]
        step, per_step = pl.program_id(0), fields_ref.shape[0]
        half = table.shape[1] // 2
        below = iota((rows, LANES), 0) >= iota((rows, LANES), 1)

        @pl.when(step == 0)
        def _():
            table[...] = jnp.concatenate([left_ref[...], left_sum_ref[...]], axis=1)
            matrices[...] = jnp.zeros_like(matrices)

        for u in range(per_step):
            place = turn_block(where_ref, first + step, quarters, blocks) * per_step + u
            left, left_sum = lane_of(table[...], place), lane_of(table[...], place + half)
            right, right_sum = right_ref[u : u + 1, :], right_sum_ref[u : u + 1, :]
            high, low = split2(jnp.where(below, left_sum * right, left * right_sum))
            matrices[u, :rows, :LANES] = high
            matrices[u, :rows, LANES:] = high
            matrices[u, rows:, :LANES] = low
        for u in range(per_step):
            result = dot_nn(matrices[u], fields_ref[u])
            field_ref[u] = result[:rows] + result[rows:]

    return kernel


def pair_kernel(where_ref, own_ref, got_ref, chain_ref, send1_ref, send2_ref, send3_ref, *, pairs, places):
    lon = where_ref[2]
    second = jnp.bitwise_and(lon, 1) == 1
    pair = jnp.right_shift(lon, 1)
    chain = chain_ref[places, :]
    over, partner_over = chain[:, 32:33], chain[:, 34:35]
    end, returning = own_ref[0], own_ref[1]
    got_end, got_returning = got_ref[0], got_ref[1]
    pair_end = jnp.where(second, end + over * got_end, got_end + partner_over * end)
    pair_returning = jnp.where(
        second, got_returning + partner_over * returning, returning + over * got_returning
    )
    for shift, ref in ((1, send1_ref), (2, send2_ref), (3, send3_ref)):
        ref[...] = jnp.where(pair + shift < pairs, pair_end, pair_returning)


def first_send_kernel(
    sizes, turn, places, where_ref, own_ref, got_ref, got1_ref, got2_ref, got3_ref, chain_ref, left_ref, left_sum_ref,
    field_ref, spread_ref, out_ref, enter_ref, leave_ref, table_ref,
):
    @pl.when(pl.program_id(0) == 0)
    def _():
        second = jnp.bitwise_and(where_ref[2], 1) == 1
        chain = chain_ref[places, :]
        over, echo = chain[:, 32:33], chain[:, 33:34]
        enter = jnp.where(second, got_ref[0], 0.0)
        leave = jnp.where(second, 0.0, got_ref[1])
        for shift, ref in ((1, got1_ref), (2, got2_ref), (3, got3_ref)):
            enter = enter + chain[:, shift : shift + 1] * ref[...]
            leave = leave + chain[:, 64 + shift : 65 + shift] * ref[...]
        enter_ref[...] = enter
        leave_ref[...] = over * (leave + echo * (own_ref[0] + over * enter))
        table_ref[...] = jnp.concatenate([left_ref[...], left_sum_ref[...]], axis=1)

    send_kernel(sizes, turn, 0, where_ref, enter_ref, leave_ref, table_ref, field_ref, spread_ref, out_ref)


def one_product(where_ref, refs, sizes, turn, step, u):
    field_ref, spread_ref, enter_ref, leave_ref, table_ref = refs
    first_place, steps, quarters = sizes
    cols = field_ref.shape[-1]
    row = lax.rem(where_ref[0] + turn, quarters) * steps + step
    place = first_place + row
    half = table_ref.shape[1] // 2
    wide = lambda lane: jnp.concatenate([lane_of(table_ref[...], lane)] * (cols // LANES), axis=1)
    enter, leave = enter_ref[pl.ds(row, 1), :], leave_ref[pl.ds(row, 1), :]
    filtered = field_ref[u] + wide(place + half) * enter + wide(place) * leave
    return spread_ref[0, u].astype(F32) * filtered.astype(BF16).astype(F32)


def send_kernel(sizes, turn, start, where_ref, enter_ref, leave_ref, table_ref, field_ref, spread_ref, *refs):
    *adds, out_ref = refs
    row_refs = (field_ref, spread_ref, enter_ref, leave_ref, table_ref)
    for u in range(PRODUCT_STEP):
        step = start + pl.program_id(0) * PRODUCT_STEP + u
        value = one_product(where_ref, row_refs, sizes, turn, step, u)
        for ref in adds:
            value = value + ref[u].astype(F32)
        out_ref[u] = value.astype(BF16)


def here_kernel(sizes, first_part, where_ref, enter_ref, leave_ref, table_ref, field_ref, spread_ref, got0_ref, got1_ref, out_ref):
    in_first = pl.program_id(0) * PRODUCT_STEP < first_part
    row_refs = (field_ref, spread_ref, enter_ref, leave_ref, table_ref)
    for u in range(PRODUCT_STEP):
        step = pl.program_id(0) * PRODUCT_STEP + u
        value = one_product(where_ref, row_refs, sizes, 0, step, u)
        out_ref[u] = value + jnp.where(in_first, got0_ref[u], got1_ref[u]).astype(F32)


def whole(shape):
    return pl.BlockSpec(shape, lambda *_: (0,) * len(shape))


def call(
    kernel, name, inputs, in_specs, outputs, out_specs, scratch=(), grid=(1,), cost=None, after=(), vmem=VMEM_LIMIT, aliases=None
):
    count = len(inputs)

    def ordered(*refs):
        return kernel(*refs[:count], *refs[count + len(after) :])

    inputs = (*inputs, *after)
    in_specs = [*in_specs, *([pl.BlockSpec(memory_space=pl.ANY)] * len(after))]
    return pl.pallas_call(
        ordered,
        out_shape=outputs,
        grid_spec=pltpu.PrefetchScalarGridSpec(
            num_scalar_prefetch=1,
            grid=grid,
            in_specs=in_specs,
            out_specs=out_specs,
            scratch_shapes=list(scratch),
        ),
        input_output_aliases=aliases or {},
        compiler_params=pltpu.CompilerParams(vmem_limit_bytes=vmem),
        cost_estimate=cost,
        name=name,
    )(*inputs)


def cost(flops, data):
    return pl.CostEstimate(flops=flops, bytes_accessed=data, transcendentals=0)


def triangle_table():
    at = np.arange(LANES)
    table = np.zeros((2 * LANES, 2 * LANES), np.float32)
    table[:LANES, :LANES] = at[:, None] <= at[None, :]
    table[LANES:, LANES:] = at[:, None] > at[None, :]
    return jnp.asarray(table, BF16)


def ring(axis, shift):
    count = lax.axis_size(axis)
    return [(i, (i + shift) % count) for i in range(count)]


def per_device(control, perturbation, slab_levels, member_group, band_width, zonal_rate, meridional_rate):
    _, levels, rows, cols = control.shape
    quarters, lat_count, lon_count = (lax.axis_size(a) for a in ("mem", "lat", "lon"))
    per_quarter = levels // quarters
    here = jnp.stack([lax.axis_index(a) for a in ("mem", "lat", "lon")]).astype(jnp.int32)
    where = jnp.concatenate([here, member_group, band_width, slab_levels])
    sds = jax.ShapeDtypeStruct
    table = sds((rows, levels), F32)
    table_spec = pl.BlockSpec((ROW_GROUP, levels), lambda g, _: (g, 0))

    column, decay, gain, end, *sends = call(
        functools.partial(column_kernel, (levels, rows, cols, quarters, lat_count)),
        "vertical_columns",
        (where, control, zonal_rate),
        [
            pl.BlockSpec((1, levels, ROW_GROUP, cols), lambda g, _: (0, 0, g, 0)),
            pl.BlockSpec(memory_space=pltpu.HBM),
        ],
        (sds((levels, rows, cols), BF16), table, table, table, table, table, table),
        (
            pl.BlockSpec((levels, ROW_GROUP, cols), lambda g, _: (0, g, 0)),
            whole((rows, levels)), whole((rows, levels)),
            table_spec, table_spec, table_spec, table_spec,
        ),
        scratch=[
            pltpu.VMEM((levels * 8, levels * 8), BF16),
            pltpu.VMEM((rows, levels), F32),
            pltpu.VMEM((2, levels, ROW_GROUP, LANES), F32),
            pltpu.VMEM(zonal_rate.shape, F32),
            pltpu.SemaphoreType.DMA,
        ],
        grid=(rows // ROW_GROUP,),
        cost=cost(2 * 512 * 512 * 384 * 12, 2 * levels * rows * cols * 2),
        vmem=COLUMN_VMEM_LIMIT,
    )
    got = [lax.ppermute(s, "lat", ring("lat", i + 1)) for i, s in enumerate(sends)]
    left, left_sum, right, right_sum, chain = call(
        functools.partial(row_kernel, (levels, rows, quarters, lon_count)),
        "row_terms",
        (where, meridional_rate),
        [whole(meridional_rate.shape)],
        (table, table, sds((levels, LANES), F32), sds((levels, LANES), F32), sds((levels, LANES), F32)),
        (
            whole((rows, levels)), whole((rows, levels)),
            whole((levels, LANES)), whole((levels, LANES)), whole((levels, LANES)),
        ),
        cost=cost(2 * 3 * 64 * 768 * 768 * 2, 1 << 20),
    )

    triangle = triangle_table()
    scale = 1.0 / math.sqrt(control.shape[0] * quarters - 1)
    plane = rows * cols
    table_wide = sds((rows, 2 * levels), F32)
    table_specs = [whole((rows, levels))] * 2
    to_partner = [(i, i ^ 1) for i in range(lon_count)]
    to_pair = lambda k: [(i, (i + 2 * k) % lon_count) for i in range(lon_count)]
    up, down = ring("mem", 1), ring("mem", -1)
    by_step = lambda offset, low=0, high=levels: pl.BlockSpec(
        (PRODUCT_STEP, rows, cols), lambda g, _: (jnp.clip(g - offset, low, high), 0, 0)
    )
    ends = np.cumsum([sum(parts) for parts in CHUNKS])

    def quarter_specs(c, turn, start):
        steps, begin = sum(CHUNKS[c]), int(ends[c]) - sum(CHUNKS[c])
        at = lambda g, w, wide, off: (
            lax.rem(w[0] + turn, quarters) * (wide // PRODUCT_STEP) + (off + start) // PRODUCT_STEP + g
        )
        return [
            pl.BlockSpec((PRODUCT_STEP, rows, cols), lambda g, w: (at(g, w, steps, 0), 0, 0)),
            pl.BlockSpec(
                (1, PRODUCT_STEP, rows, cols), lambda g, w: (0, at(g, w, per_quarter, begin), 0, 0)
            ),
        ]

    def edge_specs(steps):
        row = whole((steps * quarters, cols))
        return [row, row, whole(table_wide.shape)]

    def product_sizes(c):
        steps = sum(CHUNKS[c])
        return (int(ends[c]) - steps) * quarters, steps, quarters

    def send(c, turn, part, adds=(), after=()):
        field, enter, leave, lanes = states[c]
        start, count = part * CHUNKS[c][0], CHUNKS[c][part]
        (piece,) = call(
            functools.partial(send_kernel, product_sizes(c), turn, start),
            f"products_{turn}",
            (where, enter, leave, lanes, field, perturbation, *adds),
            edge_specs(sum(CHUNKS[c])) + quarter_specs(c, turn, start) + [by_step(0)] * len(adds),
            (sds((count, rows, cols), BF16),),
            (by_step(0),),
            grid=(count // PRODUCT_STEP,),
            cost=cost(count * plane * 8, count * plane * 8),
            after=after,
        )
        return piece

    def finish(c, two, one, after=()):
        sum_up = send(c, 1, 0, (two[0],), after)
        moved_up = lax.ppermute(sum_up, "mem", up)
        sum_down = send(c, 3, 1, (two[1],), (sum_up, *after))
        moved_down = lax.ppermute(sum_down, "mem", down)
        steps, first = sum(CHUNKS[c]), CHUNKS[c][0] // PRODUCT_STEP
        halves = [by_step(0, 0, first - 1), by_step(first, 0)]
        field, enter, leave, lanes = states[c]
        own = sds((steps, rows, cols), F32)
        here = call(
            functools.partial(here_kernel, product_sizes(c), CHUNKS[c][0]),
            "products_here",
            (where, enter, leave, lanes, field, perturbation, one[1], one[0]),
            edge_specs(steps) + quarter_specs(c, 0, 0) + halves,
            own,
            by_step(0),
            grid=(steps // PRODUCT_STEP,),
            cost=cost(steps * plane * 8, steps * plane * 14),
            after=(sum_down,),
        )
        moved = jnp.concatenate([moved_up, moved_down]).astype(F32)
        return (here + moved) * scale

    states, increments = [], []
    for c, parts in enumerate(CHUNKS):
        steps = sum(parts)
        in_chunk, first_place = steps * quarters, (int(ends[c]) - steps) * quarters
        places = slice(first_place, first_place + in_chunk)
        edge_spec, row_spec = whole((2, in_chunk, cols)), whole((in_chunk, cols))
        edge_row = sds((in_chunk, cols), F32)
        block = first_place // FIELD_STEP
        by_place = pl.BlockSpec((FIELD_STEP, LANES), lambda g, _, block=block: (block + g, 0))
        fields, edge = call(
            functools.partial(field_kernel, (rows, cols, first_place, FIELD_STEP, lat_count)),
            "zonal_rows",
            (where, column, decay, gain, end, *got, right, right_sum, chain, triangle),
            [pl.BlockSpec((FIELD_STEP, rows, cols), lambda g, _, block=block: (block + g, 0, 0))]
            + [whole((rows, levels))] * 6
            + [by_place, by_place, by_place, whole(triangle.shape)],
            (sds((in_chunk, 2 * LANES, cols), BF16), sds((2, in_chunk, cols), F32)),
            (pl.BlockSpec((FIELD_STEP, 2 * LANES, cols), lambda g, _: (g, 0, 0)), edge_spec),
            scratch=[
                pltpu.VMEM((2, rows, 2 * levels), F32),
                pltpu.VMEM((FIELD_STEP, 3, rows, LANES), F32),
                pltpu.VMEM((FIELD_STEP, 2, rows, LANES), F32),
                pltpu.VMEM((FIELD_STEP * rows * cols // LANES, 2 * LANES), BF16),
                pltpu.VMEM((FIELD_STEP * rows * cols // LANES, 2 * LANES), F32),
            ],
            grid=(in_chunk // FIELD_STEP,),
            cost=cost(in_chunk * plane * 2 * 1024 * 3, in_chunk * plane * 6),
            vmem=FIELD_VMEM_LIMIT,
        )
        def filter_rows(first, count, before, after=()):
            blocks = steps // FIELD_STEP
            number = lambda g, w: turn_block(w, first + g, quarters, blocks)
            level_rows = pl.BlockSpec((FIELD_STEP, LANES), lambda g, w: (number(g, w), 0))
            step_of = lambda height: pl.BlockSpec(
                (FIELD_STEP, height, cols), lambda g, w: (number(g, w), 0, 0)
            )
            extra = () if before is None else (before,)
            return call(
                row_kernel_of(rows, first, quarters, blocks),
                "row_filter",
                (where, fields, left, left_sum, right, right_sum, *extra),
                [step_of(2 * LANES), *table_specs, level_rows, level_rows]
                + [pl.BlockSpec(memory_space=pl.ANY)] * len(extra),
                sds((in_chunk, rows, cols), F32),
                step_of(rows),
                scratch=[
                    pltpu.VMEM((rows, 2 * levels), F32),
                    pltpu.VMEM((FIELD_STEP, 2 * rows, 2 * LANES), BF16),
                ],
                grid=(count,),
                cost=cost(count * FIELD_STEP * plane * 512, count * FIELD_STEP * plane * 8),
                after=after,
                aliases={6: 0} if extra else None,
            )

        partner = lax.ppermute(edge, "lon", to_partner)
        field = filter_rows(0, 4, None)
        pair_sends = call(
            functools.partial(pair_kernel, pairs=lon_count // 2, places=places),
            "pair_ends",
            (where, edge, partner, chain),
            [edge_spec, edge_spec, whole((levels, LANES))],
            (edge_row,) * 3,
            (row_spec,) * 3,
            after=(field,),
        )
        field = filter_rows(4, 2, field, after=(pair_sends[0],))
        pair_got = [lax.ppermute(p, "lon", to_pair(k + 1)) for k, p in enumerate(pair_sends)]
        count = parts[0]
        two_up, enter, leave, lanes = call(
            functools.partial(first_send_kernel, product_sizes(c), 2, places),
            "products_2",
            (where, edge, partner, *pair_got, chain, left, left_sum, field, perturbation),
            [edge_spec, edge_spec, row_spec, row_spec, row_spec, whole((levels, LANES)), *table_specs]
            + quarter_specs(c, 2, 0),
            (sds((count, rows, cols), BF16), edge_row, edge_row, table_wide),
            (by_step(0), row_spec, row_spec, whole(table_wide.shape)),
            grid=(count // PRODUCT_STEP,),
            cost=cost(count * plane * 8, count * plane * 8),
        )
        states.append((field, enter, leave, lanes))
        two_up_moved = lax.ppermute(two_up, "mem", up)
        two_down = send(c, 2, 1, after=(two_up,))
        two = two_up_moved, lax.ppermute(two_down, "mem", down)
        one_up = send(c, 1, 1, after=(two_down,))
        one_up_moved = lax.ppermute(one_up, "mem", up)
        one_down = send(c, 3, 0, after=(one_up,))
        one = one_up_moved, lax.ppermute(one_down, "mem", down)
        field = filter_rows(6, 2, field, after=(one_down,))
        states[c] = (field, enter, leave, lanes)
        increments.append(finish(c, two, one))
    return increments[0] if len(increments) == 1 else jnp.concatenate(increments)


def solution(mesh):
    return jax.shard_map(
        per_device,
        mesh=mesh,
        in_specs=(
            P("mem", None, "lon", "lat"),
            P("mem", None, "lon", "lat"),
            P(),
            P("mem"),
            P(),
            P(),
            P(),
        ),
        out_specs=P("mem", "lon", "lat"),
        check_vma=False,
    )
```

```python
import functools
import math

import jax
import jax.numpy as jnp
import numpy as np
from jax import lax
from jax.experimental import pallas as pl
from jax.experimental.pallas import tpu as pltpu
from jax.sharding import PartitionSpec as P

CHUNKS = ((8, 8),)
LANES = 128
GROUP_AT = 3
BAND_AT = 4
SLAB_AT = 8
ROW_GROUP = 32
FIELD_STEP = 8
PRODUCT_STEP = 4
VMEM_LIMIT = 8 * 1024 * 1024
COLUMN_VMEM_LIMIT = 48 * 1024 * 1024
FIELD_VMEM_LIMIT = 16 * 1024 * 1024

F32 = jnp.float32
BF16 = jnp.bfloat16


def iota(shape, axis):
    return lax.broadcasted_iota(jnp.int32, shape, axis)


def log_decay(rate):
    t = rate / (2.0 - rate)
    s = t * t
    series = 1.0 + s * (1 / 3 + s * (1 / 5 + s * (1 / 7 + s * (1 / 9 + s * (1 / 11 + s / 13)))))
    return -2.0 * t * series


def split3(x):
    hi = x.astype(BF16)
    rest = x - hi.astype(F32)
    mid = rest.astype(BF16)
    return hi, mid, (rest - mid.astype(F32)).astype(BF16)


def split2(x):
    hi = x.astype(BF16)
    return hi, (x - hi.astype(F32)).astype(BF16)


def dot_nn(a, b):
    return lax.dot_general(a, b, (((1,), (0,)), ((), ())), preferred_element_type=F32)


def dot_nt(a, b):
    return lax.dot_general(a, b, (((1,), (1,)), ((), ())), preferred_element_type=F32)


def times_exact(x, zero_one):
    rows = x.shape[0]
    product = dot_nn(jnp.concatenate(split3(x), axis=0), zero_one)
    return product[:rows] + product[rows : 2 * rows] + product[2 * rows :]


def exact_times_t(zero_one, x):
    return sum(dot_nt(zero_one, part) for part in split3(x))


def traced_level(place, levels, quarters):
    level = jnp.zeros_like(place)
    first, begin = 0, 0
    for parts in CHUNKS:
        steps = sum(parts)
        rest = place - first
        quarter = sum((rest >= k * steps).astype(jnp.int32) for k in range(1, quarters))
        here = quarter * (levels // quarters - steps) + rest + begin
        level = jnp.where(rest >= 0, here, level)
        first, begin = first + steps * quarters, begin + steps
    return level


def rates_by_place(slab_levels, rates, levels, quarters):
    slabs = rates.shape[0]
    level = traced_level(iota((levels, slabs), 0), levels, quarters)
    index = jnp.zeros((levels, slabs), jnp.int32)
    end = jnp.int32(0)
    for s in range(slabs):
        end = end + slab_levels[SLAB_AT + s]
        index = index + (level >= end).astype(jnp.int32)
    chosen = (index == iota((levels, slabs), 1)).astype(F32).astype(BF16)
    return sum(dot_nn(chosen, part) for part in split3(rates))


def lane_of(table, lane):
    return jnp.take_along_axis(table, jnp.full(table.shape, lane, jnp.int32), axis=1)


def column_kernel(
    sizes, where_ref, control_ref, rate_hbm,
    column_ref, decay_ref, gain_ref, end_ref, send1_ref, send2_ref, send3_ref,
    kron, decay_all, weighted, rate_ref, arrived,
):
    levels, rows, cols, quarters, lat_count = sizes
    step = pl.program_id(0)
    lat, lon = where_ref[1], where_ref[2]
    full = levels * 8

    @pl.when(step == 0)
    def _():
        fetch = pltpu.make_async_copy(rate_hbm, rate_ref, arrived)
        fetch.start()
        band = where_ref[BAND_AT + where_ref[GROUP_AT]].astype(F32)
        out_level = traced_level(jnp.right_shift(iota((full, full), 0), 3), levels, quarters)
        spacing = out_level - jnp.right_shift(iota((full, full), 1), 3)
        same = jnp.bitwise_and(iota((full, full), 0), 7) == jnp.bitwise_and(iota((full, full), 1), 7)
        ratio = spacing.astype(F32) / band
        weight = jnp.exp(-2.0 * (ratio * ratio))
        keep = jnp.logical_and(same, jnp.abs(spacing).astype(F32) <= band)
        kron[...] = jnp.where(keep, weight, 0.0).astype(BF16)
        fetch.wait()
        level_rates = rates_by_place(where_ref, rate_ref[...], levels, quarters)
        own = iota((rows, rate_ref.shape[1]), 1) == lon * rows + iota((rows, rate_ref.shape[1]), 0)
        rate = exact_times_t(own.astype(F32).astype(BF16), level_rates)
        remain = 1.0 - rate
        decay_all[...] = log_decay(rate)
        decay_ref[...] = decay_all[...]
        gain_ref[...] = jnp.sqrt(rate * (2.0 - rate) / (1.0 + remain * remain))

    block = control_ref[0].astype(F32)
    halves = []
    for half in range(ROW_GROUP // 8):
        part = block[:, 8 * half : 8 * half + 8, :].reshape(full, cols).astype(BF16)
        halves.append(dot_nn(kron[...], part).reshape(levels, 8, cols))
    column = jnp.concatenate(halves, axis=1).astype(BF16)
    column_ref[...] = column

    log_a = decay_all[pl.ds(step * ROW_GROUP, ROW_GROUP), :]
    lane = iota((ROW_GROUP, LANES), 1).astype(F32)
    blocks = cols // LANES
    for place in range(levels):
        log_b = jnp.broadcast_to(log_a[:, place : place + 1], (ROW_GROUP, LANES))
        over = jnp.exp(log_b * float(LANES))
        x = column_ref[place].astype(F32)
        parts = [x[:, LANES * b : LANES * (b + 1)] for b in range(blocks)]
        along, against = parts[0], parts[-1]
        for b in range(1, blocks):
            along = parts[b] + over * along
            against = parts[-1 - b] + over * against
        weighted[0, place] = along * jnp.exp(log_b * (LANES - 1.0 - lane))
        weighted[1, place] = against * jnp.exp(log_b * lane)
    place_lane = iota((ROW_GROUP, levels), 1)
    forward = jnp.zeros((ROW_GROUP, levels), F32)
    backward = jnp.zeros((ROW_GROUP, levels), F32)
    for place in range(levels):
        along = jnp.sum(weighted[0, place], axis=1, keepdims=True)
        against = jnp.sum(weighted[1, place], axis=1, keepdims=True)
        forward = jnp.where(place_lane == place, along, forward)
        backward = jnp.where(place_lane == place, against, backward)
    power = (1 + cols * (2 * (lat_count - 1 - lat) + 1)).astype(F32)
    returning = backward - jnp.exp(log_a * power) * forward
    end_ref[...] = forward
    for shift, ref in ((1, send1_ref), (2, send2_ref), (3, send3_ref)):
        ref[...] = jnp.where(lat + shift < lat_count, forward, returning)


def row_kernel(
    sizes, where_ref, rate_ref,
    left_ref, left_sum_ref, right_ref, right_sum_ref, chain_ref,
):
    levels, rows, quarters, lon_count = sizes
    lon = where_ref[2]
    total = rate_ref.shape[1]
    rate = rates_by_place(where_ref, rate_ref[...], levels, quarters)
    remain = 1.0 - rate
    root = jnp.sqrt(rate * (2.0 - rate))
    gain = root * jnp.sqrt(root) / jnp.sqrt(jnp.sqrt(1.0 + remain * remain))
    log_c = log_decay(rate)
    owner = lambda at: jnp.right_shift(at * ((1 << 16) // rows + 1), 16)
    first, second = iota((total, total), 0), iota((total, total), 1)
    same = owner(first) == owner(second)
    upper = jnp.logical_and(same, first <= second).astype(F32).astype(BF16)
    lower = jnp.logical_and(same, first >= second).astype(F32).astype(BF16)
    running = times_exact(log_c, upper)
    before = running - log_c
    weight = gain * jnp.exp(running + before)
    sums = times_exact(weight, lower)
    left = jnp.exp(-before)
    right = gain * jnp.exp(-running)
    own = (iota((rows, total), 1) == lon * rows + iota((rows, total), 0)).astype(F32).astype(BF16)
    own_t = iota((total, LANES), 0) == lon * rows + iota((total, LANES), 1)
    own_t = jnp.logical_and(own_t, iota((total, LANES), 1) < rows).astype(F32).astype(BF16)
    left_ref[...] = exact_times_t(own, left)
    left_sum_ref[...] = exact_times_t(own, left * sums)
    right_ref[...] = times_exact(right, own_t)
    right_sum_ref[...] = times_exact(right * sums, own_t)

    inside = (owner(iota((total, LANES), 0)) == iota((total, LANES), 1)).astype(F32).astype(BF16)
    log_over = times_exact(log_c, inside)
    bounce = times_exact(weight, inside)
    source, target = iota((LANES, LANES), 0), iota((LANES, LANES), 1)
    between = jnp.logical_and(source > lon, source < target).astype(F32).astype(BF16)
    device = iota((levels, LANES), 1)
    beyond = jnp.logical_and(device > lon, device < lon_count)
    echo = jnp.sum(
        jnp.where(beyond, bounce * jnp.exp(2.0 * times_exact(log_over, between)), 0.0),
        axis=1,
        keepdims=True,
    )
    every = jnp.exp(log_over)
    over = jnp.sum(jnp.where(device == lon, every, 0.0), axis=1, keepdims=True)
    partner = jnp.bitwise_xor(lon, 1)
    partner_over = jnp.sum(jnp.where(device == partner, every, 0.0), axis=1, keepdims=True)
    pair, pairs = jnp.right_shift(lon, 1), lon_count // 2
    shift = jnp.bitwise_and(target, 63)
    is_before = pair >= shift
    low = jnp.where(is_before, 2 * (pair - shift) + 1, lon)
    high = jnp.where(is_before, lon, 2 * (pair - shift + pairs))
    path = jnp.logical_and(source > low, source < high).astype(F32).astype(BF16)
    reach = jnp.exp(times_exact(log_over, path))
    shift = jnp.bitwise_and(device, 63)
    counted = jnp.logical_and(shift >= 1, shift < pairs)
    counted = jnp.logical_and(counted, (pair >= shift) == (device < 64))
    chain = jnp.where(counted, reach, 0.0)
    for at, value in ((32, over), (33, echo), (34, partner_over)):
        chain = jnp.where(device == at, value, chain)
    chain_ref[...] = chain


def field_kernel(
    sizes, where_ref, column_ref, decay_ref, gain_ref, end_ref, got1_ref, got2_ref, got3_ref,
    right_ref, right_sum_ref, chain_ref, triangle_ref,
    fields, edge_ref, edge_send_ref, tables, powers, enters, scaled, sums,
):
    rows, cols, first_place, per_step, lat_count = sizes
    step = pl.program_id(0)
    lat = where_ref[1]
    blocks = cols // LANES

    @pl.when(step == 0)
    def _():
        log_a, gain = decay_ref[...], gain_ref[...]
        enter_left = jnp.zeros(log_a.shape, F32)
        enter_right = jnp.zeros(log_a.shape, F32)
        for shift, ref in ((1, got1_ref), (2, got2_ref), (3, got3_ref)):
            got = ref[...]
            is_left = lat >= shift
            power = jnp.where(is_left, shift - 1, lat_count - 1 - shift) * cols
            scaled = jnp.exp(log_a * power.astype(F32)) * got
            enter_left = enter_left + jnp.where(is_left, scaled, 0.0)
            enter_right = enter_right + jnp.where(is_left, 0.0, scaled)
        leaving = end_ref[...] + jnp.exp(log_a * float(cols)) * enter_left
        power = (1 + 2 * cols * (lat_count - 1 - lat)).astype(F32)
        enter_right = enter_right - jnp.exp(log_a * power) * leaving
        enter_left = gain * jnp.exp(log_a) * enter_left
        enter_right = gain * jnp.exp(log_a * float(LANES)) * enter_right
        tables[0] = jnp.concatenate([log_a, gain], axis=1)
        tables[1] = jnp.concatenate([enter_left, enter_right], axis=1)

    half = tables.shape[2] // 2
    lane = iota((rows, LANES), 1).astype(F32)
    row_number = iota((16, LANES), 0)
    tall = blocks * rows
    place_of = lambda u: first_place + step * per_step + u
    for u in range(per_step):
        log_a = lane_of(tables[0], place_of(u))
        gain = lane_of(tables[0], place_of(u) + half)
        enters[u, 0] = lane_of(tables[1], place_of(u))
        enters[u, 1] = lane_of(tables[1], place_of(u) + half)
        grow = jnp.exp(log_a * lane)
        shrink = jnp.exp(log_a * (-lane))
        powers[u, 0] = grow
        powers[u, 1] = shrink
        powers[u, 2] = jnp.exp(log_a * float(LANES))
        gain_grow, gain_shrink = gain * grow, gain * shrink
        x = column_ref[u].astype(F32)
        for b in range(blocks):
            part = x[:, LANES * b : LANES * (b + 1)]
            rows_at = slice(u * tall + b * rows, u * tall + (b + 1) * rows)
            for side, factor in enumerate((gain_shrink, gain_grow)):
                scaled[rows_at, LANES * side : LANES * (side + 1)] = (part * factor).astype(BF16)
    for u in range(per_step):
        at = slice(u * tall, (u + 1) * tall)
        sums[at, :] = dot_nn(scaled[at, :], triangle_ref[...])
    for u in range(per_step):
        grow, shrink, over = (powers[u, k] for k in range(3))
        at = lambda b: slice(u * tall + b * rows, u * tall + (b + 1) * rows)
        ahead = [sums[at(b), :LANES] for b in range(blocks)]
        behind = [sums[at(b), LANES:] for b in range(blocks)]
        lefts, rights_in = [enters[u, 0]], [enters[u, 1]]
        for b in range(blocks - 1):
            end = jnp.broadcast_to(ahead[b][:, LANES - 1 :], (rows, LANES))
            lefts.append(over * (lefts[-1] + end))
        for b in range(blocks - 1, 0, -1):
            first = scaled[at(b), LANES:].astype(F32) + behind[b]
            end = jnp.broadcast_to(first[:, :1], (rows, LANES))
            rights_in.append(over * (rights_in[-1] + end))
        rights_in = rights_in[::-1]
        for b in range(blocks):
            field = grow * (ahead[b] + lefts[b]) + shrink * (behind[b] + rights_in[b])
            high, low = split2(field)
            fields[u, :rows, LANES * b : LANES * (b + 1)] = high
            fields[u, LANES : LANES + rows, LANES * b : LANES * (b + 1)] = low
        nothing = jnp.zeros((LANES - rows, cols), BF16)
        fields[u, rows:LANES, :] = nothing
        fields[u, LANES + rows :, :] = nothing
    for u in range(per_step):
        ends = [split2(ref[u : u + 1, :]) for ref in (right_ref, right_sum_ref)]
        first = jnp.zeros((16, LANES), F32)
        for at, part in enumerate((ends[0][0], ends[1][0], ends[0][1], ends[1][1])):
            first = jnp.where(row_number == at, part.astype(F32), first)
        second = jnp.where(row_number < 2, first, 0.0)
        result = dot_nn(jnp.concatenate([first, second], axis=1).astype(BF16), fields[u])
        row = step * per_step + u
        chain_row = chain_ref[u : u + 1, :]
        over_rows, echo = chain_row[:, 32:33], chain_row[:, 33:34]
        end = over_rows * (result[0:1] + result[2:3])
        edge_ref[0, pl.ds(row, 1), :] = end
        edge_ref[1, pl.ds(row, 1), :] = result[1:2] + result[3:4] + over_rows * echo * end

    @pl.when(step == pl.num_programs(0) - 1)
    def _():
        edge_send_ref[...] = edge_ref[...].astype(BF16)


def turn_block(scalars, number, quarters, blocks):
    turn = number // blocks
    turn = jnp.where(turn == 0, 2, jnp.where(turn == 1, 1, jnp.where(turn == 2, 3, 0)))
    return lax.rem(scalars[0] + turn, quarters) * blocks + lax.rem(number, blocks)


def row_kernel_of(rows, first, quarters, blocks):
    def kernel(where_ref, fields_ref, left_ref, left_sum_ref, right_ref, right_sum_ref, *rest):
        field_ref, table, matrices = rest[-3:]
        step, per_step = pl.program_id(0), fields_ref.shape[0]
        half = table.shape[1] // 2
        below = iota((rows, LANES), 0) >= iota((rows, LANES), 1)

        @pl.when(step == 0)
        def _():
            table[...] = jnp.concatenate([left_ref[...], left_sum_ref[...]], axis=1)
            matrices[...] = jnp.zeros_like(matrices)

        for u in range(per_step):
            place = turn_block(where_ref, first + step, quarters, blocks) * per_step + u
            left, left_sum = lane_of(table[...], place), lane_of(table[...], place + half)
            right, right_sum = right_ref[u : u + 1, :], right_sum_ref[u : u + 1, :]
            high, low = split2(jnp.where(below, left_sum * right, left * right_sum))
            matrices[u, :rows, :LANES] = high
            matrices[u, :rows, LANES:] = high
            matrices[u, rows:, :LANES] = low
        for u in range(per_step):
            result = dot_nn(matrices[u], fields_ref[u])
            field_ref[u] = result[:rows] + result[rows:]

    return kernel


def pair_kernel(where_ref, own_ref, got_ref, chain_ref, send1_ref, send2_ref, send3_ref, *, pairs, places):
    lon = where_ref[2]
    second = jnp.bitwise_and(lon, 1) == 1
    pair = jnp.right_shift(lon, 1)
    chain = chain_ref[places, :]
    over, partner_over = chain[:, 32:33], chain[:, 34:35]
    end, returning = own_ref[0], own_ref[1]
    got_end, got_returning = got_ref[0].astype(F32), got_ref[1].astype(F32)
    pair_end = jnp.where(second, end + over * got_end, got_end + partner_over * end)
    pair_returning = jnp.where(
        second, got_returning + partner_over * returning, returning + over * got_returning
    )
    for shift, ref in ((1, send1_ref), (2, send2_ref), (3, send3_ref)):
        ref[...] = jnp.where(pair + shift < pairs, pair_end, pair_returning).astype(BF16)


def first_send_kernel(
    sizes, turn, places, where_ref, own_ref, got_ref, got1_ref, got2_ref, got3_ref, chain_ref, left_ref, left_sum_ref,
    field_ref, spread_ref, out_ref, enter_ref, leave_ref, table_ref,
):
    @pl.when(pl.program_id(0) == 0)
    def _():
        second = jnp.bitwise_and(where_ref[2], 1) == 1
        chain = chain_ref[places, :]
        over, echo = chain[:, 32:33], chain[:, 33:34]
        enter = jnp.where(second, got_ref[0].astype(F32), 0.0)
        leave = jnp.where(second, 0.0, got_ref[1].astype(F32))
        for shift, ref in ((1, got1_ref), (2, got2_ref), (3, got3_ref)):
            got = ref[...].astype(F32)
            enter = enter + chain[:, shift : shift + 1] * got
            leave = leave + chain[:, 64 + shift : 65 + shift] * got
        enter_ref[...] = enter
        leave_ref[...] = over * (leave + echo * (own_ref[0] + over * enter))
        table_ref[...] = jnp.concatenate([left_ref[...], left_sum_ref[...]], axis=1)

    send_kernel(sizes, turn, 0, where_ref, enter_ref, leave_ref, table_ref, field_ref, spread_ref, out_ref)


def one_product(where_ref, refs, sizes, turn, step, u):
    field_ref, spread_ref, enter_ref, leave_ref, table_ref = refs
    first_place, steps, quarters = sizes
    cols = field_ref.shape[-1]
    row = lax.rem(where_ref[0] + turn, quarters) * steps + step
    place = first_place + row
    half = table_ref.shape[1] // 2
    wide = lambda lane: jnp.concatenate([lane_of(table_ref[...], lane)] * (cols // LANES), axis=1)
    enter, leave = enter_ref[pl.ds(row, 1), :], leave_ref[pl.ds(row, 1), :]
    filtered = field_ref[u] + wide(place + half) * enter + wide(place) * leave
    return spread_ref[0, u].astype(F32) * filtered


def send_kernel(sizes, turn, start, where_ref, enter_ref, leave_ref, table_ref, field_ref, spread_ref, *refs):
    *adds, out_ref = refs
    row_refs = (field_ref, spread_ref, enter_ref, leave_ref, table_ref)
    for u in range(PRODUCT_STEP):
        step = start + pl.program_id(0) * PRODUCT_STEP + u
        value = one_product(where_ref, row_refs, sizes, turn, step, u)
        for ref in adds:
            value = value + ref[u].astype(F32)
        out_ref[u] = value.astype(BF16)


def here_kernel(sizes, first_part, where_ref, enter_ref, leave_ref, table_ref, field_ref, spread_ref, got0_ref, got1_ref, out_ref):
    in_first = pl.program_id(0) * PRODUCT_STEP < first_part
    row_refs = (field_ref, spread_ref, enter_ref, leave_ref, table_ref)
    for u in range(PRODUCT_STEP):
        step = pl.program_id(0) * PRODUCT_STEP + u
        value = one_product(where_ref, row_refs, sizes, 0, step, u)
        out_ref[u] = value + jnp.where(in_first, got0_ref[u], got1_ref[u]).astype(F32)


def whole(shape):
    return pl.BlockSpec(shape, lambda *_: (0,) * len(shape))


def call(
    kernel, name, inputs, in_specs, outputs, out_specs, scratch=(), grid=(1,), cost=None, after=(), vmem=VMEM_LIMIT, aliases=None
):
    count = len(inputs)

    def ordered(*refs):
        return kernel(*refs[:count], *refs[count + len(after) :])

    inputs = (*inputs, *after)
    in_specs = [*in_specs, *([pl.BlockSpec(memory_space=pl.ANY)] * len(after))]
    return pl.pallas_call(
        ordered,
        out_shape=outputs,
        grid_spec=pltpu.PrefetchScalarGridSpec(
            num_scalar_prefetch=1,
            grid=grid,
            in_specs=in_specs,
            out_specs=out_specs,
            scratch_shapes=list(scratch),
        ),
        input_output_aliases=aliases or {},
        compiler_params=pltpu.CompilerParams(vmem_limit_bytes=vmem),
        cost_estimate=cost,
        name=name,
    )(*inputs)


def cost(flops, data):
    return pl.CostEstimate(flops=flops, bytes_accessed=data, transcendentals=0)


def triangle_table():
    at = np.arange(LANES)
    table = np.zeros((2 * LANES, 2 * LANES), np.float32)
    table[:LANES, :LANES] = at[:, None] <= at[None, :]
    table[LANES:, LANES:] = at[:, None] > at[None, :]
    return jnp.asarray(table, BF16)


def ring(axis, shift):
    count = lax.axis_size(axis)
    return [(i, (i + shift) % count) for i in range(count)]


def per_device(control, perturbation, slab_levels, member_group, band_width, zonal_rate, meridional_rate):
    _, levels, rows, cols = control.shape
    quarters, lat_count, lon_count = (lax.axis_size(a) for a in ("mem", "lat", "lon"))
    per_quarter = levels // quarters
    here = jnp.stack([lax.axis_index(a) for a in ("mem", "lat", "lon")]).astype(jnp.int32)
    where = jnp.concatenate([here, member_group, band_width, slab_levels])
    sds = jax.ShapeDtypeStruct
    table = sds((rows, levels), F32)
    table_spec = pl.BlockSpec((ROW_GROUP, levels), lambda g, _: (g, 0))

    column, decay, gain, end, *sends = call(
        functools.partial(column_kernel, (levels, rows, cols, quarters, lat_count)),
        "vertical_columns",
        (where, control, zonal_rate),
        [
            pl.BlockSpec((1, levels, ROW_GROUP, cols), lambda g, _: (0, 0, g, 0)),
            pl.BlockSpec(memory_space=pltpu.HBM),
        ],
        (sds((levels, rows, cols), BF16), table, table, table, table, table, table),
        (
            pl.BlockSpec((levels, ROW_GROUP, cols), lambda g, _: (0, g, 0)),
            whole((rows, levels)), whole((rows, levels)),
            table_spec, table_spec, table_spec, table_spec,
        ),
        scratch=[
            pltpu.VMEM((levels * 8, levels * 8), BF16),
            pltpu.VMEM((rows, levels), F32),
            pltpu.VMEM((2, levels, ROW_GROUP, LANES), F32),
            pltpu.VMEM(zonal_rate.shape, F32),
            pltpu.SemaphoreType.DMA,
        ],
        grid=(rows // ROW_GROUP,),
        cost=cost(2 * 512 * 512 * 384 * 12, 2 * levels * rows * cols * 2),
        vmem=COLUMN_VMEM_LIMIT,
    )
    got = [lax.ppermute(s, "lat", ring("lat", i + 1)) for i, s in enumerate(sends)]
    left, left_sum, right, right_sum, chain = call(
        functools.partial(row_kernel, (levels, rows, quarters, lon_count)),
        "row_terms",
        (where, meridional_rate),
        [whole(meridional_rate.shape)],
        (table, table, sds((levels, LANES), F32), sds((levels, LANES), F32), sds((levels, LANES), F32)),
        (
            whole((rows, levels)), whole((rows, levels)),
            whole((levels, LANES)), whole((levels, LANES)), whole((levels, LANES)),
        ),
        cost=cost(2 * 3 * 64 * 768 * 768 * 2, 1 << 20),
    )

    triangle = triangle_table()
    scale = 1.0 / math.sqrt(control.shape[0] * quarters - 1)
    plane = rows * cols
    table_wide = sds((rows, 2 * levels), F32)
    table_specs = [whole((rows, levels))] * 2
    to_partner = [(i, i ^ 1) for i in range(lon_count)]
    to_pair = lambda k: [(i, (i + 2 * k) % lon_count) for i in range(lon_count)]
    up, down = ring("mem", 1), ring("mem", -1)
    by_step = lambda offset, low=0, high=levels: pl.BlockSpec(
        (PRODUCT_STEP, rows, cols), lambda g, _: (jnp.clip(g - offset, low, high), 0, 0)
    )
    ends = np.cumsum([sum(parts) for parts in CHUNKS])

    def quarter_specs(c, turn, start):
        steps, begin = sum(CHUNKS[c]), int(ends[c]) - sum(CHUNKS[c])
        at = lambda g, w, wide, off: (
            lax.rem(w[0] + turn, quarters) * (wide // PRODUCT_STEP) + (off + start) // PRODUCT_STEP + g
        )
        return [
            pl.BlockSpec((PRODUCT_STEP, rows, cols), lambda g, w: (at(g, w, steps, 0), 0, 0)),
            pl.BlockSpec(
                (1, PRODUCT_STEP, rows, cols), lambda g, w: (0, at(g, w, per_quarter, begin), 0, 0)
            ),
        ]

    def edge_specs(steps):
        row = whole((steps * quarters, cols))
        return [row, row, whole(table_wide.shape)]

    def product_sizes(c):
        steps = sum(CHUNKS[c])
        return (int(ends[c]) - steps) * quarters, steps, quarters

    def send(c, turn, part, adds=(), after=()):
        field, enter, leave, lanes = states[c]
        start, count = part * CHUNKS[c][0], CHUNKS[c][part]
        (piece,) = call(
            functools.partial(send_kernel, product_sizes(c), turn, start),
            f"products_{turn}",
            (where, enter, leave, lanes, field, perturbation, *adds),
            edge_specs(sum(CHUNKS[c])) + quarter_specs(c, turn, start) + [by_step(0)] * len(adds),
            (sds((count, rows, cols), BF16),),
            (by_step(0),),
            grid=(count // PRODUCT_STEP,),
            cost=cost(count * plane * 8, count * plane * 8),
            after=after,
        )
        return piece

    def finish(c, two, one, after=()):
        sum_up = send(c, 1, 0, (two[0],), after)
        moved_up = lax.ppermute(sum_up, "mem", up)
        sum_down = send(c, 3, 1, (two[1],), (sum_up, *after))
        moved_down = lax.ppermute(sum_down, "mem", down)
        steps, first = sum(CHUNKS[c]), CHUNKS[c][0] // PRODUCT_STEP
        halves = [by_step(0, 0, first - 1), by_step(first, 0)]
        field, enter, leave, lanes = states[c]
        own = sds((steps, rows, cols), F32)
        here = call(
            functools.partial(here_kernel, product_sizes(c), CHUNKS[c][0]),
            "products_here",
            (where, enter, leave, lanes, field, perturbation, one[1], one[0]),
            edge_specs(steps) + quarter_specs(c, 0, 0) + halves,
            own,
            by_step(0),
            grid=(steps // PRODUCT_STEP,),
            cost=cost(steps * plane * 8, steps * plane * 14),
            after=(sum_down,),
        )
        moved = jnp.concatenate([moved_up, moved_down]).astype(F32)
        return (here + moved) * scale

    states, increments = [], []
    for c, parts in enumerate(CHUNKS):
        steps = sum(parts)
        in_chunk, first_place = steps * quarters, (int(ends[c]) - steps) * quarters
        places = slice(first_place, first_place + in_chunk)
        edge_spec, row_spec = whole((2, in_chunk, cols)), whole((in_chunk, cols))
        edge_row = sds((in_chunk, cols), F32)
        block = first_place // FIELD_STEP
        by_place = pl.BlockSpec((FIELD_STEP, LANES), lambda g, _, block=block: (block + g, 0))
        fields, edge, edge_send = call(
            functools.partial(field_kernel, (rows, cols, first_place, FIELD_STEP, lat_count)),
            "zonal_rows",
            (where, column, decay, gain, end, *got, right, right_sum, chain, triangle),
            [pl.BlockSpec((FIELD_STEP, rows, cols), lambda g, _, block=block: (block + g, 0, 0))]
            + [whole((rows, levels))] * 6
            + [by_place, by_place, by_place, whole(triangle.shape)],
            (sds((in_chunk, 2 * LANES, cols), BF16), sds((2, in_chunk, cols), F32), sds((2, in_chunk, cols), BF16)),
            (pl.BlockSpec((FIELD_STEP, 2 * LANES, cols), lambda g, _: (g, 0, 0)), edge_spec, edge_spec),
            scratch=[
                pltpu.VMEM((2, rows, 2 * levels), F32),
                pltpu.VMEM((FIELD_STEP, 3, rows, LANES), F32),
                pltpu.VMEM((FIELD_STEP, 2, rows, LANES), F32),
                pltpu.VMEM((FIELD_STEP * rows * cols // LANES, 2 * LANES), BF16),
                pltpu.VMEM((FIELD_STEP * rows * cols // LANES, 2 * LANES), F32),
            ],
            grid=(in_chunk // FIELD_STEP,),
            cost=cost(in_chunk * plane * 2 * 1024 * 3, in_chunk * plane * 6),
            vmem=FIELD_VMEM_LIMIT,
        )
        def filter_rows(first, count, before, after=()):
            blocks = steps // FIELD_STEP
            number = lambda g, w: turn_block(w, first + g, quarters, blocks)
            level_rows = pl.BlockSpec((FIELD_STEP, LANES), lambda g, w: (number(g, w), 0))
            step_of = lambda height: pl.BlockSpec(
                (FIELD_STEP, height, cols), lambda g, w: (number(g, w), 0, 0)
            )
            extra = () if before is None else (before,)
            return call(
                row_kernel_of(rows, first, quarters, blocks),
                "row_filter",
                (where, fields, left, left_sum, right, right_sum, *extra),
                [step_of(2 * LANES), *table_specs, level_rows, level_rows]
                + [pl.BlockSpec(memory_space=pl.ANY)] * len(extra),
                sds((in_chunk, rows, cols), F32),
                step_of(rows),
                scratch=[
                    pltpu.VMEM((rows, 2 * levels), F32),
                    pltpu.VMEM((FIELD_STEP, 2 * rows, 2 * LANES), BF16),
                ],
                grid=(count,),
                cost=cost(count * FIELD_STEP * plane * 512, count * FIELD_STEP * plane * 8),
                after=after,
                aliases={6: 0} if extra else None,
            )

        partner = lax.ppermute(edge_send, "lon", to_partner)
        field = filter_rows(0, 2, None)
        pair_sends = call(
            functools.partial(pair_kernel, pairs=lon_count // 2, places=places),
            "pair_ends",
            (where, edge, partner, chain),
            [edge_spec, edge_spec, whole((levels, LANES))],
            (sds((in_chunk, cols), BF16),) * 3,
            (row_spec,) * 3,
            after=(field,),
        )
        field = filter_rows(2, 2, field, after=(pair_sends[0],))
        pair_got = [lax.ppermute(p, "lon", to_pair(k + 1)) for k, p in enumerate(pair_sends)]
        count = parts[0]
        two_up, enter, leave, lanes = call(
            functools.partial(first_send_kernel, product_sizes(c), 2, places),
            "products_2",
            (where, edge, partner, *pair_got, chain, left, left_sum, field, perturbation),
            [edge_spec, edge_spec, row_spec, row_spec, row_spec, whole((levels, LANES)), *table_specs]
            + quarter_specs(c, 2, 0),
            (sds((count, rows, cols), BF16), edge_row, edge_row, table_wide),
            (by_step(0), row_spec, row_spec, whole(table_wide.shape)),
            grid=(count // PRODUCT_STEP,),
            cost=cost(count * plane * 8, count * plane * 8),
        )
        states.append((field, enter, leave, lanes))
        two_up_moved = lax.ppermute(two_up, "mem", up)
        two_down = send(c, 2, 1, after=(two_up,))
        two = two_up_moved, lax.ppermute(two_down, "mem", down)
        one_up = send(c, 1, 1, after=(two_down,))
        one_up_moved = lax.ppermute(one_up, "mem", up)
        field = filter_rows(4, 2, field, after=(one_up,))
        states[c] = (field, enter, leave, lanes)
        one_down = send(c, 3, 0)
        one = one_up_moved, lax.ppermute(one_down, "mem", down)
        field = filter_rows(6, 2, field, after=(one_down,))
        states[c] = (field, enter, leave, lanes)
        increments.append(finish(c, two, one))
    return increments[0] if len(increments) == 1 else jnp.concatenate(increments)


def solution(mesh):
    return jax.shard_map(
        per_device,
        mesh=mesh,
        in_specs=(
            P("mem", None, "lon", "lat"),
            P("mem", None, "lon", "lat"),
            P(),
            P("mem"),
            P(),
            P(),
            P(),
        ),
        out_specs=P("mem", "lon", "lat"),
        check_vma=False,
    )
```

```python
import functools
import math

import jax
import jax.numpy as jnp
import numpy as np
from jax import lax
from jax.experimental import pallas as pl
from jax.experimental.pallas import tpu as pltpu
from jax.sharding import PartitionSpec as P

CHUNKS = ((8, 8),)
LANES = 128
GROUP_AT = 3
BAND_AT = 4
SLAB_AT = 8
ROW_GROUP = 32
FIELD_STEP = 8
PRODUCT_STEP = 4
VMEM_LIMIT = 8 * 1024 * 1024
COLUMN_VMEM_LIMIT = 48 * 1024 * 1024
FIELD_VMEM_LIMIT = 16 * 1024 * 1024

F32 = jnp.float32
BF16 = jnp.bfloat16


def iota(shape, axis):
    return lax.broadcasted_iota(jnp.int32, shape, axis)


def log_decay(rate):
    t = rate / (2.0 - rate)
    s = t * t
    series = 1.0 + s * (1 / 3 + s * (1 / 5 + s * (1 / 7 + s * (1 / 9 + s * (1 / 11 + s / 13)))))
    return -2.0 * t * series


def split3(x):
    hi = x.astype(BF16)
    rest = x - hi.astype(F32)
    mid = rest.astype(BF16)
    return hi, mid, (rest - mid.astype(F32)).astype(BF16)


def split2(x):
    hi = x.astype(BF16)
    return hi, (x - hi.astype(F32)).astype(BF16)


def dot_nn(a, b):
    return lax.dot_general(a, b, (((1,), (0,)), ((), ())), preferred_element_type=F32)


def dot_nt(a, b):
    return lax.dot_general(a, b, (((1,), (1,)), ((), ())), preferred_element_type=F32)


def times_exact(x, zero_one):
    rows = x.shape[0]
    product = dot_nn(jnp.concatenate(split3(x), axis=0), zero_one)
    return product[:rows] + product[rows : 2 * rows] + product[2 * rows :]


def exact_times_t(zero_one, x):
    return sum(dot_nt(zero_one, part) for part in split3(x))


def traced_level(place, levels, quarters):
    level = jnp.zeros_like(place)
    first, begin = 0, 0
    for parts in CHUNKS:
        steps = sum(parts)
        rest = place - first
        quarter = sum((rest >= k * steps).astype(jnp.int32) for k in range(1, quarters))
        here = quarter * (levels // quarters - steps) + rest + begin
        level = jnp.where(rest >= 0, here, level)
        first, begin = first + steps * quarters, begin + steps
    return level


def rates_by_place(slab_levels, rates, levels, quarters):
    slabs = rates.shape[0]
    level = traced_level(iota((levels, slabs), 0), levels, quarters)
    index = jnp.zeros((levels, slabs), jnp.int32)
    end = jnp.int32(0)
    for s in range(slabs):
        end = end + slab_levels[SLAB_AT + s]
        index = index + (level >= end).astype(jnp.int32)
    chosen = (index == iota((levels, slabs), 1)).astype(F32).astype(BF16)
    return sum(dot_nn(chosen, part) for part in split3(rates))


def lane_of(table, lane):
    return jnp.take_along_axis(table, jnp.full(table.shape, lane, jnp.int32), axis=1)


def column_kernel(
    sizes, where_ref, control_ref, rate_hbm,
    column_ref, decay_ref, gain_ref, end_ref, send1_ref, send2_ref, send3_ref,
    kron, decay_all, weighted, rate_ref, arrived,
):
    levels, rows, cols, quarters, lat_count = sizes
    step = pl.program_id(0)
    lat, lon = where_ref[1], where_ref[2]
    full = levels * 8

    @pl.when(step == 0)
    def _():
        fetch = pltpu.make_async_copy(rate_hbm, rate_ref, arrived)
        fetch.start()
        band = where_ref[BAND_AT + where_ref[GROUP_AT]].astype(F32)
        out_level = traced_level(jnp.right_shift(iota((full, full), 0), 3), levels, quarters)
        spacing = out_level - jnp.right_shift(iota((full, full), 1), 3)
        same = jnp.bitwise_and(iota((full, full), 0), 7) == jnp.bitwise_and(iota((full, full), 1), 7)
        ratio = spacing.astype(F32) / band
        weight = jnp.exp(-2.0 * (ratio * ratio))
        keep = jnp.logical_and(same, jnp.abs(spacing).astype(F32) <= band)
        kron[...] = jnp.where(keep, weight, 0.0).astype(BF16)
        fetch.wait()
        level_rates = rates_by_place(where_ref, rate_ref[...], levels, quarters)
        own = iota((rows, rate_ref.shape[1]), 1) == lon * rows + iota((rows, rate_ref.shape[1]), 0)
        rate = exact_times_t(own.astype(F32).astype(BF16), level_rates)
        remain = 1.0 - rate
        decay_all[...] = log_decay(rate)
        decay_ref[...] = decay_all[...]
        gain_ref[...] = jnp.sqrt(rate * (2.0 - rate) / (1.0 + remain * remain))

    block = control_ref[0].astype(F32)
    halves = []
    for half in range(ROW_GROUP // 8):
        part = block[:, 8 * half : 8 * half + 8, :].reshape(full, cols).astype(BF16)
        halves.append(dot_nn(kron[...], part).reshape(levels, 8, cols))
    column = jnp.concatenate(halves, axis=1).astype(BF16)
    column_ref[...] = column

    log_a = decay_all[pl.ds(step * ROW_GROUP, ROW_GROUP), :]
    lane = iota((ROW_GROUP, LANES), 1).astype(F32)
    blocks = cols // LANES
    for place in range(levels):
        log_b = jnp.broadcast_to(log_a[:, place : place + 1], (ROW_GROUP, LANES))
        over = jnp.exp(log_b * float(LANES))
        x = column_ref[place].astype(F32)
        parts = [x[:, LANES * b : LANES * (b + 1)] for b in range(blocks)]
        along, against = parts[0], parts[-1]
        for b in range(1, blocks):
            along = parts[b] + over * along
            against = parts[-1 - b] + over * against
        weighted[0, place] = along * jnp.exp(log_b * (LANES - 1.0 - lane))
        weighted[1, place] = against * jnp.exp(log_b * lane)
    place_lane = iota((ROW_GROUP, levels), 1)
    forward = jnp.zeros((ROW_GROUP, levels), F32)
    backward = jnp.zeros((ROW_GROUP, levels), F32)
    for place in range(levels):
        along = jnp.sum(weighted[0, place], axis=1, keepdims=True)
        against = jnp.sum(weighted[1, place], axis=1, keepdims=True)
        forward = jnp.where(place_lane == place, along, forward)
        backward = jnp.where(place_lane == place, against, backward)
    power = (1 + cols * (2 * (lat_count - 1 - lat) + 1)).astype(F32)
    returning = backward - jnp.exp(log_a * power) * forward
    end_ref[...] = forward
    for shift, ref in ((1, send1_ref), (2, send2_ref), (3, send3_ref)):
        ref[...] = jnp.where(lat + shift < lat_count, forward, returning)


def row_kernel(
    sizes, where_ref, rate_ref,
    left_ref, left_sum_ref, right_ref, right_sum_ref, chain_ref,
):
    levels, rows, quarters, lon_count = sizes
    lon = where_ref[2]
    total = rate_ref.shape[1]
    rate = rates_by_place(where_ref, rate_ref[...], levels, quarters)
    remain = 1.0 - rate
    root = jnp.sqrt(rate * (2.0 - rate))
    gain = root * jnp.sqrt(root) / jnp.sqrt(jnp.sqrt(1.0 + remain * remain))
    log_c = log_decay(rate)
    owner = lambda at: jnp.right_shift(at * ((1 << 16) // rows + 1), 16)
    first, second = iota((total, total), 0), iota((total, total), 1)
    same = owner(first) == owner(second)
    upper = jnp.logical_and(same, first <= second).astype(F32).astype(BF16)
    lower = jnp.logical_and(same, first >= second).astype(F32).astype(BF16)
    running = times_exact(log_c, upper)
    before = running - log_c
    weight = gain * jnp.exp(running + before)
    sums = times_exact(weight, lower)
    left = jnp.exp(-before)
    right = gain * jnp.exp(-running)
    own = (iota((rows, total), 1) == lon * rows + iota((rows, total), 0)).astype(F32).astype(BF16)
    own_t = iota((total, LANES), 0) == lon * rows + iota((total, LANES), 1)
    own_t = jnp.logical_and(own_t, iota((total, LANES), 1) < rows).astype(F32).astype(BF16)
    left_ref[...] = exact_times_t(own, left)
    left_sum_ref[...] = exact_times_t(own, left * sums)
    right_ref[...] = times_exact(right, own_t)
    right_sum_ref[...] = times_exact(right * sums, own_t)

    inside = (owner(iota((total, LANES), 0)) == iota((total, LANES), 1)).astype(F32).astype(BF16)
    log_over = times_exact(log_c, inside)
    bounce = times_exact(weight, inside)
    source, target = iota((LANES, LANES), 0), iota((LANES, LANES), 1)
    between = jnp.logical_and(source > lon, source < target).astype(F32).astype(BF16)
    device = iota((levels, LANES), 1)
    beyond = jnp.logical_and(device > lon, device < lon_count)
    echo = jnp.sum(
        jnp.where(beyond, bounce * jnp.exp(2.0 * times_exact(log_over, between)), 0.0),
        axis=1,
        keepdims=True,
    )
    every = jnp.exp(log_over)
    over = jnp.sum(jnp.where(device == lon, every, 0.0), axis=1, keepdims=True)
    partner = jnp.bitwise_xor(lon, 1)
    partner_over = jnp.sum(jnp.where(device == partner, every, 0.0), axis=1, keepdims=True)
    pair, pairs = jnp.right_shift(lon, 1), lon_count // 2
    shift = jnp.bitwise_and(target, 63)
    is_before = pair >= shift
    low = jnp.where(is_before, 2 * (pair - shift) + 1, lon)
    high = jnp.where(is_before, lon, 2 * (pair - shift + pairs))
    path = jnp.logical_and(source > low, source < high).astype(F32).astype(BF16)
    reach = jnp.exp(times_exact(log_over, path))
    shift = jnp.bitwise_and(device, 63)
    counted = jnp.logical_and(shift >= 1, shift < pairs)
    counted = jnp.logical_and(counted, (pair >= shift) == (device < 64))
    chain = jnp.where(counted, reach, 0.0)
    for at, value in ((32, over), (33, echo), (34, partner_over)):
        chain = jnp.where(device == at, value, chain)
    chain_ref[...] = chain


def field_kernel(
    sizes, where_ref, column_ref, decay_ref, gain_ref, end_ref, got1_ref, got2_ref, got3_ref,
    right_ref, right_sum_ref, chain_ref, triangle_ref,
    fields, edge_ref, edge_send_ref, tables, powers, enters, scaled, sums,
):
    rows, cols, first_place, per_step, lat_count = sizes
    step = pl.program_id(0)
    lat = where_ref[1]
    blocks = cols // LANES

    @pl.when(step == 0)
    def _():
        log_a, gain = decay_ref[...], gain_ref[...]
        enter_left = jnp.zeros(log_a.shape, F32)
        enter_right = jnp.zeros(log_a.shape, F32)
        for shift, ref in ((1, got1_ref), (2, got2_ref), (3, got3_ref)):
            got = ref[...]
            is_left = lat >= shift
            power = jnp.where(is_left, shift - 1, lat_count - 1 - shift) * cols
            scaled = jnp.exp(log_a * power.astype(F32)) * got
            enter_left = enter_left + jnp.where(is_left, scaled, 0.0)
            enter_right = enter_right + jnp.where(is_left, 0.0, scaled)
        leaving = end_ref[...] + jnp.exp(log_a * float(cols)) * enter_left
        power = (1 + 2 * cols * (lat_count - 1 - lat)).astype(F32)
        enter_right = enter_right - jnp.exp(log_a * power) * leaving
        enter_left = gain * jnp.exp(log_a) * enter_left
        enter_right = gain * jnp.exp(log_a * float(LANES)) * enter_right
        tables[0] = jnp.concatenate([log_a, gain], axis=1)
        tables[1] = jnp.concatenate([enter_left, enter_right], axis=1)

    half = tables.shape[2] // 2
    lane = iota((rows, LANES), 1).astype(F32)
    row_number = iota((16, LANES), 0)
    tall = blocks * rows
    place_of = lambda u: first_place + step * per_step + u
    for u in range(per_step):
        log_a = lane_of(tables[0], place_of(u))
        gain = lane_of(tables[0], place_of(u) + half)
        enters[u, 0] = lane_of(tables[1], place_of(u))
        enters[u, 1] = lane_of(tables[1], place_of(u) + half)
        grow = jnp.exp(log_a * lane)
        shrink = jnp.exp(log_a * (-lane))
        powers[u, 0] = grow
        powers[u, 1] = shrink
        powers[u, 2] = jnp.exp(log_a * float(LANES))
        gain_grow, gain_shrink = gain * grow, gain * shrink
        x = column_ref[u].astype(F32)
        for b in range(blocks):
            part = x[:, LANES * b : LANES * (b + 1)]
            rows_at = slice(u * tall + b * rows, u * tall + (b + 1) * rows)
            for side, factor in enumerate((gain_shrink, gain_grow)):
                scaled[rows_at, LANES * side : LANES * (side + 1)] = (part * factor).astype(BF16)
    for u in range(per_step):
        at = slice(u * tall, (u + 1) * tall)
        sums[at, :] = dot_nn(scaled[at, :], triangle_ref[...])
    for u in range(per_step):
        grow, shrink, over = (powers[u, k] for k in range(3))
        at = lambda b: slice(u * tall + b * rows, u * tall + (b + 1) * rows)
        ahead = [sums[at(b), :LANES] for b in range(blocks)]
        behind = [sums[at(b), LANES:] for b in range(blocks)]
        lefts, rights_in = [enters[u, 0]], [enters[u, 1]]
        for b in range(blocks - 1):
            end = jnp.broadcast_to(ahead[b][:, LANES - 1 :], (rows, LANES))
            lefts.append(over * (lefts[-1] + end))
        for b in range(blocks - 1, 0, -1):
            first = scaled[at(b), LANES:].astype(F32) + behind[b]
            end = jnp.broadcast_to(first[:, :1], (rows, LANES))
            rights_in.append(over * (rights_in[-1] + end))
        rights_in = rights_in[::-1]
        for b in range(blocks):
            field = grow * (ahead[b] + lefts[b]) + shrink * (behind[b] + rights_in[b])
            high, low = split2(field)
            fields[u, :rows, LANES * b : LANES * (b + 1)] = high
            fields[u, LANES : LANES + rows, LANES * b : LANES * (b + 1)] = low
        nothing = jnp.zeros((LANES - rows, cols), BF16)
        fields[u, rows:LANES, :] = nothing
        fields[u, LANES + rows :, :] = nothing
    for u in range(per_step):
        ends = [split2(ref[u : u + 1, :]) for ref in (right_ref, right_sum_ref)]
        first = jnp.zeros((16, LANES), F32)
        for at, part in enumerate((ends[0][0], ends[1][0], ends[0][1], ends[1][1])):
            first = jnp.where(row_number == at, part.astype(F32), first)
        second = jnp.where(row_number < 2, first, 0.0)
        result = dot_nn(jnp.concatenate([first, second], axis=1).astype(BF16), fields[u])
        row = step * per_step + u
        chain_row = chain_ref[u : u + 1, :]
        over_rows, echo = chain_row[:, 32:33], chain_row[:, 33:34]
        end = over_rows * (result[0:1] + result[2:3])
        edge_ref[0, pl.ds(row, 1), :] = end
        edge_ref[1, pl.ds(row, 1), :] = result[1:2] + result[3:4] + over_rows * echo * end

    @pl.when(step == pl.num_programs(0) - 1)
    def _():
        edge_send_ref[...] = edge_ref[...].astype(BF16)


def turn_block(scalars, number, quarters, blocks):
    turn = number // blocks
    turn = jnp.where(turn == 0, 2, jnp.where(turn == 1, 1, jnp.where(turn == 2, 3, 0)))
    return lax.rem(scalars[0] + turn, quarters) * blocks + lax.rem(number, blocks)


def row_kernel_of(rows, first, quarters, blocks):
    def kernel(where_ref, fields_ref, left_ref, left_sum_ref, right_ref, right_sum_ref, *rest):
        field_ref, table, matrices = rest[-3:]
        step, per_step = pl.program_id(0), fields_ref.shape[0]
        half = table.shape[1] // 2
        below = iota((rows, LANES), 0) >= iota((rows, LANES), 1)

        @pl.when(step == 0)
        def _():
            table[...] = jnp.concatenate([left_ref[...], left_sum_ref[...]], axis=1)
            matrices[...] = jnp.zeros_like(matrices)

        for u in range(per_step):
            place = turn_block(where_ref, first + step, quarters, blocks) * per_step + u
            left, left_sum = lane_of(table[...], place), lane_of(table[...], place + half)
            right, right_sum = right_ref[u : u + 1, :], right_sum_ref[u : u + 1, :]
            high, low = split2(jnp.where(below, left_sum * right, left * right_sum))
            matrices[u, :rows, :LANES] = high
            matrices[u, :rows, LANES:] = high
            matrices[u, rows:, :LANES] = low
        for u in range(per_step):
            result = dot_nn(matrices[u], fields_ref[u])
            field_ref[u] = result[:rows] + result[rows:]

    return kernel


def pair_kernel(where_ref, own_ref, got_ref, chain_ref, send1_ref, send2_ref, send3_ref, *, pairs, places):
    lon = where_ref[2]
    second = jnp.bitwise_and(lon, 1) == 1
    pair = jnp.right_shift(lon, 1)
    chain = chain_ref[places, :]
    over, partner_over = chain[:, 32:33], chain[:, 34:35]
    end, returning = own_ref[0], own_ref[1]
    got_end, got_returning = got_ref[0].astype(F32), got_ref[1].astype(F32)
    pair_end = jnp.where(second, end + over * got_end, got_end + partner_over * end)
    pair_returning = jnp.where(
        second, got_returning + partner_over * returning, returning + over * got_returning
    )
    for shift, ref in ((1, send1_ref), (2, send2_ref), (3, send3_ref)):
        ref[...] = jnp.where(pair + shift < pairs, pair_end, pair_returning).astype(BF16)


def first_send_kernel(
    sizes, turn, places, where_ref, own_ref, got_ref, got1_ref, got2_ref, got3_ref, chain_ref, left_ref, left_sum_ref,
    field0_ref, spread0_ref, field1_ref, spread1_ref, out0_ref, out1_ref, enter_ref, leave_ref, table_ref,
):
    @pl.when(pl.program_id(0) == 0)
    def _():
        second = jnp.bitwise_and(where_ref[2], 1) == 1
        chain = chain_ref[places, :]
        over, echo = chain[:, 32:33], chain[:, 33:34]
        enter = jnp.where(second, got_ref[0].astype(F32), 0.0)
        leave = jnp.where(second, 0.0, got_ref[1].astype(F32))
        for shift, ref in ((1, got1_ref), (2, got2_ref), (3, got3_ref)):
            got = ref[...].astype(F32)
            enter = enter + chain[:, shift : shift + 1] * got
            leave = leave + chain[:, 64 + shift : 65 + shift] * got
        enter_ref[...] = enter
        leave_ref[...] = over * (leave + echo * (own_ref[0] + over * enter))
        table_ref[...] = jnp.concatenate([left_ref[...], left_sum_ref[...]], axis=1)

    state = (where_ref, enter_ref, leave_ref, table_ref)
    send_kernel(sizes, turn, 0, *state, field0_ref, spread0_ref, out0_ref)
    send_kernel(sizes, turn, sizes[1] // 2, *state, field1_ref, spread1_ref, out1_ref)


def one_product(where_ref, refs, sizes, turn, step, u):
    field_ref, spread_ref, enter_ref, leave_ref, table_ref = refs
    first_place, steps, quarters = sizes
    cols = field_ref.shape[-1]
    row = lax.rem(where_ref[0] + turn, quarters) * steps + step
    place = first_place + row
    half = table_ref.shape[1] // 2
    wide = lambda lane: jnp.concatenate([lane_of(table_ref[...], lane)] * (cols // LANES), axis=1)
    enter, leave = enter_ref[pl.ds(row, 1), :], leave_ref[pl.ds(row, 1), :]
    filtered = field_ref[u] + wide(place + half) * enter + wide(place) * leave
    return spread_ref[0, u].astype(F32) * filtered


def send_kernel(sizes, turn, start, where_ref, enter_ref, leave_ref, table_ref, field_ref, spread_ref, *refs):
    *adds, out_ref = refs
    row_refs = (field_ref, spread_ref, enter_ref, leave_ref, table_ref)
    for u in range(PRODUCT_STEP):
        step = start + pl.program_id(0) * PRODUCT_STEP + u
        value = one_product(where_ref, row_refs, sizes, turn, step, u)
        for ref in adds:
            value = value + ref[u].astype(F32)
        out_ref[u] = value.astype(BF16)


def here_kernel(sizes, first_part, where_ref, enter_ref, leave_ref, table_ref, field_ref, spread_ref, got0_ref, got1_ref, out_ref):
    in_first = pl.program_id(0) * PRODUCT_STEP < first_part
    row_refs = (field_ref, spread_ref, enter_ref, leave_ref, table_ref)
    for u in range(PRODUCT_STEP):
        step = pl.program_id(0) * PRODUCT_STEP + u
        value = one_product(where_ref, row_refs, sizes, 0, step, u)
        out_ref[u] = value + jnp.where(in_first, got0_ref[u], got1_ref[u]).astype(F32)


def whole(shape):
    return pl.BlockSpec(shape, lambda *_: (0,) * len(shape))


def call(
    kernel, name, inputs, in_specs, outputs, out_specs, scratch=(), grid=(1,), cost=None, after=(), vmem=VMEM_LIMIT, aliases=None
):
    count = len(inputs)

    def ordered(*refs):
        return kernel(*refs[:count], *refs[count + len(after) :])

    inputs = (*inputs, *after)
    in_specs = [*in_specs, *([pl.BlockSpec(memory_space=pl.ANY)] * len(after))]
    return pl.pallas_call(
        ordered,
        out_shape=outputs,
        grid_spec=pltpu.PrefetchScalarGridSpec(
            num_scalar_prefetch=1,
            grid=grid,
            in_specs=in_specs,
            out_specs=out_specs,
            scratch_shapes=list(scratch),
        ),
        input_output_aliases=aliases or {},
        compiler_params=pltpu.CompilerParams(vmem_limit_bytes=vmem),
        cost_estimate=cost,
        name=name,
    )(*inputs)


def cost(flops, data):
    return pl.CostEstimate(flops=flops, bytes_accessed=data, transcendentals=0)


def triangle_table():
    at = np.arange(LANES)
    table = np.zeros((2 * LANES, 2 * LANES), np.float32)
    table[:LANES, :LANES] = at[:, None] <= at[None, :]
    table[LANES:, LANES:] = at[:, None] > at[None, :]
    return jnp.asarray(table, BF16)


def ring(axis, shift):
    count = lax.axis_size(axis)
    return [(i, (i + shift) % count) for i in range(count)]


def per_device(control, perturbation, slab_levels, member_group, band_width, zonal_rate, meridional_rate):
    _, levels, rows, cols = control.shape
    quarters, lat_count, lon_count = (lax.axis_size(a) for a in ("mem", "lat", "lon"))
    per_quarter = levels // quarters
    here = jnp.stack([lax.axis_index(a) for a in ("mem", "lat", "lon")]).astype(jnp.int32)
    where = jnp.concatenate([here, member_group, band_width, slab_levels])
    sds = jax.ShapeDtypeStruct
    table = sds((rows, levels), F32)
    table_spec = pl.BlockSpec((ROW_GROUP, levels), lambda g, _: (g, 0))

    column, decay, gain, end, *sends = call(
        functools.partial(column_kernel, (levels, rows, cols, quarters, lat_count)),
        "vertical_columns",
        (where, control, zonal_rate),
        [
            pl.BlockSpec((1, levels, ROW_GROUP, cols), lambda g, _: (0, 0, g, 0)),
            pl.BlockSpec(memory_space=pltpu.HBM),
        ],
        (sds((levels, rows, cols), BF16), table, table, table, table, table, table),
        (
            pl.BlockSpec((levels, ROW_GROUP, cols), lambda g, _: (0, g, 0)),
            whole((rows, levels)), whole((rows, levels)),
            table_spec, table_spec, table_spec, table_spec,
        ),
        scratch=[
            pltpu.VMEM((levels * 8, levels * 8), BF16),
            pltpu.VMEM((rows, levels), F32),
            pltpu.VMEM((2, levels, ROW_GROUP, LANES), F32),
            pltpu.VMEM(zonal_rate.shape, F32),
            pltpu.SemaphoreType.DMA,
        ],
        grid=(rows // ROW_GROUP,),
        cost=cost(2 * 512 * 512 * 384 * 12, 2 * levels * rows * cols * 2),
        vmem=COLUMN_VMEM_LIMIT,
    )
    got = [lax.ppermute(s, "lat", ring("lat", i + 1)) for i, s in enumerate(sends)]
    left, left_sum, right, right_sum, chain = call(
        functools.partial(row_kernel, (levels, rows, quarters, lon_count)),
        "row_terms",
        (where, meridional_rate),
        [whole(meridional_rate.shape)],
        (table, table, sds((levels, LANES), F32), sds((levels, LANES), F32), sds((levels, LANES), F32)),
        (
            whole((rows, levels)), whole((rows, levels)),
            whole((levels, LANES)), whole((levels, LANES)), whole((levels, LANES)),
        ),
        cost=cost(2 * 3 * 64 * 768 * 768 * 2, 1 << 20),
    )

    triangle = triangle_table()
    scale = 1.0 / math.sqrt(control.shape[0] * quarters - 1)
    plane = rows * cols
    table_wide = sds((rows, 2 * levels), F32)
    table_specs = [whole((rows, levels))] * 2
    to_partner = [(i, i ^ 1) for i in range(lon_count)]
    to_pair = lambda k: [(i, (i + 2 * k) % lon_count) for i in range(lon_count)]
    up, down = ring("mem", 1), ring("mem", -1)
    by_step = lambda offset, low=0, high=levels: pl.BlockSpec(
        (PRODUCT_STEP, rows, cols), lambda g, _: (jnp.clip(g - offset, low, high), 0, 0)
    )
    ends = np.cumsum([sum(parts) for parts in CHUNKS])

    def quarter_specs(c, turn, start):
        steps, begin = sum(CHUNKS[c]), int(ends[c]) - sum(CHUNKS[c])
        at = lambda g, w, wide, off: (
            lax.rem(w[0] + turn, quarters) * (wide // PRODUCT_STEP) + (off + start) // PRODUCT_STEP + g
        )
        return [
            pl.BlockSpec((PRODUCT_STEP, rows, cols), lambda g, w: (at(g, w, steps, 0), 0, 0)),
            pl.BlockSpec(
                (1, PRODUCT_STEP, rows, cols), lambda g, w: (0, at(g, w, per_quarter, begin), 0, 0)
            ),
        ]

    def edge_specs(steps):
        row = whole((steps * quarters, cols))
        return [row, row, whole(table_wide.shape)]

    def product_sizes(c):
        steps = sum(CHUNKS[c])
        return (int(ends[c]) - steps) * quarters, steps, quarters

    def send(c, turn, part, adds=(), after=()):
        field, enter, leave, lanes = states[c]
        start, count = part * CHUNKS[c][0], CHUNKS[c][part]
        (piece,) = call(
            functools.partial(send_kernel, product_sizes(c), turn, start),
            f"products_{turn}",
            (where, enter, leave, lanes, field, perturbation, *adds),
            edge_specs(sum(CHUNKS[c])) + quarter_specs(c, turn, start) + [by_step(0)] * len(adds),
            (sds((count, rows, cols), BF16),),
            (by_step(0),),
            grid=(count // PRODUCT_STEP,),
            cost=cost(count * plane * 8, count * plane * 8),
            after=after,
        )
        return piece

    def finish(c, two, one, after=()):
        sum_up = send(c, 1, 0, (two[0],), after)
        moved_up = lax.ppermute(sum_up, "mem", up)
        sum_down = send(c, 3, 1, (two[1],), (sum_up, *after))
        moved_down = lax.ppermute(sum_down, "mem", down)
        steps, first = sum(CHUNKS[c]), CHUNKS[c][0] // PRODUCT_STEP
        halves = [by_step(0, 0, first - 1), by_step(first, 0)]
        field, enter, leave, lanes = states[c]
        own = sds((steps, rows, cols), F32)
        here = call(
            functools.partial(here_kernel, product_sizes(c), CHUNKS[c][0]),
            "products_here",
            (where, enter, leave, lanes, field, perturbation, one[1], one[0]),
            edge_specs(steps) + quarter_specs(c, 0, 0) + halves,
            own,
            by_step(0),
            grid=(steps // PRODUCT_STEP,),
            cost=cost(steps * plane * 8, steps * plane * 14),
            after=(sum_down,),
        )
        moved = jnp.concatenate([moved_up, moved_down]).astype(F32)
        return (here + moved) * scale

    states, increments = [], []
    for c, parts in enumerate(CHUNKS):
        steps = sum(parts)
        in_chunk, first_place = steps * quarters, (int(ends[c]) - steps) * quarters
        places = slice(first_place, first_place + in_chunk)
        edge_spec, row_spec = whole((2, in_chunk, cols)), whole((in_chunk, cols))
        edge_row = sds((in_chunk, cols), F32)
        block = first_place // FIELD_STEP
        by_place = pl.BlockSpec((FIELD_STEP, LANES), lambda g, _, block=block: (block + g, 0))
        fields, edge, edge_send = call(
            functools.partial(field_kernel, (rows, cols, first_place, FIELD_STEP, lat_count)),
            "zonal_rows",
            (where, column, decay, gain, end, *got, right, right_sum, chain, triangle),
            [pl.BlockSpec((FIELD_STEP, rows, cols), lambda g, _, block=block: (block + g, 0, 0))]
            + [whole((rows, levels))] * 6
            + [by_place, by_place, by_place, whole(triangle.shape)],
            (sds((in_chunk, 2 * LANES, cols), BF16), sds((2, in_chunk, cols), F32), sds((2, in_chunk, cols), BF16)),
            (pl.BlockSpec((FIELD_STEP, 2 * LANES, cols), lambda g, _: (g, 0, 0)), edge_spec, edge_spec),
            scratch=[
                pltpu.VMEM((2, rows, 2 * levels), F32),
                pltpu.VMEM((FIELD_STEP, 3, rows, LANES), F32),
                pltpu.VMEM((FIELD_STEP, 2, rows, LANES), F32),
                pltpu.VMEM((FIELD_STEP * rows * cols // LANES, 2 * LANES), BF16),
                pltpu.VMEM((FIELD_STEP * rows * cols // LANES, 2 * LANES), F32),
            ],
            grid=(in_chunk // FIELD_STEP,),
            cost=cost(in_chunk * plane * 2 * 1024 * 3, in_chunk * plane * 6),
            vmem=FIELD_VMEM_LIMIT,
        )
        def filter_rows(first, count, before, after=()):
            blocks = steps // FIELD_STEP
            number = lambda g, w: turn_block(w, first + g, quarters, blocks)
            level_rows = pl.BlockSpec((FIELD_STEP, LANES), lambda g, w: (number(g, w), 0))
            step_of = lambda height: pl.BlockSpec(
                (FIELD_STEP, height, cols), lambda g, w: (number(g, w), 0, 0)
            )
            extra = () if before is None else (before,)
            return call(
                row_kernel_of(rows, first, quarters, blocks),
                "row_filter",
                (where, fields, left, left_sum, right, right_sum, *extra),
                [step_of(2 * LANES), *table_specs, level_rows, level_rows]
                + [pl.BlockSpec(memory_space=pl.ANY)] * len(extra),
                sds((in_chunk, rows, cols), F32),
                step_of(rows),
                scratch=[
                    pltpu.VMEM((rows, 2 * levels), F32),
                    pltpu.VMEM((FIELD_STEP, 2 * rows, 2 * LANES), BF16),
                ],
                grid=(count,),
                cost=cost(count * FIELD_STEP * plane * 512, count * FIELD_STEP * plane * 8),
                after=after,
                aliases={6: 0} if extra else None,
            )

        partner = lax.ppermute(edge_send, "lon", to_partner)
        field = filter_rows(0, 2, None)
        pair_sends = call(
            functools.partial(pair_kernel, pairs=lon_count // 2, places=places),
            "pair_ends",
            (where, edge, partner, chain),
            [edge_spec, edge_spec, whole((levels, LANES))],
            (sds((in_chunk, cols), BF16),) * 3,
            (row_spec,) * 3,
            after=(field,),
        )
        field = filter_rows(2, 2, field, after=(pair_sends[0],))
        pair_got = [lax.ppermute(p, "lon", to_pair(k + 1)) for k, p in enumerate(pair_sends)]
        count = parts[0]
        two_up, two_down, enter, leave, lanes = call(
            functools.partial(first_send_kernel, product_sizes(c), 2, places),
            "products_2",
            (where, edge, partner, *pair_got, chain, left, left_sum, *((field, perturbation) * 2)),
            [edge_spec, edge_spec, row_spec, row_spec, row_spec, whole((levels, LANES)), *table_specs]
            + quarter_specs(c, 2, 0)
            + quarter_specs(c, 2, count),
            (sds((count, rows, cols), BF16),) * 2 + (edge_row, edge_row, table_wide),
            (by_step(0), by_step(0), row_spec, row_spec, whole(table_wide.shape)),
            grid=(count // PRODUCT_STEP,),
            cost=cost(count * plane * 8, count * plane * 8),
        )
        states.append((field, enter, leave, lanes))
        two_up_moved = lax.ppermute(two_up, "mem", up)
        two = two_up_moved, lax.ppermute(two_down, "mem", down)
        one_up = send(c, 1, 1, after=(two_down,))
        one_up_moved = lax.ppermute(one_up, "mem", up)
        field = filter_rows(4, 2, field, after=(one_up,))
        states[c] = (field, enter, leave, lanes)
        one_down = send(c, 3, 0)
        one = one_up_moved, lax.ppermute(one_down, "mem", down)
        field = filter_rows(6, 2, field, after=(one_down,))
        states[c] = (field, enter, leave, lanes)
        increments.append(finish(c, two, one))
    return increments[0] if len(increments) == 1 else jnp.concatenate(increments)


def solution(mesh):
    return jax.shard_map(
        per_device,
        mesh=mesh,
        in_specs=(
            P("mem", None, "lon", "lat"),
            P("mem", None, "lon", "lat"),
            P(),
            P("mem"),
            P(),
            P(),
            P(),
        ),
        out_specs=P("mem", "lon", "lat"),
        check_vma=False,
    )
```

```python
import functools
import math

import jax
import jax.numpy as jnp
import numpy as np
from jax import lax
from jax.experimental import pallas as pl
from jax.experimental.pallas import tpu as pltpu
from jax.sharding import PartitionSpec as P

CHUNKS = ((8, 8),)
LANES = 128
GROUP_AT = 3
BAND_AT = 4
SLAB_AT = 8
ROW_GROUP = 32
FIELD_STEP = 8
PRODUCT_STEP = 8
VMEM_LIMIT = 12 * 1024 * 1024
COLUMN_VMEM_LIMIT = 48 * 1024 * 1024
FIELD_VMEM_LIMIT = 16 * 1024 * 1024

F32 = jnp.float32
BF16 = jnp.bfloat16


def iota(shape, axis):
    return lax.broadcasted_iota(jnp.int32, shape, axis)


def log_decay(rate):
    t = rate / (2.0 - rate)
    s = t * t
    series = 1.0 + s * (1 / 3 + s * (1 / 5 + s * (1 / 7 + s * (1 / 9 + s * (1 / 11 + s / 13)))))
    return -2.0 * t * series


def split3(x):
    hi = x.astype(BF16)
    rest = x - hi.astype(F32)
    mid = rest.astype(BF16)
    return hi, mid, (rest - mid.astype(F32)).astype(BF16)


def split2(x):
    hi = x.astype(BF16)
    return hi, (x - hi.astype(F32)).astype(BF16)


def dot_nn(a, b):
    return lax.dot_general(a, b, (((1,), (0,)), ((), ())), preferred_element_type=F32)


def dot_nt(a, b):
    return lax.dot_general(a, b, (((1,), (1,)), ((), ())), preferred_element_type=F32)


def times_exact(x, zero_one):
    rows = x.shape[0]
    product = dot_nn(jnp.concatenate(split3(x), axis=0), zero_one)
    return product[:rows] + product[rows : 2 * rows] + product[2 * rows :]


def exact_times_t(zero_one, x):
    return sum(dot_nt(zero_one, part) for part in split3(x))


def traced_level(place, levels, quarters):
    level = jnp.zeros_like(place)
    first, begin = 0, 0
    for parts in CHUNKS:
        steps = sum(parts)
        rest = place - first
        quarter = sum((rest >= k * steps).astype(jnp.int32) for k in range(1, quarters))
        here = quarter * (levels // quarters - steps) + rest + begin
        level = jnp.where(rest >= 0, here, level)
        first, begin = first + steps * quarters, begin + steps
    return level


def rates_by_place(slab_levels, rates, levels, quarters):
    slabs = rates.shape[0]
    level = traced_level(iota((levels, slabs), 0), levels, quarters)
    index = jnp.zeros((levels, slabs), jnp.int32)
    end = jnp.int32(0)
    for s in range(slabs):
        end = end + slab_levels[SLAB_AT + s]
        index = index + (level >= end).astype(jnp.int32)
    chosen = (index == iota((levels, slabs), 1)).astype(F32).astype(BF16)
    return sum(dot_nn(chosen, part) for part in split3(rates))


def lane_of(table, lane):
    return jnp.take_along_axis(table, jnp.full(table.shape, lane, jnp.int32), axis=1)


def column_kernel(
    sizes, where_ref, control_ref, rate_hbm,
    column_ref, decay_ref, gain_ref, end_ref, send1_ref, send2_ref, send3_ref,
    kron, decay_all, weighted, rate_ref, arrived,
):
    levels, rows, cols, quarters, lat_count = sizes
    step = pl.program_id(0)
    lat, lon = where_ref[1], where_ref[2]
    full = levels * 8

    @pl.when(step == 0)
    def _():
        fetch = pltpu.make_async_copy(rate_hbm, rate_ref, arrived)
        fetch.start()
        band = where_ref[BAND_AT + where_ref[GROUP_AT]].astype(F32)
        out_level = traced_level(jnp.right_shift(iota((full, full), 0), 3), levels, quarters)
        spacing = out_level - jnp.right_shift(iota((full, full), 1), 3)
        same = jnp.bitwise_and(iota((full, full), 0), 7) == jnp.bitwise_and(iota((full, full), 1), 7)
        ratio = spacing.astype(F32) / band
        weight = jnp.exp(-2.0 * (ratio * ratio))
        keep = jnp.logical_and(same, jnp.abs(spacing).astype(F32) <= band)
        kron[...] = jnp.where(keep, weight, 0.0).astype(BF16)
        fetch.wait()
        level_rates = rates_by_place(where_ref, rate_ref[...], levels, quarters)
        own = iota((rows, rate_ref.shape[1]), 1) == lon * rows + iota((rows, rate_ref.shape[1]), 0)
        rate = exact_times_t(own.astype(F32).astype(BF16), level_rates)
        remain = 1.0 - rate
        decay_all[...] = log_decay(rate)
        decay_ref[...] = decay_all[...]
        gain_ref[...] = jnp.sqrt(rate * (2.0 - rate) / (1.0 + remain * remain))

    block = control_ref[0].astype(F32)
    halves = []
    for half in range(ROW_GROUP // 8):
        part = block[:, 8 * half : 8 * half + 8, :].reshape(full, cols).astype(BF16)
        halves.append(dot_nn(kron[...], part).reshape(levels, 8, cols))
    column = jnp.concatenate(halves, axis=1).astype(BF16)
    column_ref[...] = column

    log_a = decay_all[pl.ds(step * ROW_GROUP, ROW_GROUP), :]
    lane = iota((ROW_GROUP, LANES), 1).astype(F32)
    blocks = cols // LANES
    for place in range(levels):
        log_b = jnp.broadcast_to(log_a[:, place : place + 1], (ROW_GROUP, LANES))
        over = jnp.exp(log_b * float(LANES))
        x = column_ref[place].astype(F32)
        parts = [x[:, LANES * b : LANES * (b + 1)] for b in range(blocks)]
        along, against = parts[0], parts[-1]
        for b in range(1, blocks):
            along = parts[b] + over * along
            against = parts[-1 - b] + over * against
        weighted[0, place] = along * jnp.exp(log_b * (LANES - 1.0 - lane))
        weighted[1, place] = against * jnp.exp(log_b * lane)
    place_lane = iota((ROW_GROUP, levels), 1)
    forward = jnp.zeros((ROW_GROUP, levels), F32)
    backward = jnp.zeros((ROW_GROUP, levels), F32)
    for place in range(levels):
        along = jnp.sum(weighted[0, place], axis=1, keepdims=True)
        against = jnp.sum(weighted[1, place], axis=1, keepdims=True)
        forward = jnp.where(place_lane == place, along, forward)
        backward = jnp.where(place_lane == place, against, backward)
    power = (1 + cols * (2 * (lat_count - 1 - lat) + 1)).astype(F32)
    returning = backward - jnp.exp(log_a * power) * forward
    end_ref[...] = forward
    for shift, ref in ((1, send1_ref), (2, send2_ref), (3, send3_ref)):
        ref[...] = jnp.where(lat + shift < lat_count, forward, returning)


def row_kernel(
    sizes, where_ref, rate_ref,
    left_ref, left_sum_ref, right_ref, right_sum_ref, chain_ref,
):
    levels, rows, quarters, lon_count = sizes
    lon = where_ref[2]
    total = rate_ref.shape[1]
    rate = rates_by_place(where_ref, rate_ref[...], levels, quarters)
    remain = 1.0 - rate
    root = jnp.sqrt(rate * (2.0 - rate))
    gain = root * jnp.sqrt(root) / jnp.sqrt(jnp.sqrt(1.0 + remain * remain))
    log_c = log_decay(rate)
    owner = lambda at: jnp.right_shift(at * ((1 << 16) // rows + 1), 16)
    first, second = iota((total, total), 0), iota((total, total), 1)
    same = owner(first) == owner(second)
    upper = jnp.logical_and(same, first <= second).astype(F32).astype(BF16)
    lower = jnp.logical_and(same, first >= second).astype(F32).astype(BF16)
    running = times_exact(log_c, upper)
    before = running - log_c
    weight = gain * jnp.exp(running + before)
    sums = times_exact(weight, lower)
    left = jnp.exp(-before)
    right = gain * jnp.exp(-running)
    own = (iota((rows, total), 1) == lon * rows + iota((rows, total), 0)).astype(F32).astype(BF16)
    own_t = iota((total, LANES), 0) == lon * rows + iota((total, LANES), 1)
    own_t = jnp.logical_and(own_t, iota((total, LANES), 1) < rows).astype(F32).astype(BF16)
    left_ref[...] = exact_times_t(own, left)
    left_sum_ref[...] = exact_times_t(own, left * sums)
    right_ref[...] = times_exact(right, own_t)
    right_sum_ref[...] = times_exact(right * sums, own_t)

    inside = (owner(iota((total, LANES), 0)) == iota((total, LANES), 1)).astype(F32).astype(BF16)
    log_over = times_exact(log_c, inside)
    bounce = times_exact(weight, inside)
    source, target = iota((LANES, LANES), 0), iota((LANES, LANES), 1)
    between = jnp.logical_and(source > lon, source < target).astype(F32).astype(BF16)
    device = iota((levels, LANES), 1)
    beyond = jnp.logical_and(device > lon, device < lon_count)
    echo = jnp.sum(
        jnp.where(beyond, bounce * jnp.exp(2.0 * times_exact(log_over, between)), 0.0),
        axis=1,
        keepdims=True,
    )
    every = jnp.exp(log_over)
    over = jnp.sum(jnp.where(device == lon, every, 0.0), axis=1, keepdims=True)
    partner = jnp.bitwise_xor(lon, 1)
    partner_over = jnp.sum(jnp.where(device == partner, every, 0.0), axis=1, keepdims=True)
    pair, pairs = jnp.right_shift(lon, 1), lon_count // 2
    shift = jnp.bitwise_and(target, 63)
    is_before = pair >= shift
    low = jnp.where(is_before, 2 * (pair - shift) + 1, lon)
    high = jnp.where(is_before, lon, 2 * (pair - shift + pairs))
    path = jnp.logical_and(source > low, source < high).astype(F32).astype(BF16)
    reach = jnp.exp(times_exact(log_over, path))
    shift = jnp.bitwise_and(device, 63)
    counted = jnp.logical_and(shift >= 1, shift < pairs)
    counted = jnp.logical_and(counted, (pair >= shift) == (device < 64))
    chain = jnp.where(counted, reach, 0.0)
    for at, value in ((32, over), (33, echo), (34, partner_over)):
        chain = jnp.where(device == at, value, chain)
    chain_ref[...] = chain


def field_kernel(
    sizes, where_ref, column_ref, decay_ref, gain_ref, end_ref, got1_ref, got2_ref, got3_ref,
    right_ref, right_sum_ref, chain_ref, triangle_ref,
    fields, edge_ref, edge_send_ref, tables, powers, enters, scaled, sums,
):
    rows, cols, first_place, per_step, lat_count = sizes
    step = pl.program_id(0)
    lat = where_ref[1]
    blocks = cols // LANES

    @pl.when(step == 0)
    def _():
        log_a, gain = decay_ref[...], gain_ref[...]
        enter_left = jnp.zeros(log_a.shape, F32)
        enter_right = jnp.zeros(log_a.shape, F32)
        for shift, ref in ((1, got1_ref), (2, got2_ref), (3, got3_ref)):
            got = ref[...]
            is_left = lat >= shift
            power = jnp.where(is_left, shift - 1, lat_count - 1 - shift) * cols
            scaled = jnp.exp(log_a * power.astype(F32)) * got
            enter_left = enter_left + jnp.where(is_left, scaled, 0.0)
            enter_right = enter_right + jnp.where(is_left, 0.0, scaled)
        leaving = end_ref[...] + jnp.exp(log_a * float(cols)) * enter_left
        power = (1 + 2 * cols * (lat_count - 1 - lat)).astype(F32)
        enter_right = enter_right - jnp.exp(log_a * power) * leaving
        enter_left = gain * jnp.exp(log_a) * enter_left
        enter_right = gain * jnp.exp(log_a * float(LANES)) * enter_right
        tables[0] = jnp.concatenate([log_a, gain], axis=1)
        tables[1] = jnp.concatenate([enter_left, enter_right], axis=1)

    half = tables.shape[2] // 2
    lane = iota((rows, LANES), 1).astype(F32)
    row_number = iota((16, LANES), 0)
    tall = blocks * rows
    place_of = lambda u: first_place + step * per_step + u
    for u in range(per_step):
        log_a = lane_of(tables[0], place_of(u))
        gain = lane_of(tables[0], place_of(u) + half)
        enters[u, 0] = lane_of(tables[1], place_of(u))
        enters[u, 1] = lane_of(tables[1], place_of(u) + half)
        grow = jnp.exp(log_a * lane)
        shrink = jnp.exp(log_a * (-lane))
        powers[u, 0] = grow
        powers[u, 1] = shrink
        powers[u, 2] = jnp.exp(log_a * float(LANES))
        gain_grow, gain_shrink = gain * grow, gain * shrink
        x = column_ref[u].astype(F32)
        for b in range(blocks):
            part = x[:, LANES * b : LANES * (b + 1)]
            rows_at = slice(u * tall + b * rows, u * tall + (b + 1) * rows)
            for side, factor in enumerate((gain_shrink, gain_grow)):
                scaled[rows_at, LANES * side : LANES * (side + 1)] = (part * factor).astype(BF16)
    for u in range(per_step):
        at = slice(u * tall, (u + 1) * tall)
        sums[at, :] = dot_nn(scaled[at, :], triangle_ref[...])
    for u in range(per_step):
        grow, shrink, over = (powers[u, k] for k in range(3))
        at = lambda b: slice(u * tall + b * rows, u * tall + (b + 1) * rows)
        ahead = [sums[at(b), :LANES] for b in range(blocks)]
        behind = [sums[at(b), LANES:] for b in range(blocks)]
        lefts, rights_in = [enters[u, 0]], [enters[u, 1]]
        for b in range(blocks - 1):
            end = jnp.broadcast_to(ahead[b][:, LANES - 1 :], (rows, LANES))
            lefts.append(over * (lefts[-1] + end))
        for b in range(blocks - 1, 0, -1):
            first = scaled[at(b), LANES:].astype(F32) + behind[b]
            end = jnp.broadcast_to(first[:, :1], (rows, LANES))
            rights_in.append(over * (rights_in[-1] + end))
        rights_in = rights_in[::-1]
        for b in range(blocks):
            field = grow * (ahead[b] + lefts[b]) + shrink * (behind[b] + rights_in[b])
            high, low = split2(field)
            fields[u, :rows, LANES * b : LANES * (b + 1)] = high
            fields[u, LANES : LANES + rows, LANES * b : LANES * (b + 1)] = low
        nothing = jnp.zeros((LANES - rows, cols), BF16)
        fields[u, rows:LANES, :] = nothing
        fields[u, LANES + rows :, :] = nothing
    for u in range(per_step):
        ends = [split2(ref[u : u + 1, :]) for ref in (right_ref, right_sum_ref)]
        first = jnp.zeros((16, LANES), F32)
        for at, part in enumerate((ends[0][0], ends[1][0], ends[0][1], ends[1][1])):
            first = jnp.where(row_number == at, part.astype(F32), first)
        second = jnp.where(row_number < 2, first, 0.0)
        result = dot_nn(jnp.concatenate([first, second], axis=1).astype(BF16), fields[u])
        row = step * per_step + u
        chain_row = chain_ref[u : u + 1, :]
        over_rows, echo = chain_row[:, 32:33], chain_row[:, 33:34]
        end = over_rows * (result[0:1] + result[2:3])
        edge_ref[0, pl.ds(row, 1), :] = end
        edge_ref[1, pl.ds(row, 1), :] = result[1:2] + result[3:4] + over_rows * echo * end

    @pl.when(step == pl.num_programs(0) - 1)
    def _():
        edge_send_ref[...] = edge_ref[...].astype(BF16)


def turn_block(scalars, number, quarters, blocks):
    turn = number // blocks
    turn = jnp.where(turn == 0, 2, jnp.where(turn == 1, 1, jnp.where(turn == 2, 3, 0)))
    return lax.rem(scalars[0] + turn, quarters) * blocks + lax.rem(number, blocks)


def row_kernel_of(rows, first, quarters, blocks):
    def kernel(where_ref, fields_ref, left_ref, left_sum_ref, right_ref, right_sum_ref, *rest):
        field_ref, table, matrices = rest[-3:]
        step, per_step = pl.program_id(0), fields_ref.shape[0]
        half = table.shape[1] // 2
        below = iota((rows, LANES), 0) >= iota((rows, LANES), 1)

        @pl.when(step == 0)
        def _():
            table[...] = jnp.concatenate([left_ref[...], left_sum_ref[...]], axis=1)
            matrices[...] = jnp.zeros_like(matrices)

        for u in range(per_step):
            place = turn_block(where_ref, first + step, quarters, blocks) * per_step + u
            left, left_sum = lane_of(table[...], place), lane_of(table[...], place + half)
            right, right_sum = right_ref[u : u + 1, :], right_sum_ref[u : u + 1, :]
            high, low = split2(jnp.where(below, left_sum * right, left * right_sum))
            matrices[u, :rows, :LANES] = high
            matrices[u, :rows, LANES:] = high
            matrices[u, rows:, :LANES] = low
        for u in range(per_step):
            result = dot_nn(matrices[u], fields_ref[u])
            field_ref[u] = result[:rows] + result[rows:]

    return kernel


def pair_kernel(where_ref, own_ref, got_ref, chain_ref, send1_ref, send2_ref, send3_ref, *, pairs, places):
    lon = where_ref[2]
    second = jnp.bitwise_and(lon, 1) == 1
    pair = jnp.right_shift(lon, 1)
    chain = chain_ref[places, :]
    over, partner_over = chain[:, 32:33], chain[:, 34:35]
    end, returning = own_ref[0], own_ref[1]
    got_end, got_returning = got_ref[0].astype(F32), got_ref[1].astype(F32)
    pair_end = jnp.where(second, end + over * got_end, got_end + partner_over * end)
    pair_returning = jnp.where(
        second, got_returning + partner_over * returning, returning + over * got_returning
    )
    for shift, ref in ((1, send1_ref), (2, send2_ref), (3, send3_ref)):
        ref[...] = jnp.where(pair + shift < pairs, pair_end, pair_returning).astype(BF16)


def first_send_kernel(
    sizes, turn, places, where_ref, own_ref, got_ref, got1_ref, got2_ref, got3_ref, chain_ref, left_ref, left_sum_ref,
    field0_ref, spread0_ref, field1_ref, spread1_ref, out0_ref, out1_ref, enter_ref, leave_ref, table_ref,
):
    @pl.when(pl.program_id(0) == 0)
    def _():
        second = jnp.bitwise_and(where_ref[2], 1) == 1
        chain = chain_ref[places, :]
        over, echo = chain[:, 32:33], chain[:, 33:34]
        enter = jnp.where(second, got_ref[0].astype(F32), 0.0)
        leave = jnp.where(second, 0.0, got_ref[1].astype(F32))
        for shift, ref in ((1, got1_ref), (2, got2_ref), (3, got3_ref)):
            got = ref[...].astype(F32)
            enter = enter + chain[:, shift : shift + 1] * got
            leave = leave + chain[:, 64 + shift : 65 + shift] * got
        enter_ref[...] = enter
        leave_ref[...] = over * (leave + echo * (own_ref[0] + over * enter))
        table_ref[...] = jnp.concatenate([left_ref[...], left_sum_ref[...]], axis=1)

    state = (where_ref, enter_ref, leave_ref, table_ref)
    send_kernel(sizes, turn, 0, *state, field0_ref, spread0_ref, out0_ref)
    send_kernel(sizes, turn, sizes[1] // 2, *state, field1_ref, spread1_ref, out1_ref)


def one_product(where_ref, refs, sizes, turn, step, u):
    field_ref, spread_ref, enter_ref, leave_ref, table_ref = refs
    first_place, steps, quarters = sizes
    cols = field_ref.shape[-1]
    row = lax.rem(where_ref[0] + turn, quarters) * steps + step
    place = first_place + row
    half = table_ref.shape[1] // 2
    wide = lambda lane: jnp.concatenate([lane_of(table_ref[...], lane)] * (cols // LANES), axis=1)
    enter, leave = enter_ref[pl.ds(row, 1), :], leave_ref[pl.ds(row, 1), :]
    filtered = field_ref[u] + wide(place + half) * enter + wide(place) * leave
    return spread_ref[0, u].astype(F32) * filtered


def send_kernel(sizes, turn, start, where_ref, enter_ref, leave_ref, table_ref, field_ref, spread_ref, *refs):
    *adds, out_ref = refs
    row_refs = (field_ref, spread_ref, enter_ref, leave_ref, table_ref)
    for u in range(PRODUCT_STEP):
        step = start + pl.program_id(0) * PRODUCT_STEP + u
        value = one_product(where_ref, row_refs, sizes, turn, step, u)
        for ref in adds:
            value = value + ref[u].astype(F32)
        out_ref[u] = value.astype(BF16)


def here_kernel(sizes, first_part, where_ref, enter_ref, leave_ref, table_ref, field_ref, spread_ref, got0_ref, got1_ref, out_ref):
    in_first = pl.program_id(0) * PRODUCT_STEP < first_part
    row_refs = (field_ref, spread_ref, enter_ref, leave_ref, table_ref)
    for u in range(PRODUCT_STEP):
        step = pl.program_id(0) * PRODUCT_STEP + u
        value = one_product(where_ref, row_refs, sizes, 0, step, u)
        out_ref[u] = value + jnp.where(in_first, got0_ref[u], got1_ref[u]).astype(F32)


def whole(shape):
    return pl.BlockSpec(shape, lambda *_: (0,) * len(shape))


def call(
    kernel, name, inputs, in_specs, outputs, out_specs, scratch=(), grid=(1,), cost=None, after=(), vmem=VMEM_LIMIT, aliases=None
):
    count = len(inputs)

    def ordered(*refs):
        return kernel(*refs[:count], *refs[count + len(after) :])

    inputs = (*inputs, *after)
    in_specs = [*in_specs, *([pl.BlockSpec(memory_space=pl.ANY)] * len(after))]
    return pl.pallas_call(
        ordered,
        out_shape=outputs,
        grid_spec=pltpu.PrefetchScalarGridSpec(
            num_scalar_prefetch=1,
            grid=grid,
            in_specs=in_specs,
            out_specs=out_specs,
            scratch_shapes=list(scratch),
        ),
        input_output_aliases=aliases or {},
        compiler_params=pltpu.CompilerParams(vmem_limit_bytes=vmem),
        cost_estimate=cost,
        name=name,
    )(*inputs)


def cost(flops, data):
    return pl.CostEstimate(flops=flops, bytes_accessed=data, transcendentals=0)


def triangle_table():
    at = np.arange(LANES)
    table = np.zeros((2 * LANES, 2 * LANES), np.float32)
    table[:LANES, :LANES] = at[:, None] <= at[None, :]
    table[LANES:, LANES:] = at[:, None] > at[None, :]
    return jnp.asarray(table, BF16)


def ring(axis, shift):
    count = lax.axis_size(axis)
    return [(i, (i + shift) % count) for i in range(count)]


def per_device(control, perturbation, slab_levels, member_group, band_width, zonal_rate, meridional_rate):
    _, levels, rows, cols = control.shape
    quarters, lat_count, lon_count = (lax.axis_size(a) for a in ("mem", "lat", "lon"))
    per_quarter = levels // quarters
    here = jnp.stack([lax.axis_index(a) for a in ("mem", "lat", "lon")]).astype(jnp.int32)
    where = jnp.concatenate([here, member_group, band_width, slab_levels])
    sds = jax.ShapeDtypeStruct
    table = sds((rows, levels), F32)
    table_spec = pl.BlockSpec((ROW_GROUP, levels), lambda g, _: (g, 0))

    column, decay, gain, end, *sends = call(
        functools.partial(column_kernel, (levels, rows, cols, quarters, lat_count)),
        "vertical_columns",
        (where, control, zonal_rate),
        [
            pl.BlockSpec((1, levels, ROW_GROUP, cols), lambda g, _: (0, 0, g, 0)),
            pl.BlockSpec(memory_space=pltpu.HBM),
        ],
        (sds((levels, rows, cols), BF16), table, table, table, table, table, table),
        (
            pl.BlockSpec((levels, ROW_GROUP, cols), lambda g, _: (0, g, 0)),
            whole((rows, levels)), whole((rows, levels)),
            table_spec, table_spec, table_spec, table_spec,
        ),
        scratch=[
            pltpu.VMEM((levels * 8, levels * 8), BF16),
            pltpu.VMEM((rows, levels), F32),
            pltpu.VMEM((2, levels, ROW_GROUP, LANES), F32),
            pltpu.VMEM(zonal_rate.shape, F32),
            pltpu.SemaphoreType.DMA,
        ],
        grid=(rows // ROW_GROUP,),
        cost=cost(2 * 512 * 512 * 384 * 12, 2 * levels * rows * cols * 2),
        vmem=COLUMN_VMEM_LIMIT,
    )
    got = [lax.ppermute(s, "lat", ring("lat", i + 1)) for i, s in enumerate(sends)]
    left, left_sum, right, right_sum, chain = call(
        functools.partial(row_kernel, (levels, rows, quarters, lon_count)),
        "row_terms",
        (where, meridional_rate),
        [whole(meridional_rate.shape)],
        (table, table, sds((levels, LANES), F32), sds((levels, LANES), F32), sds((levels, LANES), F32)),
        (
            whole((rows, levels)), whole((rows, levels)),
            whole((levels, LANES)), whole((levels, LANES)), whole((levels, LANES)),
        ),
        cost=cost(2 * 3 * 64 * 768 * 768 * 2, 1 << 20),
    )

    triangle = triangle_table()
    scale = 1.0 / math.sqrt(control.shape[0] * quarters - 1)
    plane = rows * cols
    table_wide = sds((rows, 2 * levels), F32)
    table_specs = [whole((rows, levels))] * 2
    to_partner = [(i, i ^ 1) for i in range(lon_count)]
    to_pair = lambda k: [(i, (i + 2 * k) % lon_count) for i in range(lon_count)]
    up, down = ring("mem", 1), ring("mem", -1)
    by_step = lambda offset, low=0, high=levels: pl.BlockSpec(
        (PRODUCT_STEP, rows, cols), lambda g, _: (jnp.clip(g - offset, low, high), 0, 0)
    )
    ends = np.cumsum([sum(parts) for parts in CHUNKS])

    def quarter_specs(c, turn, start):
        steps, begin = sum(CHUNKS[c]), int(ends[c]) - sum(CHUNKS[c])
        at = lambda g, w, wide, off: (
            lax.rem(w[0] + turn, quarters) * (wide // PRODUCT_STEP) + (off + start) // PRODUCT_STEP + g
        )
        return [
            pl.BlockSpec((PRODUCT_STEP, rows, cols), lambda g, w: (at(g, w, steps, 0), 0, 0)),
            pl.BlockSpec(
                (1, PRODUCT_STEP, rows, cols), lambda g, w: (0, at(g, w, per_quarter, begin), 0, 0)
            ),
        ]

    def edge_specs(steps):
        row = whole((steps * quarters, cols))
        return [row, row, whole(table_wide.shape)]

    def product_sizes(c):
        steps = sum(CHUNKS[c])
        return (int(ends[c]) - steps) * quarters, steps, quarters

    def send(c, turn, part, adds=(), after=()):
        field, enter, leave, lanes = states[c]
        start, count = part * CHUNKS[c][0], CHUNKS[c][part]
        (piece,) = call(
            functools.partial(send_kernel, product_sizes(c), turn, start),
            f"products_{turn}",
            (where, enter, leave, lanes, field, perturbation, *adds),
            edge_specs(sum(CHUNKS[c])) + quarter_specs(c, turn, start) + [by_step(0)] * len(adds),
            (sds((count, rows, cols), BF16),),
            (by_step(0),),
            grid=(count // PRODUCT_STEP,),
            cost=cost(count * plane * 8, count * plane * 8),
            after=after,
        )
        return piece

    def finish(c, two, one, after=()):
        sum_up = send(c, 1, 0, (two[0],), after)
        moved_up = lax.ppermute(sum_up, "mem", up)
        sum_down = send(c, 3, 1, (two[1],), (sum_up, *after))
        moved_down = lax.ppermute(sum_down, "mem", down)
        steps, first = sum(CHUNKS[c]), CHUNKS[c][0] // PRODUCT_STEP
        halves = [by_step(0, 0, first - 1), by_step(first, 0)]
        field, enter, leave, lanes = states[c]
        own = sds((steps, rows, cols), F32)
        here = call(
            functools.partial(here_kernel, product_sizes(c), CHUNKS[c][0]),
            "products_here",
            (where, enter, leave, lanes, field, perturbation, one[1], one[0]),
            edge_specs(steps) + quarter_specs(c, 0, 0) + halves,
            own,
            by_step(0),
            grid=(steps // PRODUCT_STEP,),
            cost=cost(steps * plane * 8, steps * plane * 14),
            after=(sum_down,),
        )
        moved = jnp.concatenate([moved_up, moved_down]).astype(F32)
        return (here + moved) * scale

    states, increments = [], []
    for c, parts in enumerate(CHUNKS):
        steps = sum(parts)
        in_chunk, first_place = steps * quarters, (int(ends[c]) - steps) * quarters
        places = slice(first_place, first_place + in_chunk)
        edge_spec, row_spec = whole((2, in_chunk, cols)), whole((in_chunk, cols))
        edge_row = sds((in_chunk, cols), F32)
        block = first_place // FIELD_STEP
        by_place = pl.BlockSpec((FIELD_STEP, LANES), lambda g, _, block=block: (block + g, 0))
        fields, edge, edge_send = call(
            functools.partial(field_kernel, (rows, cols, first_place, FIELD_STEP, lat_count)),
            "zonal_rows",
            (where, column, decay, gain, end, *got, right, right_sum, chain, triangle),
            [pl.BlockSpec((FIELD_STEP, rows, cols), lambda g, _, block=block: (block + g, 0, 0))]
            + [whole((rows, levels))] * 6
            + [by_place, by_place, by_place, whole(triangle.shape)],
            (sds((in_chunk, 2 * LANES, cols), BF16), sds((2, in_chunk, cols), F32), sds((2, in_chunk, cols), BF16)),
            (pl.BlockSpec((FIELD_STEP, 2 * LANES, cols), lambda g, _: (g, 0, 0)), edge_spec, edge_spec),
            scratch=[
                pltpu.VMEM((2, rows, 2 * levels), F32),
                pltpu.VMEM((FIELD_STEP, 3, rows, LANES), F32),
                pltpu.VMEM((FIELD_STEP, 2, rows, LANES), F32),
                pltpu.VMEM((FIELD_STEP * rows * cols // LANES, 2 * LANES), BF16),
                pltpu.VMEM((FIELD_STEP * rows * cols // LANES, 2 * LANES), F32),
            ],
            grid=(in_chunk // FIELD_STEP,),
            cost=cost(in_chunk * plane * 2 * 1024 * 3, in_chunk * plane * 6),
            vmem=FIELD_VMEM_LIMIT,
        )
        def filter_rows(first, count, before, after=()):
            blocks = steps // FIELD_STEP
            number = lambda g, w: turn_block(w, first + g, quarters, blocks)
            level_rows = pl.BlockSpec((FIELD_STEP, LANES), lambda g, w: (number(g, w), 0))
            step_of = lambda height: pl.BlockSpec(
                (FIELD_STEP, height, cols), lambda g, w: (number(g, w), 0, 0)
            )
            extra = () if before is None else (before,)
            return call(
                row_kernel_of(rows, first, quarters, blocks),
                "row_filter",
                (where, fields, left, left_sum, right, right_sum, *extra),
                [step_of(2 * LANES), *table_specs, level_rows, level_rows]
                + [pl.BlockSpec(memory_space=pl.ANY)] * len(extra),
                sds((in_chunk, rows, cols), F32),
                step_of(rows),
                scratch=[
                    pltpu.VMEM((rows, 2 * levels), F32),
                    pltpu.VMEM((FIELD_STEP, 2 * rows, 2 * LANES), BF16),
                ],
                grid=(count,),
                cost=cost(count * FIELD_STEP * plane * 512, count * FIELD_STEP * plane * 8),
                after=after,
                aliases={6: 0} if extra else None,
            )

        partner = lax.ppermute(edge_send, "lon", to_partner)
        field = filter_rows(0, 2, None)
        pair_sends = call(
            functools.partial(pair_kernel, pairs=lon_count // 2, places=places),
            "pair_ends",
            (where, edge, partner, chain),
            [edge_spec, edge_spec, whole((levels, LANES))],
            (sds((in_chunk, cols), BF16),) * 3,
            (row_spec,) * 3,
            after=(field,),
        )
        field = filter_rows(2, 2, field, after=(pair_sends[0],))
        pair_got = [lax.ppermute(p, "lon", to_pair(k + 1)) for k, p in enumerate(pair_sends)]
        count = parts[0]
        two_up, two_down, enter, leave, lanes = call(
            functools.partial(first_send_kernel, product_sizes(c), 2, places),
            "products_2",
            (where, edge, partner, *pair_got, chain, left, left_sum, *((field, perturbation) * 2)),
            [edge_spec, edge_spec, row_spec, row_spec, row_spec, whole((levels, LANES)), *table_specs]
            + quarter_specs(c, 2, 0)
            + quarter_specs(c, 2, count),
            (sds((count, rows, cols), BF16),) * 2 + (edge_row, edge_row, table_wide),
            (by_step(0), by_step(0), row_spec, row_spec, whole(table_wide.shape)),
            grid=(count // PRODUCT_STEP,),
            cost=cost(count * plane * 8, count * plane * 8),
        )
        states.append((field, enter, leave, lanes))
        two_up_moved = lax.ppermute(two_up, "mem", up)
        two = two_up_moved, lax.ppermute(two_down, "mem", down)
        one_up = send(c, 1, 1, after=(two_down,))
        one_up_moved = lax.ppermute(one_up, "mem", up)
        field = filter_rows(4, 2, field, after=(one_up,))
        states[c] = (field, enter, leave, lanes)
        one_down = send(c, 3, 0)
        one = one_up_moved, lax.ppermute(one_down, "mem", down)
        field = filter_rows(6, 2, field, after=(one_down,))
        states[c] = (field, enter, leave, lanes)
        increments.append(finish(c, two, one))
    return increments[0] if len(increments) == 1 else jnp.concatenate(increments)


def solution(mesh):
    return jax.shard_map(
        per_device,
        mesh=mesh,
        in_specs=(
            P("mem", None, "lon", "lat"),
            P("mem", None, "lon", "lat"),
            P(),
            P("mem"),
            P(),
            P(),
            P(),
        ),
        out_specs=P("mem", "lon", "lat"),
        check_vma=False,
    )
```

```python
import functools
import math

import jax
import jax.numpy as jnp
import numpy as np
from jax import lax
from jax.experimental import pallas as pl
from jax.experimental.pallas import tpu as pltpu
from jax.sharding import PartitionSpec as P

CHUNKS = ((8, 8),)
LANES = 128
GROUP_AT = 3
BAND_AT = 4
SLAB_AT = 8
ROW_GROUP = 32
FIELD_STEP = 8
PRODUCT_STEP = 4
VMEM_LIMIT = 8 * 1024 * 1024
COLUMN_VMEM_LIMIT = 48 * 1024 * 1024
FIELD_VMEM_LIMIT = 16 * 1024 * 1024

F32 = jnp.float32
BF16 = jnp.bfloat16


def iota(shape, axis):
    return lax.broadcasted_iota(jnp.int32, shape, axis)


def log_decay(rate):
    t = rate / (2.0 - rate)
    s = t * t
    series = 1.0 + s * (1 / 3 + s * (1 / 5 + s * (1 / 7 + s * (1 / 9 + s * (1 / 11 + s / 13)))))
    return -2.0 * t * series


def split3(x):
    hi = x.astype(BF16)
    rest = x - hi.astype(F32)
    mid = rest.astype(BF16)
    return hi, mid, (rest - mid.astype(F32)).astype(BF16)


def split2(x):
    hi = x.astype(BF16)
    return hi, (x - hi.astype(F32)).astype(BF16)


def dot_nn(a, b):
    return lax.dot_general(a, b, (((1,), (0,)), ((), ())), preferred_element_type=F32)


def dot_nt(a, b):
    return lax.dot_general(a, b, (((1,), (1,)), ((), ())), preferred_element_type=F32)


def times_exact(x, zero_one):
    rows = x.shape[0]
    product = dot_nn(jnp.concatenate(split3(x), axis=0), zero_one)
    return product[:rows] + product[rows : 2 * rows] + product[2 * rows :]


def exact_times_t(zero_one, x):
    return sum(dot_nt(zero_one, part) for part in split3(x))


def traced_level(place, levels, quarters):
    level = jnp.zeros_like(place)
    first, begin = 0, 0
    for parts in CHUNKS:
        steps = sum(parts)
        rest = place - first
        quarter = sum((rest >= k * steps).astype(jnp.int32) for k in range(1, quarters))
        here = quarter * (levels // quarters - steps) + rest + begin
        level = jnp.where(rest >= 0, here, level)
        first, begin = first + steps * quarters, begin + steps
    return level


def rates_by_place(slab_levels, rates, levels, quarters):
    slabs = rates.shape[0]
    level = traced_level(iota((levels, slabs), 0), levels, quarters)
    index = jnp.zeros((levels, slabs), jnp.int32)
    end = jnp.int32(0)
    for s in range(slabs):
        end = end + slab_levels[SLAB_AT + s]
        index = index + (level >= end).astype(jnp.int32)
    chosen = (index == iota((levels, slabs), 1)).astype(F32).astype(BF16)
    return sum(dot_nn(chosen, part) for part in split3(rates))


def lane_of(table, lane):
    return jnp.take_along_axis(table, jnp.full(table.shape, lane, jnp.int32), axis=1)


def column_kernel(
    sizes, where_ref, control_ref, rate_hbm,
    column_ref, decay_ref, gain_ref, end_ref, send1_ref, send2_ref, send3_ref,
    kron, decay_all, weighted, rate_ref, arrived,
):
    levels, rows, cols, quarters, lat_count = sizes
    step = pl.program_id(0)
    lat, lon = where_ref[1], where_ref[2]
    full = levels * 8

    @pl.when(step == 0)
    def _():
        fetch = pltpu.make_async_copy(rate_hbm, rate_ref, arrived)
        fetch.start()
        band = where_ref[BAND_AT + where_ref[GROUP_AT]].astype(F32)
        out_level = traced_level(jnp.right_shift(iota((full, full), 0), 3), levels, quarters)
        spacing = out_level - jnp.right_shift(iota((full, full), 1), 3)
        same = jnp.bitwise_and(iota((full, full), 0), 7) == jnp.bitwise_and(iota((full, full), 1), 7)
        ratio = spacing.astype(F32) / band
        weight = jnp.exp(-2.0 * (ratio * ratio))
        keep = jnp.logical_and(same, jnp.abs(spacing).astype(F32) <= band)
        kron[...] = jnp.where(keep, weight, 0.0).astype(BF16)
        fetch.wait()
        level_rates = rates_by_place(where_ref, rate_ref[...], levels, quarters)
        own = iota((rows, rate_ref.shape[1]), 1) == lon * rows + iota((rows, rate_ref.shape[1]), 0)
        rate = exact_times_t(own.astype(F32).astype(BF16), level_rates)
        remain = 1.0 - rate
        decay_all[...] = log_decay(rate)
        decay_ref[...] = decay_all[...]
        gain_ref[...] = jnp.sqrt(rate * (2.0 - rate) / (1.0 + remain * remain))

    block = control_ref[0].astype(F32)
    halves = []
    for half in range(ROW_GROUP // 8):
        part = block[:, 8 * half : 8 * half + 8, :].reshape(full, cols).astype(BF16)
        halves.append(dot_nn(kron[...], part).reshape(levels, 8, cols))
    column = jnp.concatenate(halves, axis=1).astype(BF16)
    column_ref[...] = column

    log_a = decay_all[pl.ds(step * ROW_GROUP, ROW_GROUP), :]
    lane = iota((ROW_GROUP, LANES), 1).astype(F32)
    blocks = cols // LANES
    for place in range(levels):
        log_b = jnp.broadcast_to(log_a[:, place : place + 1], (ROW_GROUP, LANES))
        over = jnp.exp(log_b * float(LANES))
        x = column_ref[place].astype(F32)
        parts = [x[:, LANES * b : LANES * (b + 1)] for b in range(blocks)]
        along, against = parts[0], parts[-1]
        for b in range(1, blocks):
            along = parts[b] + over * along
            against = parts[-1 - b] + over * against
        weighted[0, place] = along * jnp.exp(log_b * (LANES - 1.0 - lane))
        weighted[1, place] = against * jnp.exp(log_b * lane)
    place_lane = iota((ROW_GROUP, levels), 1)
    forward = jnp.zeros((ROW_GROUP, levels), F32)
    backward = jnp.zeros((ROW_GROUP, levels), F32)
    for place in range(levels):
        along = jnp.sum(weighted[0, place], axis=1, keepdims=True)
        against = jnp.sum(weighted[1, place], axis=1, keepdims=True)
        forward = jnp.where(place_lane == place, along, forward)
        backward = jnp.where(place_lane == place, against, backward)
    power = (1 + cols * (2 * (lat_count - 1 - lat) + 1)).astype(F32)
    returning = backward - jnp.exp(log_a * power) * forward
    end_ref[...] = forward
    for shift, ref in ((1, send1_ref), (2, send2_ref), (3, send3_ref)):
        ref[...] = jnp.where(lat + shift < lat_count, forward, returning)


def row_kernel(
    sizes, where_ref, rate_ref,
    left_ref, left_sum_ref, right_ref, right_sum_ref, chain_ref,
):
    levels, rows, quarters, lon_count = sizes
    lon = where_ref[2]
    total = rate_ref.shape[1]
    rate = rates_by_place(where_ref, rate_ref[...], levels, quarters)
    remain = 1.0 - rate
    root = jnp.sqrt(rate * (2.0 - rate))
    gain = root * jnp.sqrt(root) / jnp.sqrt(jnp.sqrt(1.0 + remain * remain))
    log_c = log_decay(rate)
    owner = lambda at: jnp.right_shift(at * ((1 << 16) // rows + 1), 16)
    first, second = iota((total, total), 0), iota((total, total), 1)
    same = owner(first) == owner(second)
    upper = jnp.logical_and(same, first <= second).astype(F32).astype(BF16)
    lower = jnp.logical_and(same, first >= second).astype(F32).astype(BF16)
    running = times_exact(log_c, upper)
    before = running - log_c
    weight = gain * jnp.exp(running + before)
    sums = times_exact(weight, lower)
    left = jnp.exp(-before)
    right = gain * jnp.exp(-running)
    own = (iota((rows, total), 1) == lon * rows + iota((rows, total), 0)).astype(F32).astype(BF16)
    own_t = iota((total, LANES), 0) == lon * rows + iota((total, LANES), 1)
    own_t = jnp.logical_and(own_t, iota((total, LANES), 1) < rows).astype(F32).astype(BF16)
    left_ref[...] = exact_times_t(own, left)
    left_sum_ref[...] = exact_times_t(own, left * sums)
    right_ref[...] = times_exact(right, own_t)
    right_sum_ref[...] = times_exact(right * sums, own_t)

    inside = (owner(iota((total, LANES), 0)) == iota((total, LANES), 1)).astype(F32).astype(BF16)
    log_over = times_exact(log_c, inside)
    bounce = times_exact(weight, inside)
    source, target = iota((LANES, LANES), 0), iota((LANES, LANES), 1)
    between = jnp.logical_and(source > lon, source < target).astype(F32).astype(BF16)
    device = iota((levels, LANES), 1)
    beyond = jnp.logical_and(device > lon, device < lon_count)
    echo = jnp.sum(
        jnp.where(beyond, bounce * jnp.exp(2.0 * times_exact(log_over, between)), 0.0),
        axis=1,
        keepdims=True,
    )
    every = jnp.exp(log_over)
    over = jnp.sum(jnp.where(device == lon, every, 0.0), axis=1, keepdims=True)
    partner = jnp.bitwise_xor(lon, 1)
    partner_over = jnp.sum(jnp.where(device == partner, every, 0.0), axis=1, keepdims=True)
    pair, pairs = jnp.right_shift(lon, 1), lon_count // 2
    shift = jnp.bitwise_and(target, 63)
    is_before = pair >= shift
    low = jnp.where(is_before, 2 * (pair - shift) + 1, lon)
    high = jnp.where(is_before, lon, 2 * (pair - shift + pairs))
    path = jnp.logical_and(source > low, source < high).astype(F32).astype(BF16)
    reach = jnp.exp(times_exact(log_over, path))
    shift = jnp.bitwise_and(device, 63)
    counted = jnp.logical_and(shift >= 1, shift < pairs)
    counted = jnp.logical_and(counted, (pair >= shift) == (device < 64))
    chain = jnp.where(counted, reach, 0.0)
    for at, value in ((32, over), (33, echo), (34, partner_over)):
        chain = jnp.where(device == at, value, chain)
    chain_ref[...] = chain


def field_kernel(
    sizes, where_ref, column_ref, decay_ref, gain_ref, end_ref, got1_ref, got2_ref, got3_ref,
    right_ref, right_sum_ref, chain_ref, triangle_ref,
    fields, edge_ref, edge_send_ref, tables, powers, enters, scaled, sums,
):
    rows, cols, first_place, per_step, lat_count = sizes
    step = pl.program_id(0)
    lat = where_ref[1]
    blocks = cols // LANES

    @pl.when(step == 0)
    def _():
        log_a, gain = decay_ref[...], gain_ref[...]
        enter_left = jnp.zeros(log_a.shape, F32)
        enter_right = jnp.zeros(log_a.shape, F32)
        for shift, ref in ((1, got1_ref), (2, got2_ref), (3, got3_ref)):
            got = ref[...]
            is_left = lat >= shift
            power = jnp.where(is_left, shift - 1, lat_count - 1 - shift) * cols
            scaled = jnp.exp(log_a * power.astype(F32)) * got
            enter_left = enter_left + jnp.where(is_left, scaled, 0.0)
            enter_right = enter_right + jnp.where(is_left, 0.0, scaled)
        leaving = end_ref[...] + jnp.exp(log_a * float(cols)) * enter_left
        power = (1 + 2 * cols * (lat_count - 1 - lat)).astype(F32)
        enter_right = enter_right - jnp.exp(log_a * power) * leaving
        enter_left = gain * jnp.exp(log_a) * enter_left
        enter_right = gain * jnp.exp(log_a * float(LANES)) * enter_right
        tables[0] = jnp.concatenate([log_a, gain], axis=1)
        tables[1] = jnp.concatenate([enter_left, enter_right], axis=1)

    half = tables.shape[2] // 2
    lane = iota((rows, LANES), 1).astype(F32)
    row_number = iota((16, LANES), 0)
    tall = blocks * rows
    place_of = lambda u: first_place + step * per_step + u
    for u in range(per_step):
        log_a = lane_of(tables[0], place_of(u))
        gain = lane_of(tables[0], place_of(u) + half)
        enters[u, 0] = lane_of(tables[1], place_of(u))
        enters[u, 1] = lane_of(tables[1], place_of(u) + half)
        grow = jnp.exp(log_a * lane)
        shrink = jnp.exp(log_a * (-lane))
        powers[u, 0] = grow
        powers[u, 1] = shrink
        powers[u, 2] = jnp.exp(log_a * float(LANES))
        gain_grow, gain_shrink = gain * grow, gain * shrink
        x = column_ref[u].astype(F32)
        for b in range(blocks):
            part = x[:, LANES * b : LANES * (b + 1)]
            rows_at = slice(u * tall + b * rows, u * tall + (b + 1) * rows)
            for side, factor in enumerate((gain_shrink, gain_grow)):
                scaled[rows_at, LANES * side : LANES * (side + 1)] = (part * factor).astype(BF16)
    for u in range(per_step):
        at = slice(u * tall, (u + 1) * tall)
        sums[at, :] = dot_nn(scaled[at, :], triangle_ref[...])
    for u in range(per_step):
        grow, shrink, over = (powers[u, k] for k in range(3))
        at = lambda b: slice(u * tall + b * rows, u * tall + (b + 1) * rows)
        ahead = [sums[at(b), :LANES] for b in range(blocks)]
        behind = [sums[at(b), LANES:] for b in range(blocks)]
        lefts, rights_in = [enters[u, 0]], [enters[u, 1]]
        for b in range(blocks - 1):
            end = jnp.broadcast_to(ahead[b][:, LANES - 1 :], (rows, LANES))
            lefts.append(over * (lefts[-1] + end))
        for b in range(blocks - 1, 0, -1):
            first = scaled[at(b), LANES:].astype(F32) + behind[b]
            end = jnp.broadcast_to(first[:, :1], (rows, LANES))
            rights_in.append(over * (rights_in[-1] + end))
        rights_in = rights_in[::-1]
        for b in range(blocks):
            field = grow * (ahead[b] + lefts[b]) + shrink * (behind[b] + rights_in[b])
            high, low = split2(field)
            fields[u, :rows, LANES * b : LANES * (b + 1)] = high
            fields[u, LANES : LANES + rows, LANES * b : LANES * (b + 1)] = low
        nothing = jnp.zeros((LANES - rows, cols), BF16)
        fields[u, rows:LANES, :] = nothing
        fields[u, LANES + rows :, :] = nothing
    for u in range(per_step):
        ends = [split2(ref[u : u + 1, :]) for ref in (right_ref, right_sum_ref)]
        first = jnp.zeros((16, LANES), F32)
        for at, part in enumerate((ends[0][0], ends[1][0], ends[0][1], ends[1][1])):
            first = jnp.where(row_number == at, part.astype(F32), first)
        second = jnp.where(row_number < 2, first, 0.0)
        result = dot_nn(jnp.concatenate([first, second], axis=1).astype(BF16), fields[u])
        row = step * per_step + u
        chain_row = chain_ref[u : u + 1, :]
        over_rows, echo = chain_row[:, 32:33], chain_row[:, 33:34]
        end = over_rows * (result[0:1] + result[2:3])
        edge_ref[0, pl.ds(row, 1), :] = end
        edge_ref[1, pl.ds(row, 1), :] = result[1:2] + result[3:4] + over_rows * echo * end

    @pl.when(step == pl.num_programs(0) - 1)
    def _():
        edge_send_ref[...] = edge_ref[...].astype(BF16)


def turn_block(scalars, number, quarters, blocks):
    turn = number // blocks
    turn = jnp.where(turn == 0, 2, jnp.where(turn == 1, 1, jnp.where(turn == 2, 3, 0)))
    return lax.rem(scalars[0] + turn, quarters) * blocks + lax.rem(number, blocks)


def row_kernel_of(rows, first, quarters, blocks):
    def kernel(where_ref, fields_ref, left_ref, left_sum_ref, right_ref, right_sum_ref, *rest):
        field_ref, table, matrices = rest[-3:]
        step, per_step = pl.program_id(0), fields_ref.shape[0]
        half = table.shape[1] // 2
        below = iota((rows, LANES), 0) >= iota((rows, LANES), 1)

        @pl.when(step == 0)
        def _():
            table[...] = jnp.concatenate([left_ref[...], left_sum_ref[...]], axis=1)
            matrices[...] = jnp.zeros_like(matrices)

        for u in range(per_step):
            place = turn_block(where_ref, first + step, quarters, blocks) * per_step + u
            left, left_sum = lane_of(table[...], place), lane_of(table[...], place + half)
            right, right_sum = right_ref[u : u + 1, :], right_sum_ref[u : u + 1, :]
            high, low = split2(jnp.where(below, left_sum * right, left * right_sum))
            matrices[u, :rows, :LANES] = high
            matrices[u, :rows, LANES:] = high
            matrices[u, rows:, :LANES] = low
        for u in range(per_step):
            result = dot_nn(matrices[u], fields_ref[u])
            field_ref[u] = result[:rows] + result[rows:]

    return kernel


def pair_kernel(where_ref, own_ref, got_ref, chain_ref, send1_ref, send2_ref, send3_ref, *, pairs, places):
    lon = where_ref[2]
    second = jnp.bitwise_and(lon, 1) == 1
    pair = jnp.right_shift(lon, 1)
    chain = chain_ref[places, :]
    over, partner_over = chain[:, 32:33], chain[:, 34:35]
    end, returning = own_ref[0], own_ref[1]
    got_end, got_returning = got_ref[0].astype(F32), got_ref[1].astype(F32)
    pair_end = jnp.where(second, end + over * got_end, got_end + partner_over * end)
    pair_returning = jnp.where(
        second, got_returning + partner_over * returning, returning + over * got_returning
    )
    for shift, ref in ((1, send1_ref), (2, send2_ref), (3, send3_ref)):
        ref[...] = jnp.where(pair + shift < pairs, pair_end, pair_returning).astype(BF16)


def first_send_kernel(
    sizes, turn, places, where_ref, own_ref, got_ref, got1_ref, got2_ref, got3_ref, chain_ref, left_ref, left_sum_ref,
    field0_ref, spread0_ref, field1_ref, spread1_ref, out0_ref, out1_ref, enter_ref, leave_ref, table_ref,
):
    @pl.when(pl.program_id(0) == 0)
    def _():
        second = jnp.bitwise_and(where_ref[2], 1) == 1
        chain = chain_ref[places, :]
        over, echo = chain[:, 32:33], chain[:, 33:34]
        enter = jnp.where(second, got_ref[0].astype(F32), 0.0)
        leave = jnp.where(second, 0.0, got_ref[1].astype(F32))
        for shift, ref in ((1, got1_ref), (2, got2_ref), (3, got3_ref)):
            got = ref[...].astype(F32)
            enter = enter + chain[:, shift : shift + 1] * got
            leave = leave + chain[:, 64 + shift : 65 + shift] * got
        enter_ref[...] = enter
        leave_ref[...] = over * (leave + echo * (own_ref[0] + over * enter))
        table_ref[...] = jnp.concatenate([left_ref[...], left_sum_ref[...]], axis=1)

    state = (where_ref, enter_ref, leave_ref, table_ref)
    send_kernel(sizes, turn, 0, *state, field0_ref, spread0_ref, out0_ref)
    send_kernel(sizes, turn, sizes[1] // 2, *state, field1_ref, spread1_ref, out1_ref)


def one_product(where_ref, refs, sizes, turn, step, u):
    field_ref, spread_ref, enter_ref, leave_ref, table_ref = refs
    first_place, steps, quarters = sizes
    cols = field_ref.shape[-1]
    row = lax.rem(where_ref[0] + turn, quarters) * steps + step
    place = first_place + row
    half = table_ref.shape[1] // 2
    wide = lambda lane: jnp.concatenate([lane_of(table_ref[...], lane)] * (cols // LANES), axis=1)
    enter, leave = enter_ref[pl.ds(row, 1), :], leave_ref[pl.ds(row, 1), :]
    filtered = field_ref[u] + wide(place + half) * enter + wide(place) * leave
    return spread_ref[0, u].astype(F32) * filtered


def send_kernel(sizes, turn, start, where_ref, enter_ref, leave_ref, table_ref, field_ref, spread_ref, *refs):
    *adds, out_ref = refs
    row_refs = (field_ref, spread_ref, enter_ref, leave_ref, table_ref)
    for u in range(PRODUCT_STEP):
        step = start + pl.program_id(0) * PRODUCT_STEP + u
        value = one_product(where_ref, row_refs, sizes, turn, step, u)
        for ref in adds:
            value = value + ref[u].astype(F32)
        out_ref[u] = value.astype(BF16)


def here_kernel(sizes, first_part, where_ref, enter_ref, leave_ref, table_ref, field_ref, spread_ref, got0_ref, got1_ref, out_ref):
    in_first = pl.program_id(0) * PRODUCT_STEP < first_part
    row_refs = (field_ref, spread_ref, enter_ref, leave_ref, table_ref)
    for u in range(PRODUCT_STEP):
        step = pl.program_id(0) * PRODUCT_STEP + u
        value = one_product(where_ref, row_refs, sizes, 0, step, u)
        out_ref[u] = value + jnp.where(in_first, got0_ref[u], got1_ref[u]).astype(F32)


def whole(shape):
    return pl.BlockSpec(shape, lambda *_: (0,) * len(shape))


def call(
    kernel, name, inputs, in_specs, outputs, out_specs, scratch=(), grid=(1,), cost=None, after=(), vmem=VMEM_LIMIT, aliases=None
):
    count = len(inputs)

    def ordered(*refs):
        return kernel(*refs[:count], *refs[count + len(after) :])

    inputs = (*inputs, *after)
    in_specs = [*in_specs, *([pl.BlockSpec(memory_space=pl.ANY)] * len(after))]
    return pl.pallas_call(
        ordered,
        out_shape=outputs,
        grid_spec=pltpu.PrefetchScalarGridSpec(
            num_scalar_prefetch=1,
            grid=grid,
            in_specs=in_specs,
            out_specs=out_specs,
            scratch_shapes=list(scratch),
        ),
        input_output_aliases=aliases or {},
        compiler_params=pltpu.CompilerParams(vmem_limit_bytes=vmem),
        cost_estimate=cost,
        name=name,
    )(*inputs)


def cost(flops, data):
    return pl.CostEstimate(flops=flops, bytes_accessed=data, transcendentals=0)


def triangle_table():
    at = np.arange(LANES)
    table = np.zeros((2 * LANES, 2 * LANES), np.float32)
    table[:LANES, :LANES] = at[:, None] <= at[None, :]
    table[LANES:, LANES:] = at[:, None] > at[None, :]
    return jnp.asarray(table, BF16)


def ring(axis, shift):
    count = lax.axis_size(axis)
    return [(i, (i + shift) % count) for i in range(count)]


def per_device(control, perturbation, slab_levels, member_group, band_width, zonal_rate, meridional_rate):
    _, levels, rows, cols = control.shape
    quarters, lat_count, lon_count = (lax.axis_size(a) for a in ("mem", "lat", "lon"))
    per_quarter = levels // quarters
    here = jnp.stack([lax.axis_index(a) for a in ("mem", "lat", "lon")]).astype(jnp.int32)
    where = jnp.concatenate([here, member_group, band_width, slab_levels])
    sds = jax.ShapeDtypeStruct
    table = sds((rows, levels), F32)
    table_spec = pl.BlockSpec((ROW_GROUP, levels), lambda g, _: (g, 0))

    column, decay, gain, end, *sends = call(
        functools.partial(column_kernel, (levels, rows, cols, quarters, lat_count)),
        "vertical_columns",
        (where, control, zonal_rate),
        [
            pl.BlockSpec((1, levels, ROW_GROUP, cols), lambda g, _: (0, 0, g, 0)),
            pl.BlockSpec(memory_space=pltpu.HBM),
        ],
        (sds((levels, rows, cols), BF16), table, table, table, table, table, table),
        (
            pl.BlockSpec((levels, ROW_GROUP, cols), lambda g, _: (0, g, 0)),
            whole((rows, levels)), whole((rows, levels)),
            table_spec, table_spec, table_spec, table_spec,
        ),
        scratch=[
            pltpu.VMEM((levels * 8, levels * 8), BF16),
            pltpu.VMEM((rows, levels), F32),
            pltpu.VMEM((2, levels, ROW_GROUP, LANES), F32),
            pltpu.VMEM(zonal_rate.shape, F32),
            pltpu.SemaphoreType.DMA,
        ],
        grid=(rows // ROW_GROUP,),
        cost=cost(2 * 512 * 512 * 384 * 12, 2 * levels * rows * cols * 2),
        vmem=COLUMN_VMEM_LIMIT,
    )
    got = [lax.ppermute(s, "lat", ring("lat", i + 1)) for i, s in enumerate(sends)]
    left, left_sum, right, right_sum, chain = call(
        functools.partial(row_kernel, (levels, rows, quarters, lon_count)),
        "row_terms",
        (where, meridional_rate),
        [whole(meridional_rate.shape)],
        (table, table, sds((levels, LANES), F32), sds((levels, LANES), F32), sds((levels, LANES), F32)),
        (
            whole((rows, levels)), whole((rows, levels)),
            whole((levels, LANES)), whole((levels, LANES)), whole((levels, LANES)),
        ),
        cost=cost(2 * 3 * 64 * 768 * 768 * 2, 1 << 20),
    )

    triangle = triangle_table()
    scale = 1.0 / math.sqrt(control.shape[0] * quarters - 1)
    plane = rows * cols
    table_wide = sds((rows, 2 * levels), F32)
    table_specs = [whole((rows, levels))] * 2
    to_partner = [(i, i ^ 1) for i in range(lon_count)]
    to_pair = lambda k: [(i, (i + 2 * k) % lon_count) for i in range(lon_count)]
    up, down = ring("mem", 1), ring("mem", -1)
    by_step = lambda offset, low=0, high=levels: pl.BlockSpec(
        (PRODUCT_STEP, rows, cols), lambda g, _: (jnp.clip(g - offset, low, high), 0, 0)
    )
    ends = np.cumsum([sum(parts) for parts in CHUNKS])

    def quarter_specs(c, turn, start):
        steps, begin = sum(CHUNKS[c]), int(ends[c]) - sum(CHUNKS[c])
        at = lambda g, w, wide, off: (
            lax.rem(w[0] + turn, quarters) * (wide // PRODUCT_STEP) + (off + start) // PRODUCT_STEP + g
        )
        return [
            pl.BlockSpec((PRODUCT_STEP, rows, cols), lambda g, w: (at(g, w, steps, 0), 0, 0)),
            pl.BlockSpec(
                (1, PRODUCT_STEP, rows, cols), lambda g, w: (0, at(g, w, per_quarter, begin), 0, 0)
            ),
        ]

    def edge_specs(steps):
        row = whole((steps * quarters, cols))
        return [row, row, whole(table_wide.shape)]

    def product_sizes(c):
        steps = sum(CHUNKS[c])
        return (int(ends[c]) - steps) * quarters, steps, quarters

    def send(c, turn, part, adds=(), after=()):
        field, enter, leave, lanes = states[c]
        start, count = part * CHUNKS[c][0], CHUNKS[c][part]
        (piece,) = call(
            functools.partial(send_kernel, product_sizes(c), turn, start),
            f"products_{turn}",
            (where, enter, leave, lanes, field, perturbation, *adds),
            edge_specs(sum(CHUNKS[c])) + quarter_specs(c, turn, start) + [by_step(0)] * len(adds),
            (sds((count, rows, cols), BF16),),
            (by_step(0),),
            grid=(count // PRODUCT_STEP,),
            cost=cost(count * plane * 8, count * plane * 8),
            after=after,
        )
        return piece

    def finish(c, two, one, after=()):
        sum_up = send(c, 1, 0, (two[0],), after)
        moved_up = lax.ppermute(sum_up, "mem", up)
        sum_down = send(c, 3, 1, (two[1],), (sum_up, *after))
        moved_down = lax.ppermute(sum_down, "mem", down)
        steps, first = sum(CHUNKS[c]), CHUNKS[c][0] // PRODUCT_STEP
        halves = [by_step(0, 0, first - 1), by_step(first, 0)]
        field, enter, leave, lanes = states[c]
        own = sds((steps, rows, cols), F32)
        here = call(
            functools.partial(here_kernel, product_sizes(c), CHUNKS[c][0]),
            "products_here",
            (where, enter, leave, lanes, field, perturbation, one[1], one[0]),
            edge_specs(steps) + quarter_specs(c, 0, 0) + halves,
            own,
            by_step(0),
            grid=(steps // PRODUCT_STEP,),
            cost=cost(steps * plane * 8, steps * plane * 14),
            after=(sum_down,),
        )
        moved = jnp.concatenate([moved_up, moved_down]).astype(F32)
        return (here + moved) * scale

    states, increments = [], []
    for c, parts in enumerate(CHUNKS):
        steps = sum(parts)
        in_chunk, first_place = steps * quarters, (int(ends[c]) - steps) * quarters
        places = slice(first_place, first_place + in_chunk)
        edge_spec, row_spec = whole((2, in_chunk, cols)), whole((in_chunk, cols))
        edge_row = sds((in_chunk, cols), F32)
        block = first_place // FIELD_STEP
        by_place = pl.BlockSpec((FIELD_STEP, LANES), lambda g, _, block=block: (block + g, 0))
        fields, edge, edge_send = call(
            functools.partial(field_kernel, (rows, cols, first_place, FIELD_STEP, lat_count)),
            "zonal_rows",
            (where, column, decay, gain, end, *got, right, right_sum, chain, triangle),
            [pl.BlockSpec((FIELD_STEP, rows, cols), lambda g, _, block=block: (block + g, 0, 0))]
            + [whole((rows, levels))] * 6
            + [by_place, by_place, by_place, whole(triangle.shape)],
            (sds((in_chunk, 2 * LANES, cols), BF16), sds((2, in_chunk, cols), F32), sds((2, in_chunk, cols), BF16)),
            (pl.BlockSpec((FIELD_STEP, 2 * LANES, cols), lambda g, _: (g, 0, 0)), edge_spec, edge_spec),
            scratch=[
                pltpu.VMEM((2, rows, 2 * levels), F32),
                pltpu.VMEM((FIELD_STEP, 3, rows, LANES), F32),
                pltpu.VMEM((FIELD_STEP, 2, rows, LANES), F32),
                pltpu.VMEM((FIELD_STEP * rows * cols // LANES, 2 * LANES), BF16),
                pltpu.VMEM((FIELD_STEP * rows * cols // LANES, 2 * LANES), F32),
            ],
            grid=(in_chunk // FIELD_STEP,),
            cost=cost(in_chunk * plane * 2 * 1024 * 3, in_chunk * plane * 6),
            vmem=FIELD_VMEM_LIMIT,
        )
        def filter_rows(first, count, before, after=()):
            blocks = steps // FIELD_STEP
            number = lambda g, w: turn_block(w, first + g, quarters, blocks)
            level_rows = pl.BlockSpec((FIELD_STEP, LANES), lambda g, w: (number(g, w), 0))
            step_of = lambda height: pl.BlockSpec(
                (FIELD_STEP, height, cols), lambda g, w: (number(g, w), 0, 0)
            )
            extra = () if before is None else (before,)
            return call(
                row_kernel_of(rows, first, quarters, blocks),
                "row_filter",
                (where, fields, left, left_sum, right, right_sum, *extra),
                [step_of(2 * LANES), *table_specs, level_rows, level_rows]
                + [pl.BlockSpec(memory_space=pl.ANY)] * len(extra),
                sds((in_chunk, rows, cols), F32),
                step_of(rows),
                scratch=[
                    pltpu.VMEM((rows, 2 * levels), F32),
                    pltpu.VMEM((FIELD_STEP, 2 * rows, 2 * LANES), BF16),
                ],
                grid=(count,),
                cost=cost(count * FIELD_STEP * plane * 512, count * FIELD_STEP * plane * 8),
                after=after,
                aliases={6: 0} if extra else None,
            )

        partner = lax.ppermute(edge_send, "lon", to_partner)
        field = filter_rows(0, 2, None)
        pair_sends = call(
            functools.partial(pair_kernel, pairs=lon_count // 2, places=places),
            "pair_ends",
            (where, edge, partner, chain),
            [edge_spec, edge_spec, whole((levels, LANES))],
            (sds((in_chunk, cols), BF16),) * 3,
            (row_spec,) * 3,
            after=(field,),
        )
        field = filter_rows(2, 4, field, after=(pair_sends[0],))
        pair_got = [lax.ppermute(p, "lon", to_pair(k + 1)) for k, p in enumerate(pair_sends)]
        count = parts[0]
        two_up, two_down, enter, leave, lanes = call(
            functools.partial(first_send_kernel, product_sizes(c), 2, places),
            "products_2",
            (where, edge, partner, *pair_got, chain, left, left_sum, *((field, perturbation) * 2)),
            [edge_spec, edge_spec, row_spec, row_spec, row_spec, whole((levels, LANES)), *table_specs]
            + quarter_specs(c, 2, 0)
            + quarter_specs(c, 2, count),
            (sds((count, rows, cols), BF16),) * 2 + (edge_row, edge_row, table_wide),
            (by_step(0), by_step(0), row_spec, row_spec, whole(table_wide.shape)),
            grid=(count // PRODUCT_STEP,),
            cost=cost(count * plane * 8, count * plane * 8),
        )
        states.append((field, enter, leave, lanes))
        two_up_moved = lax.ppermute(two_up, "mem", up)
        two = two_up_moved, lax.ppermute(two_down, "mem", down)
        one_up = send(c, 1, 1, after=(two_down,))
        one_up_moved = lax.ppermute(one_up, "mem", up)
        one_down = send(c, 3, 0, after=(one_up,))
        one = one_up_moved, lax.ppermute(one_down, "mem", down)
        field = filter_rows(6, 2, field, after=(one_down,))
        states[c] = (field, enter, leave, lanes)
        increments.append(finish(c, two, one))
    return increments[0] if len(increments) == 1 else jnp.concatenate(increments)


def solution(mesh):
    return jax.shard_map(
        per_device,
        mesh=mesh,
        in_specs=(
            P("mem", None, "lon", "lat"),
            P("mem", None, "lon", "lat"),
            P(),
            P("mem"),
            P(),
            P(),
            P(),
        ),
        out_specs=P("mem", "lon", "lat"),
        check_vma=False,
    )
```
